32 devices in a mesh: dp: 4 (over z), seq: 8 (over y, x, core).
Axes of the slice: x: 2, y: 2, z: 4, core: 2. Of those that a mesh axis runs over, the one named last changes fastest.
Arguments:
- latents: bfloat16 [13056, 768], P(('dp', 'seq')), may hold values from -6 to 6
- clip_ids: int32 [13056], P('dp'), may hold values from 0 to 31, as said below
- restore: int32 [13056], P('dp'), may hold values from 0 to 2047
- counts: int32 [32], P('dp'), may hold values from 51 to 408, as said below
- embed_weight: bfloat16 [768, 512], replicated, may hold values from -0.21875 to 0.21875
- embed_bias: bfloat16 [512], replicated, may hold values from -3 to 3
- mask_token: bfloat16 [512], replicated, may hold values from -4 to 4
- first_gain: bfloat16 [512], replicated, may hold values from 0.099609375 to 1.8984375
- first_shift: bfloat16 [512], replicated, may hold values from -2 to 2
- joint_weight: bfloat16 [512, 1536], replicated, may hold values from -0.375 to 0.375
- query_bias: bfloat16 [512], replicated, may hold values from -3 to 3
- value_bias: bfloat16 [512], replicated, may hold values from -3 to 3
- output_weight: bfloat16 [512, 512], replicated, may hold values from -1.5 to 1.5
- output_bias: bfloat16 [512], replicated, may hold values from -2 to 2
- second_gain: bfloat16 [512], replicated, may hold values from 0.099609375 to 1.8984375
- second_shift: bfloat16 [512], replicated, may hold values from -2 to 2
- expand_weight: bfloat16 [512, 2048], replicated, may hold values from -0.25 to 0.25
- expand_bias: bfloat16 [2048], replicated, may hold values from -2 to 2
- contract_weight: bfloat16 [2048, 512], replicated, may hold values from -0.125 to 0.125
- contract_bias: bfloat16 [512], replicated, may hold values from -2 to 2
- cotangent: bfloat16 [32, 2048, 512], P('dp', 'seq'), may hold values from -6 to 6
Outputs:
- decoded: bfloat16 [32, 2048, 512], P('dp', 'seq')
- latent_grad: bfloat16 [13056, 768], P(('dp', 'seq'))
- grad_embed_weight: float32 [768, 512], replicated
- grad_embed_bias: float32 [512], replicated
- grad_mask_token: float32 [512], replicated
- grad_first_gain: float32 [512], replicated
- grad_first_shift: float32 [512], replicated
- grad_joint_weight: float32 [512, 1536], replicated
- grad_query_bias: float32 [512], replicated
- grad_value_bias: float32 [512], replicated
- grad_output_weight: float32 [512, 512], replicated
- grad_output_bias: float32 [512], replicated
- grad_second_gain: float32 [512], replicated
- grad_second_shift: float32 [512], replicated
- grad_expand_weight: float32 [512, 2048], replicated
- grad_expand_bias: float32 [2048], replicated
- grad_contract_weight: float32 [2048, 512], replicated
- grad_contract_bias: float32 [512], replicated
The draws below stay inside these ranges and needn't reach their ends.
Inputs may be any that keep to these rules, and one draw needn't show every extreme that they name: Only the first counts rows of each device's 408 row slots are visible latents; the others are to be ignored. In every dp group some device has exactly 408. `clip_ids`: every row's clip is one of the 8 clips of its dp index, dp index times 8 onward. Over the live rows the pairs (clip, position) are all different, and of one device's live rows at most 51 have restore // 256 equal to one value; this bound is reached on every dp index.
All inputs are finite; a program needn't handle non-finite values.
Results may differ from the reference program's by a relative error of at most 0.018.
Values may be sent and summed in bfloat16 or wider, within the bound.
A program may use at most 320 MiB of HBM per device.

```python
import math
from functools import partial
import jax
import jax.numpy as jnp
from jax import lax

D = 512
HEADS = 16
HEAD_DIM = 32
FF = 2048
ENC = 768
CLIP_LEN = 2048
CLIPS = 8
SHARE = 256
SLOT = 51
CAP = 408
GROUPS = 4
SPLITS = 8
TOTAL_CLIPS = 32
VIS_ROWS = 13056


def visible_layout(base_key):
    keys_all = jax.random.split(base_key, 7)
    held = CLIPS * SHARE
    loads = jax.random.randint(keys_all[0], (GROUPS, SPLITS, SPLITS), 0, SLOT + 1)
    busiest = jax.random.randint(keys_all[1], (GROUPS, 1, 1), 0, SPLITS)
    fullest = jax.random.randint(keys_all[2], (GROUPS, 1, 1), 0, SPLITS)
    index = jnp.arange(SPLITS)
    loads = jnp.where((index[None, :, None] == busiest) | (index[None, None, :] == fullest), SLOT, loads)
    before = jnp.cumsum(loads, axis=1) - loads
    place_keys = jax.random.split(keys_all[3], GROUPS * SPLITS)
    places = jax.vmap(lambda one_key: jax.random.permutation(one_key, held))(place_keys)
    places = jnp.broadcast_to(places.reshape(GROUPS, 1, SPLITS, held), (GROUPS, SPLITS, SPLITS, held))
    steps_in = jnp.arange(SLOT)
    alive = steps_in[None, None, None, :] < loads[..., None]
    order_in = jnp.minimum(before[..., None] + steps_in[None, None, None, :], held - 1)
    local = jnp.take_along_axis(places, order_in, axis=3)
    group = jnp.arange(GROUPS)[:, None, None, None]
    clip_num = group * CLIPS + local // SHARE
    position = index[None, None, :, None] * SHARE + local % SHARE
    pad_clip = group * CLIPS + jax.random.randint(keys_all[4], alive.shape, 0, CLIPS)
    pad_place = jax.random.randint(keys_all[5], alive.shape, 0, CLIP_LEN)
    clip_num = jnp.where(alive, clip_num, pad_clip).reshape(GROUPS, SPLITS, CAP)
    position = jnp.where(alive, position, pad_place).reshape(GROUPS, SPLITS, CAP)
    alive = alive.reshape(GROUPS, SPLITS, CAP)
    shuffle_keys = jax.random.split(keys_all[6], GROUPS * SPLITS)
    ranks = jax.vmap(lambda one_key: jax.random.permutation(one_key, CAP))(shuffle_keys).reshape(GROUPS, SPLITS, CAP)
    ranks = ranks + jnp.where(alive, 0, CAP)
    order = jnp.argsort(ranks, axis=2)
    clip_num = jnp.take_along_axis(clip_num, order, axis=2).reshape(-1).astype(jnp.int32)
    position = jnp.take_along_axis(position, order, axis=2).reshape(-1).astype(jnp.int32)
    totals = jnp.sum(loads, axis=2).reshape(-1).astype(jnp.int32)
    return (clip_num, position, totals)


def draw_clip_ids(key, part):
    layout = visible_layout(key)
    return layout[0]


def draw_restore(key, part):
    layout = visible_layout(key)
    return layout[1]


def draw_counts(key, part):
    layout = visible_layout(key)
    return layout[2]


def block_levels(key, extent, cuts, smallest, largest):
    loudness = 1.0
    for axis_at, shards_of in cuts:
        steps = jax.random.uniform(jax.random.fold_in(jax.random.fold_in(key, 6), axis_at), (shards_of,), jnp.float32, smallest / len(cuts), largest / len(cuts))
        loudness = loudness * jnp.repeat(jnp.exp(steps), extent[axis_at] // shards_of).reshape((-1,) + (1,) * (len(extent) - 1 - axis_at))
    return loudness


def scatter_about(key, dims, deviation, reach, pieces=(), kind=jnp.bfloat16):
    entries = deviation * jax.random.normal(key, dims, jnp.float32)
    if pieces:
        entries = entries * block_levels(key, dims, pieces, -0.22, 0.18)
    return jnp.clip(entries, -reach, reach).astype(kind)


def setup_inputs(seed: int = 0) -> dict:
    seeds = jax.random.split(jax.random.key(seed), 22)
    latents = scatter_about(seeds[0], (VIS_ROWS, ENC), 1.0, 6.0, ((0, 32),))
    clip_ids = draw_clip_ids(jax.random.fold_in(seeds[21], 71), 0)
    restore = draw_restore(jax.random.fold_in(seeds[21], 71), 0)
    counts = draw_counts(jax.random.fold_in(seeds[21], 71), 0)
    embed_weight = scatter_about(seeds[4], (ENC, D), ENC ** -0.5, 0.21875)
    embed_bias = scatter_about(seeds[5], (D,), 0.5, 3.0)
    mask_token = scatter_about(seeds[6], (D,), 1.0, 4.0)
    first_gain = jnp.clip(1.0 + 0.18 * jax.random.normal(seeds[7], (D,), jnp.float32), 0.099609375, 1.8984375).astype(jnp.bfloat16)
    first_shift = scatter_about(seeds[8], (D,), 0.3, 2.0)
    joint_weight = scatter_about(seeds[9], (D, 3 * D), (D // 2) ** -0.5, 0.375)
    query_bias = scatter_about(seeds[10], (D,), 0.5, 3.0)
    value_bias = scatter_about(seeds[11], (D,), 0.5, 3.0)
    output_weight = scatter_about(seeds[12], (D, D), (D // 32) ** -0.5, 1.5)
    output_bias = scatter_about(seeds[13], (D,), 0.3, 2.0)
    second_gain = jnp.clip(1.0 + 0.18 * jax.random.normal(seeds[14], (D,), jnp.float32), 0.099609375, 1.8984375).astype(jnp.bfloat16)
    second_shift = scatter_about(seeds[15], (D,), 0.3, 2.0)
    expand_weight = scatter_about(seeds[16], (D, FF), D ** -0.5, 0.25)
    expand_bias = scatter_about(seeds[17], (FF,), 0.3, 2.0)
    contract_weight = scatter_about(seeds[18], (FF, D), FF ** -0.5, 0.125)
    contract_bias = scatter_about(seeds[19], (D,), 0.3, 2.0)
    cotangent = scatter_about(seeds[20], (TOTAL_CLIPS, CLIP_LEN, D), 1.0, 6.0, ((0, 4), (1, 8)))
    return {"latents": latents, "clip_ids": clip_ids, "restore": restore, "counts": counts, "embed_weight": embed_weight, "embed_bias": embed_bias, "mask_token": mask_token, "first_gain": first_gain, "first_shift": first_shift, "joint_weight": joint_weight, "query_bias": query_bias, "value_bias": value_bias, "output_weight": output_weight, "output_bias": output_bias, "second_gain": second_gain, "second_shift": second_shift, "expand_weight": expand_weight, "expand_bias": expand_bias, "contract_weight": contract_weight, "contract_bias": contract_bias, "cotangent": cotangent}


highest = lax.Precision.HIGHEST
epsilon = 1e-06

@jax.custom_vjp
def low(v):
    return lax.optimization_barrier(v.astype(jnp.bfloat16)).astype(jnp.float32)

@jax.custom_vjp
def low_back(v):
    return v

def low_keep(v):
    return (low(v), None)

def low_pass(kept, grad):
    return (grad,)

def back_keep(v):
    return (v, None)

def back_low(kept, grad):
    return (low(grad),)
low.defvjp(low_keep, low_pass)
low_back.defvjp(back_keep, back_low)

def matmul(left, right):
    return jnp.dot(left, right, precision=highest, preferred_element_type=jnp.float32)

def layer_norm(values, gain, shift):
    center = values - lax.optimization_barrier(jnp.mean(values, axis=-1, keepdims=True))
    spread = lax.optimization_barrier(jnp.mean(center * center, axis=-1, keepdims=True))
    return center * lax.rsqrt(spread + epsilon) * gain + shift

def sinusoid(places, table_width):
    half_width = table_width // 2
    frequency = jnp.exp(-math.log(10000.0) * jnp.arange(half_width, dtype=jnp.float32) / half_width)
    angles = places.astype(jnp.float32)[:, None] * frequency[None, :]
    return jnp.concatenate([jnp.sin(angles), jnp.cos(angles)], axis=1)

def clip_block(weights, stream):
    first_gain, first_shift, joint_weight, query_bias, value_bias, output_weight, output_bias, second_gain, second_shift, expand_weight, expand_bias, contract_weight, contract_bias = weights
    first_normed = low(layer_norm(stream, first_gain, first_shift))
    joint = matmul(first_normed, joint_weight)
    query_rows = low(low_back(joint[:, :D] + query_bias))
    key_rows = low(low_back(joint[:, D:2 * D]))
    value_rows = low(low_back(joint[:, 2 * D:] + value_bias))
    key_heads = key_rows.reshape(CLIP_LEN, HEADS, HEAD_DIM)
    value_heads = value_rows.reshape(CLIP_LEN, HEADS, HEAD_DIM)
    block_rows = min(512, CLIP_LEN)
    query_blocks = query_rows.reshape(CLIP_LEN // block_rows, block_rows, HEADS, HEAD_DIM)

    def attend(block_query):
        scores = low_back(jnp.einsum('qhd,khd->hqk', block_query, key_heads, precision=highest) * HEAD_DIM ** (-0.5))
        attention = low(jax.nn.softmax(scores, axis=-1))
        return jnp.einsum('hqk,khd->qhd', attention, value_heads, precision=highest)
    attended = lax.map(jax.checkpoint(attend), query_blocks).reshape(CLIP_LEN, D)
    attended = low(low_back(attended))
    middle = stream + low_back(matmul(attended, output_weight) + output_bias)
    second_normed = low(layer_norm(middle, second_gain, second_shift))
    hidden = low_back(matmul(second_normed, expand_weight) + expand_bias)
    active = low(jax.nn.gelu(hidden, approximate=False))
    return middle + low_back(matmul(active, contract_weight) + contract_bias)

def reference(latents, clip_ids, restore, counts, embed_weight, embed_bias, mask_token, first_gain, first_shift, joint_weight, query_bias, value_bias, output_weight, output_bias, second_gain, second_shift, expand_weight, expand_bias, contract_weight, contract_bias, cotangent):
    row_index = jnp.arange(VIS_ROWS, dtype=jnp.int32)
    visible = row_index % CAP < counts[row_index // CAP]
    target = jnp.where(visible, clip_ids * CLIP_LEN + restore, TOTAL_CLIPS * CLIP_LEN).astype(jnp.int32)
    table = sinusoid(jnp.arange(CLIP_LEN, dtype=jnp.int32), D)

    def forward(params, latent_rows):
        embedded = low(low_back(matmul(latent_rows, params[0]) + params[1]))
        filled = jnp.broadcast_to(params[2], (TOTAL_CLIPS * CLIP_LEN, D)).at[target].set(embedded, mode='drop')
        stream = filled.reshape(TOTAL_CLIPS, CLIP_LEN, D) + table[None]
        return lax.map(jax.checkpoint(partial(clip_block, params[3:])), stream)
    params = tuple((weight.astype(jnp.float32) for weight in (embed_weight, embed_bias, mask_token, first_gain, first_shift, joint_weight, query_bias, value_bias, output_weight, output_bias, second_gain, second_shift, expand_weight, expand_bias, contract_weight, contract_bias)))
    decoded, pullback = jax.vjp(forward, params, latents.astype(jnp.float32))
    grad_params, grad_latents = pullback(cotangent.astype(jnp.float32))
    return (decoded.astype(jnp.bfloat16), grad_latents.astype(jnp.bfloat16), grad_params[0], grad_params[1], grad_params[2], grad_params[3], grad_params[4], grad_params[5], grad_params[6], grad_params[7], grad_params[8], grad_params[9], grad_params[10], grad_params[11], grad_params[12], grad_params[13], grad_params[14], grad_params[15])
```

```python
from functools import partial
import math

import jax
import jax.numpy as jnp
from jax import lax
from jax.experimental import pallas as pl
from jax.experimental.pallas import tpu as pltpu
from jax.sharding import PartitionSpec as P

HEADS = 16
HEAD_DIM = 32
PACK = 128 // HEAD_DIM
VMEM_LIMIT = 56 * 1024 * 1024
LOG2E = math.log2(math.e)
QUERY_SCALE = LOG2E * HEAD_DIM ** (-0.5)


epsilon = 1e-06


def layer_norm(values, gain, shift):
    center = values - jnp.mean(values, axis=-1, keepdims=True)
    spread = jnp.mean(center * center, axis=-1, keepdims=True)
    return center * lax.rsqrt(spread + epsilon) * gain + shift


def sinusoid(places, table_width):
    half_width = table_width // 2
    frequency = jnp.exp(-math.log(10000.0) * jnp.arange(half_width, dtype=jnp.float32) / half_width)
    angles = places.astype(jnp.float32)[:, None] * frequency[None, :]
    return jnp.concatenate([jnp.sin(angles), jnp.cos(angles)], axis=1)


def plain_dot(left, right):
    return jnp.dot(left, right, preferred_element_type=jnp.float32)


def lead_dot(left, right):
    return lax.dot_general(
        left, right, (((0,), (0,)), ((), ())), preferred_element_type=jnp.float32
    )


def trail_dot(left, right):
    return lax.dot_general(
        left, right, (((1,), (1,)), ((), ())), preferred_element_type=jnp.float32
    )


def column_sum(values):
    return jnp.sum(values.astype(jnp.float32), axis=0)


def attend_kernel(key_ref, query_ref, value_ref, mixed_ref, total_ref, raised_ref):
    query = query_ref[...]
    head_row = lax.broadcasted_iota(jnp.int32, query.shape, 0) // HEAD_DIM
    ones = jnp.ones((16, value_ref.shape[1]), jnp.bfloat16)
    totals = []
    for head in range(PACK):
        rows = slice(head * HEAD_DIM, (head + 1) * HEAD_DIM)
        own_query = jnp.where(head_row == head, query, jnp.zeros_like(query))
        scores = jnp.dot(key_ref[...], own_query, preferred_element_type=jnp.float32)
        highest = jnp.max(scores, axis=0, keepdims=True)
        raised = jnp.exp2(scores - highest).astype(jnp.bfloat16)
        raised_ref[head] = raised
        widened = jnp.concatenate([value_ref[rows, :], ones], axis=0)
        mixed = jnp.dot(widened, raised, preferred_element_type=jnp.float32)
        total = mixed[HEAD_DIM : HEAD_DIM + 1]
        totals.append(total)
        mixed_ref[rows, :] = (mixed[:HEAD_DIM] / total).astype(jnp.bfloat16)
    total_ref[0, 0:PACK] = jnp.concatenate(totals, axis=0)


def attend(keys, query_t, value_t):
    width, rows = query_t.shape
    span = keys.shape[0]
    block = min(256, rows)
    groups = width // 128
    return pl.pallas_call(
        attend_kernel,
        grid=(groups, rows // block),
        in_specs=[
            pl.BlockSpec((span, 128), lambda g, i: (0, g)),
            pl.BlockSpec((128, block), lambda g, i: (g, i)),
            pl.BlockSpec((128, span), lambda g, i: (g, 0)),
        ],
        out_specs=[
            pl.BlockSpec((128, block), lambda g, i: (g, i)),
            pl.BlockSpec((1, 8, block), lambda g, i: (g, 0, i)),
            pl.BlockSpec((PACK, span, block), lambda g, i: (g, 0, i)),
        ],
        out_shape=[
            jax.ShapeDtypeStruct((width, rows), jnp.bfloat16),
            jax.ShapeDtypeStruct((groups, 8, rows), jnp.float32),
            jax.ShapeDtypeStruct((HEADS, span, rows), jnp.bfloat16),
        ],
        compiler_params=pltpu.CompilerParams(vmem_limit_bytes=VMEM_LIMIT),
        cost_estimate=pl.CostEstimate(
            flops=HEADS * span * rows * 512,
            bytes_accessed=2 * HEADS * span * rows,
            transcendentals=HEADS * span * rows,
        ),
        name="attend",
    )(keys, query_t, value_t)


def attend_back_kernel(
    raised_ref, total_ref, value_ref, key_ref, query_ref, mixed_ref, grad_ref, grad_query_ref, grad_key_ref, grad_value_ref
):
    @pl.when(pl.program_id(1) == 0)
    def _():
        grad_key_ref[...] = jnp.zeros_like(grad_key_ref)
        grad_value_ref[...] = jnp.zeros_like(grad_value_ref)

    block = query_ref.shape[1]
    head_row = lax.broadcasted_iota(jnp.int32, (128, block), 0) // HEAD_DIM
    head_col = lax.broadcasted_iota(jnp.int32, (block, 128), 1) // HEAD_DIM
    inverse = 1.0 / total_ref[0, 0:PACK]
    inverse = jnp.concatenate(
        [jnp.broadcast_to(inverse[h : h + 1], (HEAD_DIM, block)) for h in range(PACK)], axis=0
    )
    grad = grad_ref[...].astype(jnp.float32) * inverse
    inner = grad * mixed_ref[...].astype(jnp.float32)
    grad_low = grad.astype(jnp.bfloat16)
    grad_turned = grad.T.astype(jnp.bfloat16)
    query_turned = query_ref[...].astype(jnp.float32).T.astype(jnp.bfloat16)
    for head in range(PACK):
        rows = slice(head * HEAD_DIM, (head + 1) * HEAD_DIM)
        own_grad = jnp.where(head_row == head, grad_low, jnp.zeros_like(grad_low))
        grad_weight = jnp.dot(value_ref[...], own_grad, preferred_element_type=jnp.float32)
        row_inner = jnp.sum(inner[rows], axis=0, keepdims=True)
        raised = raised_ref[head]
        grad_scores = raised * (grad_weight - row_inner).astype(jnp.bfloat16)
        grad_value_ref[...] += jnp.dot(
            raised,
            jnp.where(head_col == head, grad_turned, jnp.zeros_like(grad_turned)),
            preferred_element_type=jnp.float32,
        )
        grad_key_ref[...] += jnp.dot(
            grad_scores,
            jnp.where(head_col == head, query_turned, jnp.zeros_like(query_turned)),
            preferred_element_type=jnp.float32,
        )
        grad_query_ref[rows, :] = (
            jnp.dot(key_ref[rows, :], grad_scores, preferred_element_type=jnp.float32)
            * HEAD_DIM ** (-0.5)
        ).astype(jnp.bfloat16)


def attend_back(raised, total, values, key_t, query_t, mixed_t, grad_t):
    width, rows = query_t.shape
    span = values.shape[0]
    block = min(256, rows)
    groups = width // 128
    lane_block = pl.BlockSpec((128, block), lambda g, i: (g, i))
    return pl.pallas_call(
        attend_back_kernel,
        grid=(groups, rows // block),
        in_specs=[
            pl.BlockSpec((PACK, span, block), lambda g, i: (g, 0, i)),
            pl.BlockSpec((1, 8, block), lambda g, i: (g, 0, i)),
            pl.BlockSpec((span, 128), lambda g, i: (0, g)),
            pl.BlockSpec((128, span), lambda g, i: (g, 0)),
            lane_block,
            lane_block,
            lane_block,
        ],
        out_specs=[
            lane_block,
            pl.BlockSpec((span, 128), lambda g, i: (0, g)),
            pl.BlockSpec((span, 128), lambda g, i: (0, g)),
        ],
        out_shape=[
            jax.ShapeDtypeStruct((width, rows), jnp.bfloat16),
            jax.ShapeDtypeStruct((span, width), jnp.float32),
            jax.ShapeDtypeStruct((span, width), jnp.float32),
        ],
        compiler_params=pltpu.CompilerParams(vmem_limit_bytes=VMEM_LIMIT),
        cost_estimate=pl.CostEstimate(
            flops=HEADS * span * rows * 1024,
            bytes_accessed=2 * HEADS * span * rows,
            transcendentals=0,
        ),
        name="attend_back",
    )(raised, total, values, key_t, query_t, mixed_t, grad_t)


def body(
    latents,
    clip_ids,
    restore,
    counts,
    embed_weight,
    embed_bias,
    mask_token,
    first_gain,
    first_shift,
    joint_weight,
    query_bias,
    value_bias,
    output_weight,
    output_bias,
    second_gain,
    second_shift,
    expand_weight,
    expand_bias,
    contract_weight,
    contract_bias,
    cotangent,
):
    splits = lax.axis_size("seq")
    seq_index = lax.axis_index("seq")
    capacity = latents.shape[0]
    clip_count, clip_share, model_width = cotangent.shape
    sharers = splits // clip_count
    rows = clip_count * clip_share
    own_clip = seq_index % clip_count
    first_place = (seq_index // clip_count) * rows
    exchange_groups = [[s * clip_count + c for c in range(clip_count)] for s in range(sharers)]
    clip_groups = [[s * clip_count + c for s in range(sharers)] for c in range(clip_count)]

    def to_clips(blocks):
        return lax.all_to_all(
            blocks,
            "seq",
            split_axis=0,
            concat_axis=0,
            tiled=True,
            axis_index_groups=exchange_groups if sharers > 1 else None,
        )

    def flatten(parts):
        return jnp.concatenate(
            [part.reshape(-1, model_width).astype(jnp.bfloat16) for part in parts], axis=0
        )

    def sum_flat(flat, parts):
        flat = lax.psum(flat, ("dp", "seq")).astype(jnp.float32)
        out, at = [], 0
        for part in parts:
            size = part.size // model_width
            out.append(flat[at : at + size].reshape(part.shape))
            at += size
        return out

    slot = jnp.arange(splits * capacity, dtype=jnp.int32)
    live = (slot % capacity) < jnp.repeat(counts, capacity)
    mine = live & (clip_ids % clip_count == own_clip)
    slot_place = jnp.where(mine, restore - first_place, -1)
    places = jnp.arange(rows, dtype=jnp.int32)
    restore_map = (places[:, None] == slot_place[None, :]).astype(jnp.bfloat16)

    embedded = (plain_dot(latents, embed_weight) + embed_bias.astype(jnp.float32)).astype(
        jnp.bfloat16
    )
    embedded_all = lax.all_gather(embedded, "seq", axis=0, tiled=True)
    grad_output = to_clips(cotangent).reshape(rows, model_width)

    placed = plain_dot(restore_map, embedded_all)
    visible_mask = jnp.sum(restore_map, axis=1, dtype=jnp.float32)
    stream = (
        placed
        + (1.0 - visible_mask)[:, None] * mask_token.astype(jnp.float32)[None, :]
        + sinusoid(first_place + places, model_width)
    )
    first_normed, first_back = jax.vjp(
        layer_norm, stream, first_gain.astype(jnp.float32), first_shift.astype(jnp.float32)
    )
    first_low = first_normed.astype(jnp.bfloat16)
    joint = plain_dot(first_low, joint_weight)
    query_t = (
        ((joint[:, :model_width] + query_bias.astype(jnp.float32)) * QUERY_SCALE)
        .astype(jnp.bfloat16)
        .T
    )
    keys = joint[:, model_width : 2 * model_width].astype(jnp.bfloat16)
    values = (joint[:, 2 * model_width :] + value_bias.astype(jnp.float32)).astype(jnp.bfloat16)
    if sharers > 1:
        keys = lax.all_gather(keys, "seq", axis=0, tiled=True, axis_index_groups=clip_groups)
        values = lax.all_gather(values, "seq", axis=0, tiled=True, axis_index_groups=clip_groups)
    mixed_t, total, raised = attend(keys, query_t, values.T)
    attended = mixed_t.T
    middle = stream + plain_dot(attended, output_weight) + output_bias.astype(jnp.float32)
    second_normed, second_back = jax.vjp(
        layer_norm, middle, second_gain.astype(jnp.float32), second_shift.astype(jnp.float32)
    )
    second_low = second_normed.astype(jnp.bfloat16)
    hidden = plain_dot(second_low, expand_weight) + expand_bias.astype(jnp.float32)
    active, gelu_back = jax.vjp(partial(jax.nn.gelu, approximate=False), hidden)
    active_low = active.astype(jnp.bfloat16)
    output_rows = (
        middle + plain_dot(active_low, contract_weight) + contract_bias.astype(jnp.float32)
    )
    decoded = to_clips(
        output_rows.astype(jnp.bfloat16).reshape(clip_count, clip_share, model_width)
    )
    grad_contract = lead_dot(active_low, grad_output)
    grad_contract_bias = column_sum(grad_output)
    grad_hidden = gelu_back(trail_dot(grad_output, contract_weight))[0].astype(jnp.bfloat16)
    grad_expand = lead_dot(second_low, grad_hidden)
    grad_expand_bias = column_sum(grad_hidden)
    grad_middle_norm, grad_second_gain, grad_second_shift = second_back(
        trail_dot(grad_hidden, expand_weight)
    )
    grad_middle = grad_output.astype(jnp.float32) + grad_middle_norm
    grad_branch = grad_middle.astype(jnp.bfloat16)
    grad_output_weight = lead_dot(attended, grad_branch)
    grad_output_bias = column_sum(grad_branch)
    grad_attended_t = trail_dot(output_weight, grad_branch).astype(jnp.bfloat16)
    early = [
        grad_expand,
        grad_contract,
        grad_output_weight,
        grad_output_bias,
        grad_second_gain,
        grad_second_shift,
        grad_expand_bias,
        grad_contract_bias,
    ]
    early_flat, grad_attended_t = lax.optimization_barrier((flatten(early), grad_attended_t))
    (
        grad_expand,
        grad_contract,
        grad_output_weight,
        grad_output_bias,
        grad_second_gain,
        grad_second_shift,
        grad_expand_bias,
        grad_contract_bias,
    ) = sum_flat(early_flat, early)
    grad_query_t, grad_key, grad_value = attend_back(
        raised, total, values, keys.T, query_t, mixed_t, grad_attended_t
    )
    grad_sides = [(grad_key * (1.0 / LOG2E)).astype(jnp.bfloat16), grad_value.astype(jnp.bfloat16)]
    if sharers > 1:
        grad_sides = [
            lax.psum_scatter(
                side, "seq", scatter_dimension=0, tiled=True, axis_index_groups=clip_groups
            )
            for side in grad_sides
        ]
    grad_joint = jnp.concatenate([grad_query_t.T] + grad_sides, axis=1)
    grad_joint_weight = lead_dot(first_low, grad_joint)
    grad_query_bias = column_sum(grad_joint[:, :model_width])
    grad_value_bias = column_sum(grad_joint[:, 2 * model_width :])
    grad_stream_norm, grad_first_gain, grad_first_shift = first_back(
        trail_dot(grad_joint, joint_weight)
    )
    grad_stream = grad_middle + grad_stream_norm
    grad_mask = jnp.sum((1.0 - visible_mask)[:, None] * grad_stream, axis=0)
    back_rows = lead_dot(restore_map, grad_stream.astype(jnp.bfloat16)).astype(jnp.bfloat16)
    grad_embedded = lax.psum_scatter(back_rows, "seq", scatter_dimension=0, tiled=True)
    latent_grad = trail_dot(grad_embedded, embed_weight).astype(jnp.bfloat16)
    grad_embed_weight = lead_dot(latents, grad_embedded)
    grad_embed_bias = column_sum(grad_embedded)

    def sum_small(parts):
        flat = jnp.concatenate([part.reshape(-1, 128) for part in parts], axis=0)
        flat = lax.psum(flat, ("dp", "seq"))
        out, at = [], 0
        for part in parts:
            size = part.size // 128
            out.append(flat[at : at + size].reshape(part.shape))
            at += size
        return out

    late = [
        grad_joint_weight,
        grad_embed_weight,
        grad_embed_bias,
        grad_mask,
        grad_first_gain,
        grad_first_shift,
        grad_query_bias,
        grad_value_bias,
    ]
    late_flat, grad_output_weight = lax.optimization_barrier((flatten(late), grad_output_weight))
    (
        grad_joint_weight,
        grad_embed_weight,
        grad_embed_bias,
        grad_mask,
        grad_first_gain,
        grad_first_shift,
        grad_query_bias,
        grad_value_bias,
    ) = sum_flat(late_flat, late)
    return (
        decoded,
        latent_grad,
        grad_embed_weight,
        grad_embed_bias,
        grad_mask,
        grad_first_gain,
        grad_first_shift,
        grad_joint_weight,
        grad_query_bias,
        grad_value_bias,
        grad_output_weight,
        grad_output_bias,
        grad_second_gain,
        grad_second_shift,
        grad_expand,
        grad_expand_bias,
        grad_contract,
        grad_contract_bias,
    )


def solution(mesh):
    placed = (
        (P(("dp", "seq"), None),) + (P("dp"),) * 3 + (P(),) * 16 + (P("dp", "seq", None),)
    )
    return jax.shard_map(
        body,
        mesh=mesh,
        in_specs=placed,
        out_specs=(P("dp", "seq", None), P(("dp", "seq"), None)) + (P(),) * 16,
        check_vma=False,
    )
```

```python
from functools import partial
import math

import jax
import jax.numpy as jnp
from jax import lax
from jax.experimental import pallas as pl
from jax.experimental.pallas import tpu as pltpu
from jax.sharding import PartitionSpec as P

HEADS = 16
HEAD_DIM = 32
PACK = 128 // HEAD_DIM
VMEM_LIMIT = 56 * 1024 * 1024
MESH = pl.DeviceIdType.MESH
LOG2E = math.log2(math.e)
QUERY_SCALE = LOG2E * HEAD_DIM ** (-0.5)


epsilon = 1e-06


def whole(shape):
    return pl.BlockSpec(shape, lambda *_: (0,) * len(shape))


def turned(values):
    return values.astype(jnp.float32).T.astype(values.dtype)


def sinusoid(places, table_width):
    half_width = table_width // 2
    frequency = jnp.exp(-math.log(10000.0) * jnp.arange(half_width, dtype=jnp.float32) / half_width)
    angles = places.astype(jnp.float32)[:, None] * frequency[None, :]
    return jnp.concatenate([jnp.sin(angles), jnp.cos(angles)], axis=1)


def plain_dot(left, right):
    return jnp.dot(left, right, preferred_element_type=jnp.float32)


def lead_dot(left, right):
    return lax.dot_general(
        left, right, (((0,), (0,)), ((), ())), preferred_element_type=jnp.float32
    )


def trail_dot(left, right):
    return lax.dot_general(
        left, right, (((1,), (1,)), ((), ())), preferred_element_type=jnp.float32
    )


def column_sum(values):
    return jnp.sum(values.astype(jnp.float32), axis=0, keepdims=True)


def row_mean(values):
    return jnp.mean(values, axis=-1, keepdims=True)


def normalize(values):
    center = values - row_mean(values)
    scale = lax.rsqrt(row_mean(center * center) + epsilon)
    return center * scale, scale


def normalize_back(grad, normed, scale):
    return scale * (grad - row_mean(grad) - normed * row_mean(grad * normed))


class Spot:
    def __init__(self):
        self.layers, self.splits = lax.axis_size("dp"), lax.axis_size("seq")
        self.half = self.splits // 2
        self.layer, self.index = lax.axis_index("dp"), lax.axis_index("seq")
        self.core, self.chip = self.index % 2, self.index // 2

    def sibling(self):
        return (self.layer, self.chip * 2 + (1 - self.core))

    def chip_at(self, step):
        return (self.chip + step) % self.half

    def layer_at(self, step):
        return (self.layer + step) % self.layers

    def peer(self, step):
        return (self.layer, self.chip_at(step) * 2 + self.core)

    def above(self, step):
        return (self.layer_at(step), self.index)

    def meet(self, others):
        barrier = pltpu.get_barrier_semaphore()
        for other in others:
            pl.semaphore_signal(barrier, inc=1, device_id=other, device_id_type=MESH)
        return len(others)

    def tree(self, layers=True):
        others = [self.sibling()] + [self.peer(step) for step in range(1, self.half)]
        if layers:
            others += [self.above(step) for step in range(1, self.layers)]
        return others


def padded(rows, unit):
    return -(-rows // unit) * unit


def span_of(start, size):
    return pl.ds(pl.multiple_of(start, 16), size)


def send(source, target, sems, at, device):
    return pltpu.make_async_remote_copy(
        src_ref=source,
        dst_ref=target,
        send_sem=sems.at[0, at],
        recv_sem=sems.at[1, at],
        device_id=device,
        device_id_type=MESH,
    )


class TreeSum:
    def __init__(self, spot, source, result, refs, scatter):
        (
            self.near,
            self.near_sum,
            self.far,
            self.far_sum,
            self.deep,
            self.done,
            self.sems,
            self.local,
        ) = refs
        self.spot, self.source, self.result, self.scatter = spot, source, result, scatter
        self.part = self.far_sum.shape[0]
        self.piece = self.done.shape[0]

    @staticmethod
    def scratch(rows, width, scatter, splits, layers):
        half = splits // 2
        part = rows // splits
        piece = part // layers if scatter else part
        low = jnp.bfloat16
        return [
            pltpu.VMEM((half * part, width), low),
            pltpu.VMEM((half * part, width), low),
            pltpu.VMEM((max(half - 1, 1) * part, width), low),
            pltpu.VMEM((part, width), low),
            pltpu.VMEM((layers * piece, width), low),
            pltpu.VMEM((piece, width), low),
            pltpu.SemaphoreType.DMA((2, 2 + 2 * half + 2 * layers)),
            pltpu.SemaphoreType.DMA((2,)),
        ]

    def near_copy(self):
        spot = self.spot
        rows = spot.half * self.part
        return send(
            self.source.at[span_of((1 - spot.core) * rows, rows)],
            self.near,
            self.sems,
            0,
            spot.sibling(),
        )

    def own_copy(self):
        rows = self.spot.half * self.part
        return pltpu.make_async_copy(
            self.source.at[span_of(self.spot.core * rows, rows)], self.near_sum, self.local.at[0]
        )

    def far_copy(self, step):
        return send(
            self.near_sum.at[span_of(self.spot.chip_at(step) * self.part, self.part)],
            self.far.at[span_of((step - 1) * self.part, self.part)],
            self.sems,
            1 + step,
            self.spot.peer(step),
        )

    def deep_copy(self, step):
        spot = self.spot
        if self.scatter:
            source = self.far_sum.at[span_of(spot.layer_at(step) * self.piece, self.piece)]
        else:
            source = self.far_sum
        return send(
            source,
            self.deep.at[span_of(spot.layer * self.piece, self.piece)],
            self.sems,
            1 + spot.half + step,
            spot.above(step),
        )

    def place(self, core, chip, layer=None):
        spot = self.spot
        start = (core * spot.half + chip) * self.part
        if layer is None:
            return span_of(start, self.part)
        return span_of(start + layer * self.piece, self.piece)

    def done_copy(self):
        spot = self.spot
        layer = spot.layer if self.scatter else None
        return pltpu.make_async_copy(
            self.done, self.result.at[self.place(spot.core, spot.chip, layer)], self.local.at[1]
        )

    def layer_copy(self, step, arriving):
        spot = self.spot
        layer = spot.layer_at(-step) if arriving else spot.layer
        return send(
            self.done,
            self.result.at[self.place(spot.core, spot.chip, layer)],
            self.sems,
            1 + spot.half + spot.layers + step,
            spot.above(step),
        )

    def part_copy(self, step, arriving):
        spot = self.spot
        place = self.place(spot.core, spot.chip_at(-step) if arriving else spot.chip)
        return send(
            self.result.at[place] if self.scatter else self.done,
            self.result.at[place],
            self.sems,
            1 + spot.half + 2 * spot.layers + step,
            spot.peer(step),
        )

    def half_copy(self, arriving):
        spot = self.spot
        rows = spot.half * self.part
        core = 1 - spot.core if arriving else spot.core
        place = span_of(core * rows, rows)
        return send(
            self.result.at[place], self.result.at[place], self.sems, 1, spot.sibling()
        )

    def start(self):
        self.own_copy().start()
        self.near_copy().start()

    def near_to_far(self):
        self.own_copy().wait()
        self.near_copy().wait()
        unit = self.part
        while unit > 160 and unit % 32 == 0:
            unit //= 2

        def add(at, _):
            rows = span_of(at * unit, unit)
            self.near_sum[rows, :] = (
                self.near_sum[rows, :].astype(jnp.float32) + self.near[rows, :].astype(jnp.float32)
            ).astype(jnp.bfloat16)
            return 0

        lax.fori_loop(0, self.spot.half * (self.part // unit), add, 0)
        for step in range(1, self.spot.half):
            self.far_copy(step).start()

    def far_to_deep(self):
        spot = self.spot
        for step in range(1, spot.half):
            self.far_copy(step).wait()
        unit = self.part
        while unit > 160 and unit % 32 == 0:
            unit //= 2

        def add(at, _):
            start = at * unit
            total = self.near_sum[span_of(spot.chip * self.part + start, unit), :].astype(
                jnp.float32
            )
            for step in range(1, spot.half):
                total = total + self.far[span_of((step - 1) * self.part + start, unit), :].astype(
                    jnp.float32
                )
            self.far_sum[span_of(start, unit), :] = total.astype(jnp.bfloat16)
            return 0

        lax.fori_loop(0, self.part // unit, add, 0)
        for step in range(1, spot.layers):
            self.deep_copy(step).start()
        own = self.far_sum[...]
        if self.scatter:
            own = self.far_sum[span_of(spot.layer * self.piece, self.piece), :]
        self.deep[span_of(spot.layer * self.piece, self.piece), :] = own

    def deep_to_layer(self):
        spot = self.spot
        for step in range(1, spot.layers):
            self.deep_copy(step).wait_send()
        for step in range(1, spot.layers):
            send(
                self.done,
                self.deep.at[span_of(spot.layer_at(-step) * self.piece, self.piece)],
                self.sems,
                1 + spot.half + step,
                spot.above(step),
            ).wait_recv()
        total = self.deep[: self.piece, :].astype(jnp.float32)
        for layer in range(1, spot.layers):
            total = total + self.deep[layer * self.piece : (layer + 1) * self.piece, :].astype(
                jnp.float32
            )
        self.done[...] = total.astype(jnp.bfloat16)
        self.done_copy().start()
        if self.scatter:
            for step in range(1, spot.layers):
                self.layer_copy(step, False).start()
        else:
            for step in range(1, spot.half):
                self.part_copy(step, False).start()

    def layer_to_part(self):
        spot = self.spot
        if not self.scatter:
            return
        self.done_copy().wait()
        for step in range(1, spot.layers):
            self.layer_copy(step, False).wait_send()
        for step in range(1, spot.layers):
            self.layer_copy(step, True).wait_recv()
        for step in range(1, spot.half):
            self.part_copy(step, False).start()

    def part_to_half(self):
        spot = self.spot
        if not self.scatter:
            self.done_copy().wait()
        for step in range(1, spot.half):
            self.part_copy(step, False).wait_send()
        for step in range(1, spot.half):
            self.part_copy(step, True).wait_recv()
        self.half_copy(False).start()

    def finish(self):
        self.half_copy(False).wait_send()
        self.half_copy(True).wait_recv()


def enter_kernel(
    embedded_ref,
    slot_ref,
    table_ref,
    mask_ref,
    gain_ref,
    shift_ref,
    joint_ref,
    query_bias_ref,
    value_bias_ref,
    stream_ref,
    empty_ref,
    normed_ref,
    query_t_ref,
    key_ref,
    key_t_ref,
    value_ref,
    value_t_ref,
):
    block, width = stream_ref.shape
    place = lax.broadcasted_iota(jnp.int32, (block, 1), 0) + pl.program_id(0) * block
    fills = (place == slot_ref[...]).astype(jnp.float32)
    empty = 1.0 - jnp.sum(fills, axis=1, keepdims=True)
    placed = plain_dot(fills.astype(jnp.bfloat16), embedded_ref[...])
    stream = placed + empty * mask_ref[...].astype(jnp.float32) + table_ref[...]
    stream_ref[...] = stream
    empty_ref[...] = empty
    normed, _ = normalize(stream)
    low = (normed * gain_ref[...].astype(jnp.float32) + shift_ref[...].astype(jnp.float32)).astype(
        jnp.bfloat16
    )
    normed_ref[...] = low
    query = plain_dot(low, joint_ref[:, :width]) + query_bias_ref[...].astype(jnp.float32)
    query_t_ref[...] = (query * QUERY_SCALE).T.astype(jnp.bfloat16)
    keys = plain_dot(low, joint_ref[:, width : 2 * width])
    key_ref[...] = keys.astype(jnp.bfloat16)
    key_t_ref[...] = keys.T.astype(jnp.bfloat16)
    values = plain_dot(low, joint_ref[:, 2 * width :]) + value_bias_ref[...].astype(jnp.float32)
    value_ref[...] = values.astype(jnp.bfloat16)
    value_t_ref[...] = values.T.astype(jnp.bfloat16)


def enter(embedded_all, slot_place, table, mask_token, gain, shift, joint_weight, query_bias, value_bias):
    rows, width = table.shape
    slots = embedded_all.shape[0]
    block = min(256, rows)
    row_block = pl.BlockSpec((block, width), lambda i: (i, 0))
    lane_block = pl.BlockSpec((width, block), lambda i: (0, i))
    vector = whole((1, width))
    low = jax.ShapeDtypeStruct((rows, width), jnp.bfloat16)
    low_t = jax.ShapeDtypeStruct((width, rows), jnp.bfloat16)
    return pl.pallas_call(
        enter_kernel,
        grid=(rows // block,),
        in_specs=[
            whole((slots, width)),
            whole((1, slots)),
            row_block,
            vector,
            vector,
            vector,
            whole((width, 3 * width)),
            vector,
            vector,
        ],
        out_specs=[
            row_block,
            pl.BlockSpec((block, 1), lambda i: (i, 0)),
            row_block,
            lane_block,
            row_block,
            lane_block,
            row_block,
            lane_block,
        ],
        out_shape=[
            jax.ShapeDtypeStruct((rows, width), jnp.float32),
            jax.ShapeDtypeStruct((rows, 1), jnp.float32),
            low,
            low_t,
            low,
            low_t,
            low,
            low_t,
        ],
        compiler_params=pltpu.CompilerParams(vmem_limit_bytes=VMEM_LIMIT),
        cost_estimate=pl.CostEstimate(
            flops=2 * rows * width * (slots + 3 * width),
            bytes_accessed=20 * rows * width,
            transcendentals=0,
        ),
        name="enter",
    )(
        embedded_all,
        slot_place[None, :],
        table,
        mask_token[None, :],
        gain[None, :],
        shift[None, :],
        joint_weight,
        query_bias[None, :],
        value_bias[None, :],
    )


def attend_kernel(
    key_ref, query_ref, value_ref, mixed_ref, exact_ref, total_ref, raised_ref, scores_ref
):
    span = key_ref.shape[0]
    block = query_ref.shape[1]
    slice_rows = min(256, span)
    query = query_ref[...]
    head_row = lax.broadcasted_iota(jnp.int32, query.shape, 0) // HEAD_DIM
    ones = jnp.ones((16, slice_rows), jnp.bfloat16)
    highest = None
    for step in range(PACK + 1):
        if step < PACK:
            own_query = jnp.where(head_row == step, query, jnp.zeros_like(query))
            partial_highest = jnp.full((8, block), -jnp.inf, jnp.float32)
        if step > 0:
            head = step - 1
            rows = slice(head * HEAD_DIM, (head + 1) * HEAD_DIM)
            mixed = jnp.zeros((HEAD_DIM + 16, block), jnp.float32)
        for at in range(0, span, slice_rows):
            part = slice(at, at + slice_rows)
            if step < PACK:
                scores = plain_dot(key_ref[part, :], own_query)
                scores_ref[step % 2, part, :] = scores
                partial_highest = jnp.maximum(
                    partial_highest, jnp.max(scores.reshape(slice_rows // 8, 8, block), axis=0)
                )
            if step > 0:
                raised = jnp.exp2(scores_ref[(step - 1) % 2, part, :] - highest).astype(
                    jnp.bfloat16
                )
                raised_ref[head, part, :] = raised
                mixed = mixed + plain_dot(
                    jnp.concatenate([value_ref[rows, part], ones], axis=0), raised
                )
        if step > 0:
            total = mixed[HEAD_DIM : HEAD_DIM + 1]
            total_ref[0, head : head + 1, :] = total
            mixed = mixed[:HEAD_DIM] / total
            exact_ref[rows, :] = mixed
            mixed_ref[rows, :] = mixed.astype(jnp.bfloat16)
        if step < PACK:
            highest = jnp.max(partial_highest, axis=0, keepdims=True)


def attend(keys, query_t, value_t):
    width, rows = query_t.shape
    span = keys.shape[0]
    block = min(512, rows)
    groups = width // 128
    lane_block = pl.BlockSpec((128, block), lambda g, i: (g, i))
    return pl.pallas_call(
        attend_kernel,
        grid=(groups, rows // block),
        in_specs=[
            pl.BlockSpec((span, 128), lambda g, i: (0, g)),
            lane_block,
            pl.BlockSpec((128, span), lambda g, i: (g, 0)),
        ],
        out_specs=[
            lane_block,
            lane_block,
            pl.BlockSpec((1, 8, block), lambda g, i: (g, 0, i)),
            pl.BlockSpec((PACK, span, block), lambda g, i: (g, 0, i)),
        ],
        out_shape=[
            jax.ShapeDtypeStruct((width, rows), jnp.bfloat16),
            jax.ShapeDtypeStruct((width, rows), jnp.float32),
            jax.ShapeDtypeStruct((groups, 8, rows), jnp.float32),
            jax.ShapeDtypeStruct((HEADS, span, rows), jnp.bfloat16),
        ],
        scratch_shapes=[pltpu.VMEM((2, span, block), jnp.float32)],
        compiler_params=pltpu.CompilerParams(vmem_limit_bytes=VMEM_LIMIT),
        cost_estimate=pl.CostEstimate(
            flops=HEADS * span * rows * 512,
            bytes_accessed=2 * HEADS * span * rows,
            transcendentals=HEADS * span * rows,
        ),
        name="attend",
    )(keys, query_t, value_t)


def middle_kernel(
    stream_ref,
    mixed_ref,
    cotangent_ref,
    output_ref,
    output_bias_ref,
    gain_ref,
    shift_ref,
    expand_ref,
    expand_bias_ref,
    contract_ref,
    contract_bias_ref,
    decoded_ref,
    grad_middle_ref,
    grad_attended_ref,
    flat_ref,
    small_ref,
    expand_sum,
    contract_sum,
    output_sum,
    small_sum,
):
    width = stream_ref.shape[1]
    chunks = expand_ref.shape[1] // width

    @pl.when(pl.program_id(0) == 0)
    def _():
        expand_sum[...] = jnp.zeros_like(expand_sum)
        contract_sum[...] = jnp.zeros_like(contract_sum)
        output_sum[...] = jnp.zeros_like(output_sum)
        small_sum[...] = jnp.zeros_like(small_sum)

    mixed_t = mixed_ref[...]
    cotangent = cotangent_ref[...]
    middle = (
        stream_ref[...]
        + plain_dot(turned(mixed_t), output_ref[...])
        + output_bias_ref[...].astype(jnp.float32)
    )
    normed, scale = normalize(middle)
    gain = gain_ref[...].astype(jnp.float32)
    low = (normed * gain + shift_ref[...].astype(jnp.float32)).astype(jnp.bfloat16)
    low_t = turned(low)
    output = middle + contract_bias_ref[...].astype(jnp.float32)
    grad_normed = jnp.zeros_like(middle)
    for chunk in range(chunks):
        part = slice(chunk * width, (chunk + 1) * width)
        hidden = plain_dot(low, expand_ref[:, part]) + expand_bias_ref[:, part].astype(jnp.float32)
        below = 0.5 + 0.5 * lax.erf(hidden * math.sqrt(0.5))
        slope = below + hidden * jnp.exp(-0.5 * hidden * hidden) * (1.0 / math.sqrt(2 * math.pi))
        active = (hidden * below).astype(jnp.bfloat16)
        grad_hidden = (trail_dot(cotangent, contract_ref[part, :]) * slope).astype(jnp.bfloat16)
        output = output + plain_dot(active, contract_ref[part, :])
        grad_normed = grad_normed + trail_dot(grad_hidden, expand_ref[:, part])
        contract_sum[part, :] += plain_dot(turned(active), cotangent)
        expand_sum[part, :] += plain_dot(low_t, grad_hidden)
        small_sum[chunk : chunk + 1, :] += column_sum(grad_hidden)
    decoded_ref[...] = output.astype(jnp.bfloat16)
    grad_middle = cotangent.astype(jnp.float32) + normalize_back(grad_normed * gain, normed, scale)
    grad_middle_ref[...] = grad_middle
    branch = grad_middle.astype(jnp.bfloat16)
    grad_attended_ref[...] = trail_dot(output_ref[...], branch).astype(jnp.bfloat16)
    output_sum[...] += plain_dot(mixed_t, branch)
    small_sum[chunks : chunks + 1, :] += column_sum(cotangent)
    small_sum[chunks + 1 : chunks + 2, :] += column_sum(branch)
    small_sum[chunks + 2 : chunks + 3, :] += column_sum(grad_normed * normed)
    small_sum[chunks + 3 : chunks + 4, :] += column_sum(grad_normed)

    @pl.when(pl.program_id(0) == pl.num_programs(0) - 1)
    def _():
        at = 0
        for total in (expand_sum, contract_sum, output_sum):
            flat_ref[at : at + total.shape[0], :] = total[...].astype(flat_ref.dtype)
            at += total.shape[0]
        if at < flat_ref.shape[0]:
            flat_ref[at:, :] = jnp.zeros((flat_ref.shape[0] - at, width), flat_ref.dtype)
        small_ref[...] = small_sum[...]


def middle_block(
    stream,
    mixed_t,
    cotangent,
    output_weight,
    output_bias,
    gain,
    shift,
    expand_weight,
    expand_bias,
    contract_weight,
    contract_bias,
    flat_rows,
):
    rows, width = stream.shape
    hidden = expand_weight.shape[1]
    block = min(256, rows)
    row_block = pl.BlockSpec((block, width), lambda i: (i, 0))
    lane_block = pl.BlockSpec((width, block), lambda i: (0, i))
    vector = whole((1, width))
    small_rows = hidden // width + 4
    return pl.pallas_call(
        middle_kernel,
        grid=(rows // block,),
        in_specs=[
            row_block,
            lane_block,
            row_block,
            whole((width, width)),
            vector,
            vector,
            vector,
            whole((width, hidden)),
            whole((1, hidden)),
            whole((hidden, width)),
            vector,
        ],
        out_specs=[
            row_block,
            row_block,
            lane_block,
            whole((flat_rows, width)),
            whole((small_rows, width)),
        ],
        out_shape=[
            jax.ShapeDtypeStruct((rows, width), jnp.bfloat16),
            jax.ShapeDtypeStruct((rows, width), jnp.float32),
            jax.ShapeDtypeStruct((width, rows), jnp.bfloat16),
            jax.ShapeDtypeStruct((flat_rows, width), jnp.bfloat16),
            jax.ShapeDtypeStruct((small_rows, width), jnp.float32),
        ],
        scratch_shapes=[
            pltpu.VMEM((hidden, width), jnp.float32),
            pltpu.VMEM((hidden, width), jnp.float32),
            pltpu.VMEM((width, width), jnp.float32),
            pltpu.VMEM((small_rows, width), jnp.float32),
        ],
        compiler_params=pltpu.CompilerParams(vmem_limit_bytes=VMEM_LIMIT),
        cost_estimate=pl.CostEstimate(
            flops=2 * rows * width * (6 * hidden + 3 * width),
            bytes_accessed=16 * rows * width,
            transcendentals=2 * rows * hidden,
        ),
        name="middle",
    )(
        stream,
        mixed_t,
        cotangent,
        output_weight,
        output_bias[None, :],
        gain[None, :],
        shift[None, :],
        expand_weight,
        expand_bias[None, :],
        contract_weight,
        contract_bias[None, :],
    )


def attend_back_kernel(
    steps,
    raised_ref,
    total_ref,
    value_ref,
    key_ref,
    query_ref,
    exact_ref,
    grad_ref,
    flat_ref,
    rows_ref,
    grad_query_ref,
    grad_key_ref,
    grad_value_ref,
    summed_ref,
    decoded_ref,
    key_sum,
    value_sum,
    exchange_sems,
    exchange_local,
    *sum_refs,
):
    spot = Spot()
    tree = TreeSum(spot, flat_ref, summed_ref, sum_refs, True)
    clips, share = decoded_ref.shape[0], decoded_ref.shape[1]
    mine, part = spot.index % clips, spot.index // clips

    def member(step):
        return (mine + step) % clips

    def exchange(step):
        return send(
            rows_ref.at[span_of(member(step) * share, share)],
            decoded_ref.at[mine],
            exchange_sems,
            step,
            (spot.layer, part * clips + member(step)),
        )

    def own_rows():
        return pltpu.make_async_copy(
            rows_ref.at[span_of(mine * share, share)], decoded_ref.at[mine], exchange_local
        )

    step_now = pl.program_id(0) * pl.num_programs(1) + pl.program_id(1)

    def at_step(fraction):
        return pl.when(step_now == fraction * steps // 32)

    @at_step(0)
    def _():
        others = spot.tree() + [
            (spot.layer, part * clips + member(step)) for step in range(1, clips)
        ]
        count = spot.meet(others)
        pl.semaphore_wait(pltpu.get_barrier_semaphore(), count)
        tree.start()

    @at_step(2)
    def _():
        tree.near_to_far()

    @at_step(9)
    def _():
        tree.far_to_deep()
        own_rows().start()
        for step in range(1, clips):
            exchange(step).start()

    @at_step(13)
    def _():
        tree.deep_to_layer()

    @at_step(17)
    def _():
        tree.layer_to_part()

    @at_step(25)
    def _():
        tree.part_to_half()

    @at_step(31)
    def _():
        tree.finish()
        own_rows().wait()
        for step in range(1, clips):
            exchange(step).wait_send()
        for step in range(1, clips):
            send(
                rows_ref.at[span_of(mine * share, share)],
                decoded_ref.at[member(-step)],
                exchange_sems,
                step,
                (spot.layer, part * clips + member(step)),
            ).wait_recv()

    @pl.when(pl.program_id(1) == 0)
    def _():
        key_sum[...] = jnp.zeros_like(key_sum)
        value_sum[...] = jnp.zeros_like(value_sum)

    block = query_ref.shape[1]
    head_row = lax.broadcasted_iota(jnp.int32, (128, block), 0) // HEAD_DIM
    head_col = lax.broadcasted_iota(jnp.int32, (block, 128), 1) // HEAD_DIM
    inverse = 1.0 / total_ref[0, 0:PACK]
    inverse = jnp.concatenate(
        [jnp.broadcast_to(inverse[h : h + 1], (HEAD_DIM, block)) for h in range(PACK)], axis=0
    )
    grad_low = (grad_ref[...].astype(jnp.float32) * inverse).astype(jnp.bfloat16)
    grad = grad_low.astype(jnp.float32)
    inner = grad * exact_ref[...]
    grad_turned = grad.T.astype(jnp.bfloat16)
    query_turned = turned(query_ref[...])
    for head in range(PACK):
        rows = slice(head * HEAD_DIM, (head + 1) * HEAD_DIM)
        own_grad = jnp.where(head_row == head, grad_low, jnp.zeros_like(grad_low))
        grad_weight = plain_dot(value_ref[...], own_grad)
        row_inner = jnp.sum(inner[rows], axis=0, keepdims=True)
        raised = raised_ref[head]
        grad_scores = raised * (grad_weight - row_inner).astype(jnp.bfloat16)
        value_sum[...] += plain_dot(
            raised, jnp.where(head_col == head, grad_turned, jnp.zeros_like(grad_turned))
        )
        key_sum[...] += plain_dot(
            grad_scores, jnp.where(head_col == head, query_turned, jnp.zeros_like(query_turned))
        )
        grad_query_ref[rows, :] = (
            plain_dot(key_ref[rows, :], grad_scores) * HEAD_DIM ** (-0.5)
        ).astype(jnp.bfloat16)

    @pl.when(pl.program_id(1) == pl.num_programs(1) - 1)
    def _():
        grad_key_ref[...] = (key_sum[...] * (1.0 / LOG2E)).astype(jnp.bfloat16)
        grad_value_ref[...] = value_sum[...].astype(jnp.bfloat16)


def attend_back(raised, total, values, key_t, query_t, exact_t, grad_t, flat, decoded_rows):
    splits, layers = lax.axis_size("seq"), lax.axis_size("dp")
    clips, share, _ = decoded_rows.shape
    width, rows = query_t.shape
    span = values.shape[0]
    block = min(256, rows)
    groups = width // 128
    lane_block = pl.BlockSpec((128, block), lambda g, i: (g, i))
    return pl.pallas_call(
        partial(attend_back_kernel, groups * (rows // block)),
        grid=(groups, rows // block),
        in_specs=[
            pl.BlockSpec((PACK, span, block), lambda g, i: (g, 0, i)),
            pl.BlockSpec((1, 8, block), lambda g, i: (g, 0, i)),
            pl.BlockSpec((span, 128), lambda g, i: (0, g)),
            pl.BlockSpec((128, span), lambda g, i: (g, 0)),
            lane_block,
            lane_block,
            lane_block,
            pl.BlockSpec(memory_space=pl.ANY),
            pl.BlockSpec(memory_space=pl.ANY),
        ],
        out_specs=[
            lane_block,
            pl.BlockSpec((span, 128), lambda g, i: (0, g)),
            pl.BlockSpec((span, 128), lambda g, i: (0, g)),
            pl.BlockSpec(memory_space=pl.ANY),
            pl.BlockSpec(memory_space=pl.ANY),
        ],
        out_shape=[
            jax.ShapeDtypeStruct((width, rows), jnp.bfloat16),
            jax.ShapeDtypeStruct((span, width), jnp.bfloat16),
            jax.ShapeDtypeStruct((span, width), jnp.bfloat16),
            jax.ShapeDtypeStruct(flat.shape, flat.dtype),
            jax.ShapeDtypeStruct(decoded_rows.shape, decoded_rows.dtype),
        ],
        scratch_shapes=[
            pltpu.VMEM((span, 128), jnp.float32),
            pltpu.VMEM((span, 128), jnp.float32),
            pltpu.SemaphoreType.DMA((2, clips)),
            pltpu.SemaphoreType.DMA,
        ]
        + TreeSum.scratch(flat.shape[0], flat.shape[1], True, splits, layers),
        compiler_params=pltpu.CompilerParams(
            vmem_limit_bytes=VMEM_LIMIT, collective_id=1, has_side_effects=True
        ),
        cost_estimate=pl.CostEstimate(
            flops=HEADS * span * rows * 1024,
            bytes_accessed=2 * HEADS * span * rows,
            transcendentals=0,
        ),
        name="attend_back",
    )(raised, total, values, key_t, query_t, exact_t, grad_t, flat, decoded_rows.reshape(clips * share, width))


def leave_kernel(
    grad_query_ref,
    grad_key_ref,
    grad_value_ref,
    stream_ref,
    empty_ref,
    low_ref,
    grad_middle_ref,
    gain_ref,
    joint_ref,
    slot_ref,
    back_ref,
    grad_joint_ref,
    small_ref,
    joint_sum,
    small_sum,
    grad_all,
):
    block, width = stream_ref.shape
    step = pl.program_id(0)

    @pl.when(step == 0)
    def _():
        joint_sum[...] = jnp.zeros_like(joint_sum)
        small_sum[...] = jnp.zeros_like(small_sum)

    normed, scale = normalize(stream_ref[...])
    low_t = turned(low_ref[...])
    sides = [turned(grad_query_ref[...]), grad_key_ref[...], grad_value_ref[...]]
    grad_normed = jnp.zeros_like(normed)
    for at, side in enumerate(sides):
        grad_normed = grad_normed + trail_dot(side, joint_ref[:, at * width : (at + 1) * width])
        joint_sum[at * width : (at + 1) * width, :] += plain_dot(low_t, side)
    grad_stream = grad_middle_ref[...] + normalize_back(
        grad_normed * gain_ref[...].astype(jnp.float32), normed, scale
    )
    grad_all[pl.ds(pl.multiple_of(step * block, block), block), :] = grad_stream.astype(jnp.bfloat16)
    small_sum[0:1, :] += column_sum(empty_ref[...] * grad_stream)
    small_sum[1:2, :] += column_sum(grad_normed * normed)
    small_sum[2:3, :] += column_sum(grad_normed)
    small_sum[3:4, :] += column_sum(sides[0])
    small_sum[4:5, :] += column_sum(sides[2])

    @pl.when(step == pl.num_programs(0) - 1)
    def _():
        grad_joint_ref[...] = joint_sum[...].astype(grad_joint_ref.dtype)
        small_ref[...] = small_sum[...]
        slots = back_ref.shape[0]
        place = lax.broadcasted_iota(jnp.int32, (1, grad_all.shape[0]), 1)
        part = slots // 8
        for at in range(0, slots, part):
            takes = (slot_ref[at : at + part, :] == place).astype(jnp.float32).astype(jnp.bfloat16)
            back_ref[at : at + part, :] = plain_dot(takes, grad_all[...]).astype(jnp.bfloat16)


def leave(grad_query_t, grad_key, grad_value, stream, empty, low, grad_middle, gain, joint_weight, slot_place):
    rows, width = stream.shape
    slots = slot_place.shape[0]
    block = min(256, rows)
    row_block = pl.BlockSpec((block, width), lambda i: (i, 0))
    lane_block = pl.BlockSpec((width, block), lambda i: (0, i))
    return pl.pallas_call(
        leave_kernel,
        grid=(rows // block,),
        in_specs=[
            lane_block,
            row_block,
            row_block,
            row_block,
            pl.BlockSpec((block, 1), lambda i: (i, 0)),
            row_block,
            row_block,
            whole((1, width)),
            whole((width, 3 * width)),
            whole((slots, 1)),
        ],
        out_specs=[whole((slots, width)), whole((3 * width, width)), whole((8, width))],
        out_shape=[
            jax.ShapeDtypeStruct((slots, width), jnp.bfloat16),
            jax.ShapeDtypeStruct((3 * width, width), jnp.bfloat16),
            jax.ShapeDtypeStruct((8, width), jnp.float32),
        ],
        scratch_shapes=[
            pltpu.VMEM((3 * width, width), jnp.float32),
            pltpu.VMEM((8, width), jnp.float32),
            pltpu.VMEM((rows, width), jnp.bfloat16),
        ],
        compiler_params=pltpu.CompilerParams(vmem_limit_bytes=VMEM_LIMIT),
        cost_estimate=pl.CostEstimate(
            flops=2 * rows * width * (slots + 6 * width),
            bytes_accessed=20 * rows * width,
            transcendentals=0,
        ),
        name="leave",
    )(
        grad_query_t,
        grad_key,
        grad_value,
        stream,
        empty,
        low,
        grad_middle,
        gain[None, :],
        joint_weight,
        slot_place[:, None],
    )


def body(
    latents,
    clip_ids,
    restore,
    counts,
    embed_weight,
    embed_bias,
    mask_token,
    first_gain,
    first_shift,
    joint_weight,
    query_bias,
    value_bias,
    output_weight,
    output_bias,
    second_gain,
    second_shift,
    expand_weight,
    expand_bias,
    contract_weight,
    contract_bias,
    cotangent,
):
    splits = lax.axis_size("seq")
    seq_index = lax.axis_index("seq")
    capacity = latents.shape[0]
    clip_count, clip_share, model_width = cotangent.shape
    sharers = splits // clip_count
    rows = clip_count * clip_share
    own_clip = seq_index % clip_count
    first_place = (seq_index // clip_count) * rows
    exchange_groups = [[s * clip_count + c for c in range(clip_count)] for s in range(sharers)]
    clip_groups = [[s * clip_count + c for s in range(sharers)] for c in range(clip_count)]

    def to_clips(blocks):
        return lax.all_to_all(
            blocks,
            "seq",
            split_axis=0,
            concat_axis=0,
            tiled=True,
            axis_index_groups=exchange_groups if sharers > 1 else None,
        )

    slot = jnp.arange(splits * capacity, dtype=jnp.int32)
    live = (slot % capacity) < jnp.repeat(counts, capacity)
    mine = live & (clip_ids % clip_count == own_clip)
    slot_place = jnp.where(mine, restore - first_place, -1)
    table = sinusoid(first_place + jnp.arange(rows, dtype=jnp.int32), model_width)

    embedded = (plain_dot(latents, embed_weight) + embed_bias.astype(jnp.float32)).astype(
        jnp.bfloat16
    )
    embedded_all = lax.all_gather(embedded, "seq", axis=0, tiled=True)
    grad_output = to_clips(cotangent).reshape(rows, model_width)

    stream, empty, first_low, query_t, keys, key_t, values, value_t = enter(
        embedded_all,
        slot_place,
        table,
        mask_token,
        first_gain,
        first_shift,
        joint_weight,
        query_bias,
        value_bias,
    )
    if sharers > 1:
        keys = lax.all_gather(keys, "seq", axis=0, tiled=True, axis_index_groups=clip_groups)
        values = lax.all_gather(values, "seq", axis=0, tiled=True, axis_index_groups=clip_groups)
        key_t, value_t = keys.T, values.T
    mixed_t, exact_t, total, raised = attend(keys, query_t, value_t)
    (
        decoded_rows,
        grad_middle,
        grad_attended_t,
        early_flat,
        early_small,
    ) = middle_block(
        stream,
        mixed_t,
        grad_output,
        output_weight,
        output_bias,
        second_gain,
        second_shift,
        expand_weight,
        expand_bias,
        contract_weight,
        contract_bias,
        padded(2 * expand_weight.shape[1] + model_width, splits * lax.axis_size("dp") * 16),
    )
    grad_query_t, grad_key, grad_value, early_sum, decoded = attend_back(
        raised,
        total,
        values,
        key_t,
        query_t,
        exact_t,
        grad_attended_t,
        early_flat,
        decoded_rows.reshape(clip_count, clip_share, model_width),
    )
    if sharers > 1:
        grad_key, grad_value = (
            lax.psum_scatter(
                side, "seq", scatter_dimension=0, tiled=True, axis_index_groups=clip_groups
            )
            for side in (grad_key, grad_value)
        )
    back_rows, grad_joint, late_small = leave(
        grad_query_t,
        grad_key,
        grad_value,
        stream,
        empty,
        first_low,
        grad_middle,
        first_gain,
        joint_weight,
        slot_place,
    )
    grad_embedded = lax.psum_scatter(back_rows, "seq", scatter_dimension=0, tiled=True)
    latent_grad = trail_dot(grad_embedded, embed_weight).astype(jnp.bfloat16)
    grad_embed_weight = lead_dot(latents, grad_embedded)
    grad_embed_bias = column_sum(grad_embedded)
    late_flat = jnp.concatenate(
        [
            grad_joint.astype(jnp.float32),
            grad_embed_weight,
            early_small,
            late_small,
            grad_embed_bias,
        ],
        axis=0,
    )
    late_sum = lax.psum(late_flat, ("dp", "seq"))

    def columns(stack):
        return jnp.concatenate(jnp.split(stack, stack.shape[0] // model_width, axis=0), axis=1)

    hidden_width = expand_weight.shape[1]
    chunks = hidden_width // model_width
    grad_expand = columns(early_sum[:hidden_width])
    grad_contract = early_sum[hidden_width : 2 * hidden_width]
    grad_output_weight = early_sum[2 * hidden_width : 2 * hidden_width + model_width]
    grad_expand, grad_contract, grad_output_weight = (
        summed.astype(jnp.float32) for summed in (grad_expand, grad_contract, grad_output_weight)
    )
    grad_joint_weight = columns(late_sum[: 3 * model_width])
    at = 3 * model_width + embed_weight.shape[0]
    grad_embed_weight = late_sum[3 * model_width : at]
    grad_expand_bias = late_sum[at : at + chunks].reshape(-1)
    at += chunks
    grad_contract_bias, grad_output_bias, grad_second_gain, grad_second_shift = late_sum[at : at + 4]
    at += 4
    (
        grad_mask,
        grad_first_gain,
        grad_first_shift,
        grad_query_bias,
        grad_value_bias,
    ) = late_sum[at : at + 5]
    grad_embed_bias = late_sum[at + 8]
    return (
        decoded,
        latent_grad,
        grad_embed_weight,
        grad_embed_bias,
        grad_mask,
        grad_first_gain,
        grad_first_shift,
        grad_joint_weight,
        grad_query_bias,
        grad_value_bias,
        grad_output_weight,
        grad_output_bias,
        grad_second_gain,
        grad_second_shift,
        grad_expand,
        grad_expand_bias,
        grad_contract,
        grad_contract_bias,
    )


def solution(mesh):
    placed = (
        (P(("dp", "seq"), None),) + (P("dp"),) * 3 + (P(),) * 16 + (P("dp", "seq", None),)
    )
    return jax.shard_map(
        body,
        mesh=mesh,
        in_specs=placed,
        out_specs=(P("dp", "seq", None), P(("dp", "seq"), None)) + (P(),) * 16,
        check_vma=False,
    )
```

```python
from functools import partial
import math

import jax
import jax.numpy as jnp
from jax import lax
from jax.experimental import pallas as pl
from jax.experimental.pallas import tpu as pltpu
from jax.sharding import PartitionSpec as P

HEADS = 16
HEAD_DIM = 32
PACK = 128 // HEAD_DIM
VMEM_LIMIT = 56 * 1024 * 1024
MESH = pl.DeviceIdType.MESH
LOG2E = math.log2(math.e)
QUERY_SCALE = LOG2E * HEAD_DIM ** (-0.5)


epsilon = 1e-06


def whole(shape):
    return pl.BlockSpec(shape, lambda *_: (0,) * len(shape))


def turned(values):
    return values.astype(jnp.float32).T.astype(values.dtype)


def sinusoid(places, table_width):
    half_width = table_width // 2
    frequency = jnp.exp(-math.log(10000.0) * jnp.arange(half_width, dtype=jnp.float32) / half_width)
    angles = places.astype(jnp.float32)[:, None] * frequency[None, :]
    return jnp.concatenate([jnp.sin(angles), jnp.cos(angles)], axis=1)


def plain_dot(left, right):
    return jnp.dot(left, right, preferred_element_type=jnp.float32)


def lead_dot(left, right):
    return lax.dot_general(
        left, right, (((0,), (0,)), ((), ())), preferred_element_type=jnp.float32
    )


def trail_dot(left, right):
    return lax.dot_general(
        left, right, (((1,), (1,)), ((), ())), preferred_element_type=jnp.float32
    )


def column_sum(values):
    return jnp.sum(values.astype(jnp.float32), axis=0, keepdims=True)


def row_mean(values):
    return jnp.mean(values, axis=-1, keepdims=True)


def normalize(values):
    center = values - row_mean(values)
    scale = lax.rsqrt(row_mean(center * center) + epsilon)
    return center * scale, scale


def normalize_back(grad, normed, scale):
    return scale * (grad - row_mean(grad) - normed * row_mean(grad * normed))


class Spot:
    def __init__(self):
        self.layers, self.splits = lax.axis_size("dp"), lax.axis_size("seq")
        self.half = self.splits // 2
        self.layer, self.index = lax.axis_index("dp"), lax.axis_index("seq")
        self.core, self.chip = self.index % 2, self.index // 2

    def sibling(self):
        return (self.layer, self.chip * 2 + (1 - self.core))

    def chip_at(self, step):
        return (self.chip + step) % self.half

    def layer_at(self, step):
        return (self.layer + step) % self.layers

    def peer(self, step):
        return (self.layer, self.chip_at(step) * 2 + self.core)

    def above(self, step):
        return (self.layer_at(step), self.index)

    def meet(self, others):
        barrier = pltpu.get_barrier_semaphore()
        for other in others:
            pl.semaphore_signal(barrier, inc=1, device_id=other, device_id_type=MESH)
        return len(others)

    def tree(self, layers=True):
        others = [self.sibling()] + [self.peer(step) for step in range(1, self.half)]
        if layers:
            others += [self.above(step) for step in range(1, self.layers)]
        return others


def padded(rows, unit):
    return -(-rows // unit) * unit


def span_of(start, size):
    return pl.ds(pl.multiple_of(start, 16), size)


def send(source, target, sems, at, device):
    return pltpu.make_async_remote_copy(
        src_ref=source,
        dst_ref=target,
        send_sem=sems.at[0, at],
        recv_sem=sems.at[1, at],
        device_id=device,
        device_id_type=MESH,
    )


class TreeSum:
    def __init__(self, spot, source, result, refs, scatter):
        (
            self.near,
            self.near_sum,
            self.far,
            self.far_sum,
            self.deep,
            self.done,
            self.sems,
            self.local,
        ) = refs
        self.spot, self.source, self.result, self.scatter = spot, source, result, scatter
        self.part = self.far_sum.shape[0]
        self.piece = self.done.shape[0]

    @staticmethod
    def scratch(rows, width, scatter, splits, layers):
        half = splits // 2
        part = rows // splits
        piece = part // layers if scatter else part
        low = jnp.bfloat16
        return [
            pltpu.VMEM((half * part, width), low),
            pltpu.VMEM((half * part, width), low),
            pltpu.VMEM((max(half - 1, 1) * part, width), low),
            pltpu.VMEM((part, width), low),
            pltpu.VMEM((layers * piece, width), low),
            pltpu.VMEM((piece, width), low),
            pltpu.SemaphoreType.DMA((2, 2 + 2 * half + 2 * layers)),
            pltpu.SemaphoreType.DMA((2,)),
        ]

    def near_copy(self):
        spot = self.spot
        rows = spot.half * self.part
        return send(
            self.source.at[span_of((1 - spot.core) * rows, rows)],
            self.near,
            self.sems,
            0,
            spot.sibling(),
        )

    def own_copy(self):
        rows = self.spot.half * self.part
        return pltpu.make_async_copy(
            self.source.at[span_of(self.spot.core * rows, rows)], self.near_sum, self.local.at[0]
        )

    def far_copy(self, step):
        return send(
            self.near_sum.at[span_of(self.spot.chip_at(step) * self.part, self.part)],
            self.far.at[span_of((step - 1) * self.part, self.part)],
            self.sems,
            1 + step,
            self.spot.peer(step),
        )

    def deep_copy(self, step):
        spot = self.spot
        if self.scatter:
            source = self.far_sum.at[span_of(spot.layer_at(step) * self.piece, self.piece)]
        else:
            source = self.far_sum
        return send(
            source,
            self.deep.at[span_of(spot.layer * self.piece, self.piece)],
            self.sems,
            1 + spot.half + step,
            spot.above(step),
        )

    def place(self, core, chip, layer=None):
        spot = self.spot
        start = (core * spot.half + chip) * self.part
        if layer is None:
            return span_of(start, self.part)
        return span_of(start + layer * self.piece, self.piece)

    def done_copy(self):
        spot = self.spot
        layer = spot.layer if self.scatter else None
        return pltpu.make_async_copy(
            self.done, self.result.at[self.place(spot.core, spot.chip, layer)], self.local.at[1]
        )

    def layer_copy(self, step, arriving):
        spot = self.spot
        layer = spot.layer_at(-step) if arriving else spot.layer
        return send(
            self.done,
            self.result.at[self.place(spot.core, spot.chip, layer)],
            self.sems,
            1 + spot.half + spot.layers + step,
            spot.above(step),
        )

    def part_copy(self, step, arriving):
        spot = self.spot
        place = self.place(spot.core, spot.chip_at(-step) if arriving else spot.chip)
        return send(
            self.result.at[place] if self.scatter else self.done,
            self.result.at[place],
            self.sems,
            1 + spot.half + 2 * spot.layers + step,
            spot.peer(step),
        )

    def half_copy(self, arriving):
        spot = self.spot
        rows = spot.half * self.part
        core = 1 - spot.core if arriving else spot.core
        place = span_of(core * rows, rows)
        return send(
            self.result.at[place], self.result.at[place], self.sems, 1, spot.sibling()
        )

    def start(self):
        self.own_copy().start()
        self.near_copy().start()

    def near_to_far(self):
        self.own_copy().wait()
        self.near_copy().wait()
        unit = self.part
        while unit > 160 and unit % 32 == 0:
            unit //= 2

        def add(at, _):
            rows = span_of(at * unit, unit)
            self.near_sum[rows, :] = (
                self.near_sum[rows, :].astype(jnp.float32) + self.near[rows, :].astype(jnp.float32)
            ).astype(jnp.bfloat16)
            return 0

        lax.fori_loop(0, self.spot.half * (self.part // unit), add, 0)
        for step in range(1, self.spot.half):
            self.far_copy(step).start()

    def far_to_deep(self):
        spot = self.spot
        for step in range(1, spot.half):
            self.far_copy(step).wait()
        unit = self.part
        while unit > 160 and unit % 32 == 0:
            unit //= 2

        def add(at, _):
            start = at * unit
            total = self.near_sum[span_of(spot.chip * self.part + start, unit), :].astype(
                jnp.float32
            )
            for step in range(1, spot.half):
                total = total + self.far[span_of((step - 1) * self.part + start, unit), :].astype(
                    jnp.float32
                )
            self.far_sum[span_of(start, unit), :] = total.astype(jnp.bfloat16)
            return 0

        lax.fori_loop(0, self.part // unit, add, 0)
        for step in range(1, spot.layers):
            self.deep_copy(step).start()
        own = self.far_sum[...]
        if self.scatter:
            own = self.far_sum[span_of(spot.layer * self.piece, self.piece), :]
        self.deep[span_of(spot.layer * self.piece, self.piece), :] = own

    def deep_to_layer(self):
        spot = self.spot
        for step in range(1, spot.layers):
            self.deep_copy(step).wait_send()
        for step in range(1, spot.layers):
            send(
                self.done,
                self.deep.at[span_of(spot.layer_at(-step) * self.piece, self.piece)],
                self.sems,
                1 + spot.half + step,
                spot.above(step),
            ).wait_recv()
        total = self.deep[: self.piece, :].astype(jnp.float32)
        for layer in range(1, spot.layers):
            total = total + self.deep[layer * self.piece : (layer + 1) * self.piece, :].astype(
                jnp.float32
            )
        self.done[...] = total.astype(jnp.bfloat16)
        self.done_copy().start()
        if self.scatter:
            for step in range(1, spot.layers):
                self.layer_copy(step, False).start()
        else:
            for step in range(1, spot.half):
                self.part_copy(step, False).start()

    def layer_to_part(self):
        spot = self.spot
        if not self.scatter:
            return
        self.done_copy().wait()
        for step in range(1, spot.layers):
            self.layer_copy(step, False).wait_send()
        for step in range(1, spot.layers):
            self.layer_copy(step, True).wait_recv()
        for step in range(1, spot.half):
            self.part_copy(step, False).start()

    def part_to_half(self):
        spot = self.spot
        if not self.scatter:
            self.done_copy().wait()
        for step in range(1, spot.half):
            self.part_copy(step, False).wait_send()
        for step in range(1, spot.half):
            self.part_copy(step, True).wait_recv()
        self.half_copy(False).start()

    def finish(self):
        self.half_copy(False).wait_send()
        self.half_copy(True).wait_recv()


def enter_kernel(
    latents_ref,
    embed_ref,
    embed_bias_ref,
    slot_ref,
    coarse_ref,
    fine_ref,
    mask_ref,
    gain_ref,
    shift_ref,
    joint_ref,
    query_bias_ref,
    value_bias_ref,
    stream_ref,
    empty_ref,
    normed_ref,
    query_t_ref,
    key_ref,
    key_t_ref,
    value_ref,
    value_t_ref,
    embedded_ref,
    sems,
):
    block, width = stream_ref.shape
    spot = Spot()
    capacity = embedded_ref.shape[0] // spot.splits

    @pl.when(pl.program_id(0) == 0)
    def _():
        count = spot.meet(spot.tree(False))
        embedded = plain_dot(latents_ref[...], embed_ref[...]) + embed_bias_ref[...].astype(
            jnp.float32
        )
        if capacity > latents_ref.shape[0]:
            rest = jnp.zeros((capacity - latents_ref.shape[0], width), jnp.float32)
            embedded = jnp.concatenate([embedded, rest], axis=0)

        def held(core, chip):
            return embedded_ref.at[span_of((chip * 2 + core) * capacity, capacity)]

        def share(at, core, chip, device):
            return send(held(core, chip), held(core, chip), sems, at, device)

        embedded_ref[span_of(spot.index * capacity, capacity), :] = embedded.astype(jnp.bfloat16)
        pl.semaphore_wait(pltpu.get_barrier_semaphore(), count)
        for step in range(1, spot.half):
            share(step, spot.core, spot.chip, spot.peer(step)).start()
        share(0, spot.core, spot.chip, spot.sibling()).start()
        for step in range(1, spot.half):
            share(step, spot.core, spot.chip_at(-step), spot.peer(step)).wait_recv()
            share(
                spot.half + step, spot.core, spot.chip_at(-step), spot.sibling()
            ).start()
        for step in range(1, spot.half):
            share(step, spot.core, spot.chip, spot.peer(step)).wait_send()
        share(0, spot.core, spot.chip, spot.sibling()).wait_send()
        share(0, 1 - spot.core, spot.chip, spot.sibling()).wait_recv()
        for step in range(1, spot.half):
            at = spot.half + step
            share(at, spot.core, spot.chip_at(-step), spot.sibling()).wait_send()
            share(at, 1 - spot.core, spot.chip_at(-step), spot.sibling()).wait_recv()

    place = lax.broadcasted_iota(jnp.int32, (block, 1), 0) + pl.program_id(0) * block
    fills = (place == slot_ref[...]).astype(jnp.float32)
    empty = 1.0 - jnp.sum(fills, axis=1, keepdims=True)
    placed = plain_dot(fills.astype(jnp.bfloat16), embedded_ref[...])
    fine_rows = fine_ref.shape[0]
    half = width // 2
    fine_sin, fine_cos = fine_ref[:, :half], fine_ref[:, half:]
    tables = []
    for at in range(block // fine_rows):
        row = coarse_ref[0, at : at + 1, :]
        sin, cos = row[:, :half], row[:, half:]
        tables.append(
            jnp.concatenate(
                [sin * fine_cos + cos * fine_sin, cos * fine_cos - sin * fine_sin], axis=1
            )
        )
    stream = placed + empty * mask_ref[...].astype(jnp.float32) + jnp.concatenate(tables, axis=0)
    stream_ref[...] = stream
    empty_ref[...] = empty
    normed, _ = normalize(stream)
    low = (normed * gain_ref[...].astype(jnp.float32) + shift_ref[...].astype(jnp.float32)).astype(
        jnp.bfloat16
    )
    normed_ref[...] = low
    query = plain_dot(low, joint_ref[:, :width]) + query_bias_ref[...].astype(jnp.float32)
    query_t_ref[...] = (query * QUERY_SCALE).T.astype(jnp.bfloat16)
    keys = plain_dot(low, joint_ref[:, width : 2 * width])
    key_ref[...] = keys.astype(jnp.bfloat16)
    key_t_ref[...] = keys.T.astype(jnp.bfloat16)
    values = plain_dot(low, joint_ref[:, 2 * width :]) + value_bias_ref[...].astype(jnp.float32)
    value_ref[...] = values.astype(jnp.bfloat16)
    value_t_ref[...] = values.T.astype(jnp.bfloat16)


def enter(
    latents,
    embed_weight,
    embed_bias,
    slot_place,
    first_place,
    rows,
    mask_token,
    gain,
    shift,
    joint_weight,
    query_bias,
    value_bias,
):
    splits = lax.axis_size("seq")
    width = embed_weight.shape[1]
    slots = slot_place.shape[0]
    block = min(256, rows)
    fine_rows = min(32, block)
    fine = sinusoid(jnp.arange(fine_rows, dtype=jnp.int32), width)
    coarse = sinusoid(first_place + fine_rows * jnp.arange(rows // fine_rows, dtype=jnp.int32), width)
    row_block = pl.BlockSpec((block, width), lambda i: (i, 0))
    lane_block = pl.BlockSpec((width, block), lambda i: (0, i))
    vector = whole((1, width))
    low = jax.ShapeDtypeStruct((rows, width), jnp.bfloat16)
    low_t = jax.ShapeDtypeStruct((width, rows), jnp.bfloat16)
    return pl.pallas_call(
        enter_kernel,
        grid=(rows // block,),
        in_specs=[
            whole(latents.shape),
            whole(embed_weight.shape),
            vector,
            whole((1, slots)),
            pl.BlockSpec((1, block // fine_rows, width), lambda i: (i, 0, 0)),
            whole(fine.shape),
            vector,
            vector,
            vector,
            whole((width, 3 * width)),
            vector,
            vector,
        ],
        out_specs=[
            row_block,
            pl.BlockSpec((block, 1), lambda i: (i, 0)),
            row_block,
            lane_block,
            row_block,
            lane_block,
            row_block,
            lane_block,
        ],
        out_shape=[
            jax.ShapeDtypeStruct((rows, width), jnp.float32),
            jax.ShapeDtypeStruct((rows, 1), jnp.float32),
            low,
            low_t,
            low,
            low_t,
            low,
            low_t,
        ],
        scratch_shapes=[
            pltpu.VMEM((slots, width), jnp.bfloat16),
            pltpu.SemaphoreType.DMA((2, splits)),
        ],
        compiler_params=pltpu.CompilerParams(
            vmem_limit_bytes=VMEM_LIMIT, collective_id=0, has_side_effects=True
        ),
        cost_estimate=pl.CostEstimate(
            flops=2 * rows * width * (slots + 3 * width),
            bytes_accessed=20 * rows * width,
            transcendentals=0,
        ),
        name="enter",
    )(
        latents,
        embed_weight,
        embed_bias[None, :],
        slot_place[None, :],
        coarse.reshape(rows // block, block // fine_rows, width),
        fine,
        mask_token[None, :],
        gain[None, :],
        shift[None, :],
        joint_weight,
        query_bias[None, :],
        value_bias[None, :],
    )


def attend_kernel(
    key_ref, query_ref, value_ref, mixed_ref, exact_ref, total_ref, raised_ref, scores_ref
):
    span = key_ref.shape[0]
    block = query_ref.shape[1]
    slice_rows = min(256, span)
    query = query_ref[...]
    head_row = lax.broadcasted_iota(jnp.int32, query.shape, 0) // HEAD_DIM
    ones = jnp.ones((16, slice_rows), jnp.bfloat16)
    highest = None
    for step in range(PACK + 1):
        if step < PACK:
            own_query = jnp.where(head_row == step, query, jnp.zeros_like(query))
            partial_highest = jnp.full((8, block), -jnp.inf, jnp.float32)
        if step > 0:
            head = step - 1
            rows = slice(head * HEAD_DIM, (head + 1) * HEAD_DIM)
            mixed = jnp.zeros((HEAD_DIM + 16, block), jnp.float32)
        for at in range(0, span, slice_rows):
            part = slice(at, at + slice_rows)
            if step < PACK:
                scores = plain_dot(key_ref[part, :], own_query)
                scores_ref[step % 2, part, :] = scores
                partial_highest = jnp.maximum(
                    partial_highest, jnp.max(scores.reshape(slice_rows // 8, 8, block), axis=0)
                )
            if step > 0:
                raised = jnp.exp2(scores_ref[(step - 1) % 2, part, :] - highest).astype(
                    jnp.bfloat16
                )
                raised_ref[head, part, :] = raised
                mixed = mixed + plain_dot(
                    jnp.concatenate([value_ref[rows, part], ones], axis=0), raised
                )
        if step > 0:
            total = mixed[HEAD_DIM : HEAD_DIM + 1]
            total_ref[0, head : head + 1, :] = total
            mixed = mixed[:HEAD_DIM] / total
            exact_ref[rows, :] = mixed
            mixed_ref[rows, :] = mixed.astype(jnp.bfloat16)
        if step < PACK:
            highest = jnp.max(partial_highest, axis=0, keepdims=True)


def attend(keys, query_t, value_t):
    width, rows = query_t.shape
    span = keys.shape[0]
    block = min(512, rows)
    groups = width // 128
    lane_block = pl.BlockSpec((128, block), lambda g, i: (g, i))
    return pl.pallas_call(
        attend_kernel,
        grid=(groups, rows // block),
        in_specs=[
            pl.BlockSpec((span, 128), lambda g, i: (0, g)),
            lane_block,
            pl.BlockSpec((128, span), lambda g, i: (g, 0)),
        ],
        out_specs=[
            lane_block,
            lane_block,
            pl.BlockSpec((1, 8, block), lambda g, i: (g, 0, i)),
            pl.BlockSpec((PACK, span, block), lambda g, i: (g, 0, i)),
        ],
        out_shape=[
            jax.ShapeDtypeStruct((width, rows), jnp.bfloat16),
            jax.ShapeDtypeStruct((width, rows), jnp.float32),
            jax.ShapeDtypeStruct((groups, 8, rows), jnp.float32),
            jax.ShapeDtypeStruct((HEADS, span, rows), jnp.bfloat16),
        ],
        scratch_shapes=[pltpu.VMEM((2, span, block), jnp.float32)],
        compiler_params=pltpu.CompilerParams(vmem_limit_bytes=VMEM_LIMIT),
        cost_estimate=pl.CostEstimate(
            flops=HEADS * span * rows * 512,
            bytes_accessed=2 * HEADS * span * rows,
            transcendentals=HEADS * span * rows,
        ),
        name="attend",
    )(keys, query_t, value_t)


def middle_kernel(
    stream_ref,
    mixed_ref,
    cotangent_ref,
    output_ref,
    output_bias_ref,
    gain_ref,
    shift_ref,
    expand_ref,
    expand_bias_ref,
    contract_ref,
    contract_bias_ref,
    decoded_ref,
    grad_middle_ref,
    grad_attended_ref,
    flat_ref,
    small_ref,
    expand_sum,
    contract_sum,
    output_sum,
    small_sum,
):
    width = stream_ref.shape[1]
    chunks = expand_ref.shape[1] // width

    @pl.when(pl.program_id(0) == 0)
    def _():
        expand_sum[...] = jnp.zeros_like(expand_sum)
        contract_sum[...] = jnp.zeros_like(contract_sum)
        output_sum[...] = jnp.zeros_like(output_sum)
        small_sum[...] = jnp.zeros_like(small_sum)

    mixed_t = mixed_ref[...]
    cotangent = cotangent_ref[...]
    middle = (
        stream_ref[...]
        + plain_dot(turned(mixed_t), output_ref[...])
        + output_bias_ref[...].astype(jnp.float32)
    )
    normed, scale = normalize(middle)
    gain = gain_ref[...].astype(jnp.float32)
    low = (normed * gain + shift_ref[...].astype(jnp.float32)).astype(jnp.bfloat16)
    low_t = turned(low)
    output = middle + contract_bias_ref[...].astype(jnp.float32)
    grad_normed = jnp.zeros_like(middle)
    for chunk in range(chunks):
        part = slice(chunk * width, (chunk + 1) * width)
        hidden = plain_dot(low, expand_ref[:, part]) + expand_bias_ref[:, part].astype(jnp.float32)
        below = 0.5 + 0.5 * lax.erf(hidden * math.sqrt(0.5))
        slope = below + hidden * jnp.exp(-0.5 * hidden * hidden) * (1.0 / math.sqrt(2 * math.pi))
        active = (hidden * below).astype(jnp.bfloat16)
        grad_hidden = (trail_dot(cotangent, contract_ref[part, :]) * slope).astype(jnp.bfloat16)
        output = output + plain_dot(active, contract_ref[part, :])
        grad_normed = grad_normed + trail_dot(grad_hidden, expand_ref[:, part])
        contract_sum[part, :] += plain_dot(turned(active), cotangent)
        expand_sum[part, :] += plain_dot(low_t, grad_hidden)
        small_sum[chunk : chunk + 1, :] += column_sum(grad_hidden)
    decoded_ref[...] = output.astype(jnp.bfloat16)
    grad_middle = cotangent.astype(jnp.float32) + normalize_back(grad_normed * gain, normed, scale)
    grad_middle_ref[...] = grad_middle
    branch = grad_middle.astype(jnp.bfloat16)
    grad_attended_ref[...] = trail_dot(output_ref[...], branch).astype(jnp.bfloat16)
    output_sum[...] += plain_dot(mixed_t, branch)
    small_sum[chunks : chunks + 1, :] += column_sum(cotangent)
    small_sum[chunks + 1 : chunks + 2, :] += column_sum(branch)
    small_sum[chunks + 2 : chunks + 3, :] += column_sum(grad_normed * normed)
    small_sum[chunks + 3 : chunks + 4, :] += column_sum(grad_normed)

    @pl.when(pl.program_id(0) == pl.num_programs(0) - 1)
    def _():
        at = 0
        for total in (expand_sum, contract_sum, output_sum):
            flat_ref[at : at + total.shape[0], :] = total[...].astype(flat_ref.dtype)
            at += total.shape[0]
        if at < flat_ref.shape[0]:
            flat_ref[at:, :] = jnp.zeros((flat_ref.shape[0] - at, width), flat_ref.dtype)
        small_ref[...] = small_sum[...]


def middle_block(
    stream,
    mixed_t,
    cotangent,
    output_weight,
    output_bias,
    gain,
    shift,
    expand_weight,
    expand_bias,
    contract_weight,
    contract_bias,
    flat_rows,
):
    rows, width = stream.shape
    hidden = expand_weight.shape[1]
    block = min(256, rows)
    row_block = pl.BlockSpec((block, width), lambda i: (i, 0))
    lane_block = pl.BlockSpec((width, block), lambda i: (0, i))
    vector = whole((1, width))
    small_rows = hidden // width + 4
    return pl.pallas_call(
        middle_kernel,
        grid=(rows // block,),
        in_specs=[
            row_block,
            lane_block,
            row_block,
            whole((width, width)),
            vector,
            vector,
            vector,
            whole((width, hidden)),
            whole((1, hidden)),
            whole((hidden, width)),
            vector,
        ],
        out_specs=[
            row_block,
            row_block,
            lane_block,
            whole((flat_rows, width)),
            whole((small_rows, width)),
        ],
        out_shape=[
            jax.ShapeDtypeStruct((rows, width), jnp.bfloat16),
            jax.ShapeDtypeStruct((rows, width), jnp.float32),
            jax.ShapeDtypeStruct((width, rows), jnp.bfloat16),
            jax.ShapeDtypeStruct((flat_rows, width), jnp.bfloat16),
            jax.ShapeDtypeStruct((small_rows, width), jnp.float32),
        ],
        scratch_shapes=[
            pltpu.VMEM((hidden, width), jnp.float32),
            pltpu.VMEM((hidden, width), jnp.float32),
            pltpu.VMEM((width, width), jnp.float32),
            pltpu.VMEM((small_rows, width), jnp.float32),
        ],
        compiler_params=pltpu.CompilerParams(vmem_limit_bytes=VMEM_LIMIT),
        cost_estimate=pl.CostEstimate(
            flops=2 * rows * width * (6 * hidden + 3 * width),
            bytes_accessed=16 * rows * width,
            transcendentals=2 * rows * hidden,
        ),
        name="middle",
    )(
        stream,
        mixed_t,
        cotangent,
        output_weight,
        output_bias[None, :],
        gain[None, :],
        shift[None, :],
        expand_weight,
        expand_bias[None, :],
        contract_weight,
        contract_bias[None, :],
    )


def attend_back_kernel(
    steps,
    raised_ref,
    total_ref,
    value_ref,
    key_ref,
    query_ref,
    exact_ref,
    grad_ref,
    flat_ref,
    rows_ref,
    grad_query_ref,
    grad_key_ref,
    grad_value_ref,
    summed_ref,
    decoded_ref,
    key_sum,
    value_sum,
    exchange_sems,
    exchange_local,
    *sum_refs,
):
    spot = Spot()
    tree = TreeSum(spot, flat_ref, summed_ref, sum_refs, True)
    clips, share = decoded_ref.shape[0], decoded_ref.shape[1]
    mine, part = spot.index % clips, spot.index // clips

    def member(step):
        return (mine + step) % clips

    def exchange(step):
        return send(
            rows_ref.at[span_of(member(step) * share, share)],
            decoded_ref.at[mine],
            exchange_sems,
            step,
            (spot.layer, part * clips + member(step)),
        )

    def own_rows():
        return pltpu.make_async_copy(
            rows_ref.at[span_of(mine * share, share)], decoded_ref.at[mine], exchange_local
        )

    step_now = pl.program_id(0) * pl.num_programs(1) + pl.program_id(1)

    def at_step(fraction):
        return pl.when(step_now == fraction * steps // 32)

    @at_step(0)
    def _():
        others = spot.tree() + [
            (spot.layer, part * clips + member(step)) for step in range(1, clips)
        ]
        count = spot.meet(others)
        pl.semaphore_wait(pltpu.get_barrier_semaphore(), count)
        tree.start()

    @at_step(2)
    def _():
        tree.near_to_far()

    @at_step(9)
    def _():
        tree.far_to_deep()
        own_rows().start()
        for step in range(1, clips):
            exchange(step).start()

    @at_step(13)
    def _():
        tree.deep_to_layer()

    @at_step(17)
    def _():
        tree.layer_to_part()

    @at_step(25)
    def _():
        tree.part_to_half()

    @at_step(31)
    def _():
        tree.finish()
        own_rows().wait()
        for step in range(1, clips):
            exchange(step).wait_send()
        for step in range(1, clips):
            send(
                rows_ref.at[span_of(mine * share, share)],
                decoded_ref.at[member(-step)],
                exchange_sems,
                step,
                (spot.layer, part * clips + member(step)),
            ).wait_recv()

    @pl.when(pl.program_id(1) == 0)
    def _():
        key_sum[...] = jnp.zeros_like(key_sum)
        value_sum[...] = jnp.zeros_like(value_sum)

    block = query_ref.shape[1]
    head_row = lax.broadcasted_iota(jnp.int32, (128, block), 0) // HEAD_DIM
    head_col = lax.broadcasted_iota(jnp.int32, (block, 128), 1) // HEAD_DIM
    inverse = 1.0 / total_ref[0, 0:PACK]
    inverse = jnp.concatenate(
        [jnp.broadcast_to(inverse[h : h + 1], (HEAD_DIM, block)) for h in range(PACK)], axis=0
    )
    grad_low = (grad_ref[...].astype(jnp.float32) * inverse).astype(jnp.bfloat16)
    grad = grad_low.astype(jnp.float32)
    inner = grad * exact_ref[...]
    grad_turned = grad.T.astype(jnp.bfloat16)
    query_turned = turned(query_ref[...])
    for head in range(PACK):
        rows = slice(head * HEAD_DIM, (head + 1) * HEAD_DIM)
        own_grad = jnp.where(head_row == head, grad_low, jnp.zeros_like(grad_low))
        grad_weight = plain_dot(value_ref[...], own_grad)
        row_inner = jnp.sum(inner[rows], axis=0, keepdims=True)
        raised = raised_ref[head]
        grad_scores = raised * (grad_weight - row_inner).astype(jnp.bfloat16)
        value_sum[...] += plain_dot(
            raised, jnp.where(head_col == head, grad_turned, jnp.zeros_like(grad_turned))
        )
        key_sum[...] += plain_dot(
            grad_scores, jnp.where(head_col == head, query_turned, jnp.zeros_like(query_turned))
        )
        grad_query_ref[rows, :] = (
            plain_dot(key_ref[rows, :], grad_scores) * HEAD_DIM ** (-0.5)
        ).astype(jnp.bfloat16)

    @pl.when(pl.program_id(1) == pl.num_programs(1) - 1)
    def _():
        grad_key_ref[...] = (key_sum[...] * (1.0 / LOG2E)).astype(jnp.bfloat16)
        grad_value_ref[...] = value_sum[...].astype(jnp.bfloat16)


def attend_back(raised, total, values, key_t, query_t, exact_t, grad_t, flat, decoded_rows):
    splits, layers = lax.axis_size("seq"), lax.axis_size("dp")
    clips, share, _ = decoded_rows.shape
    width, rows = query_t.shape
    span = values.shape[0]
    block = min(256, rows)
    groups = width // 128
    lane_block = pl.BlockSpec((128, block), lambda g, i: (g, i))
    return pl.pallas_call(
        partial(attend_back_kernel, groups * (rows // block)),
        grid=(groups, rows // block),
        in_specs=[
            pl.BlockSpec((PACK, span, block), lambda g, i: (g, 0, i)),
            pl.BlockSpec((1, 8, block), lambda g, i: (g, 0, i)),
            pl.BlockSpec((span, 128), lambda g, i: (0, g)),
            pl.BlockSpec((128, span), lambda g, i: (g, 0)),
            lane_block,
            lane_block,
            lane_block,
            pl.BlockSpec(memory_space=pl.ANY),
            pl.BlockSpec(memory_space=pl.ANY),
        ],
        out_specs=[
            lane_block,
            pl.BlockSpec((span, 128), lambda g, i: (0, g)),
            pl.BlockSpec((span, 128), lambda g, i: (0, g)),
            pl.BlockSpec(memory_space=pl.ANY),
            pl.BlockSpec(memory_space=pl.ANY),
        ],
        out_shape=[
            jax.ShapeDtypeStruct((width, rows), jnp.bfloat16),
            jax.ShapeDtypeStruct((span, width), jnp.bfloat16),
            jax.ShapeDtypeStruct((span, width), jnp.bfloat16),
            jax.ShapeDtypeStruct(flat.shape, flat.dtype),
            jax.ShapeDtypeStruct(decoded_rows.shape, decoded_rows.dtype),
        ],
        scratch_shapes=[
            pltpu.VMEM((span, 128), jnp.float32),
            pltpu.VMEM((span, 128), jnp.float32),
            pltpu.SemaphoreType.DMA((2, clips)),
            pltpu.SemaphoreType.DMA,
        ]
        + TreeSum.scratch(flat.shape[0], flat.shape[1], True, splits, layers),
        compiler_params=pltpu.CompilerParams(
            vmem_limit_bytes=VMEM_LIMIT, collective_id=1, has_side_effects=True
        ),
        cost_estimate=pl.CostEstimate(
            flops=HEADS * span * rows * 1024,
            bytes_accessed=2 * HEADS * span * rows,
            transcendentals=0,
        ),
        name="attend_back",
    )(raised, total, values, key_t, query_t, exact_t, grad_t, flat, decoded_rows.reshape(clips * share, width))


def leave_kernel(
    grad_query_ref,
    grad_key_ref,
    grad_value_ref,
    stream_ref,
    empty_ref,
    low_ref,
    grad_middle_ref,
    gain_ref,
    joint_ref,
    slot_ref,
    latents_ref,
    embed_ref,
    early_ref,
    latent_grad_ref,
    joint_total_ref,
    embed_total_ref,
    joint_sum,
    small_sum,
    grad_all,
    joint_flat,
    embed_flat,
    near_out,
    near_in,
    far_out,
    far_in,
    sems,
    *sum_refs,
):
    block, width = stream_ref.shape
    step_now = pl.program_id(0)
    spot = Spot()
    capacity = near_out.shape[0] // spot.half
    others = spot.tree()

    @pl.when(step_now == 0)
    def _():
        spot.meet(others)
        joint_sum[...] = jnp.zeros_like(joint_sum)
        small_sum[...] = jnp.zeros_like(small_sum)

    normed, scale = normalize(stream_ref[...])
    low_t = turned(low_ref[...])
    sides = [turned(grad_query_ref[...]), grad_key_ref[...], grad_value_ref[...]]
    grad_normed = jnp.zeros_like(normed)
    for at, side in enumerate(sides):
        grad_normed = grad_normed + trail_dot(side, joint_ref[:, at * width : (at + 1) * width])
        joint_sum[at * width : (at + 1) * width, :] += plain_dot(low_t, side)
    grad_stream = grad_middle_ref[...] + normalize_back(
        grad_normed * gain_ref[...].astype(jnp.float32), normed, scale
    )
    grad_all[pl.ds(pl.multiple_of(step_now * block, block), block), :] = grad_stream.astype(
        jnp.bfloat16
    )
    small_sum[0:1, :] += column_sum(empty_ref[...] * grad_stream)
    small_sum[1:2, :] += column_sum(grad_normed * normed)
    small_sum[2:3, :] += column_sum(grad_normed)
    small_sum[3:4, :] += column_sum(sides[0])
    small_sum[4:5, :] += column_sum(sides[2])

    @pl.when(step_now == pl.num_programs(0) - 1)
    def _():
        count = len(sum_refs) // 2
        joint_tree = TreeSum(spot, joint_flat, joint_total_ref, sum_refs[:count], False)
        embed_tree = TreeSum(spot, embed_flat, embed_total_ref, sum_refs[count:], False)
        joint_flat[...] = joint_sum[...].astype(jnp.bfloat16)
        pl.semaphore_wait(pltpu.get_barrier_semaphore(), len(others))
        joint_tree.start()
        place = lax.broadcasted_iota(jnp.int32, (1, grad_all.shape[0]), 1)

        def gathered(owner):
            slots = slot_ref[pl.ds(pl.multiple_of(owner * capacity, 8), capacity), :]
            takes = (slots == place).astype(jnp.float32).astype(jnp.bfloat16)
            return plain_dot(takes, grad_all[...])

        def part(at):
            return pl.ds(at * capacity, capacity)

        def near_copy(step):
            return send(
                near_out.at[part(step)], near_in.at[part(step)], sems, step, spot.sibling()
            )

        def far_copy(step):
            return send(
                far_out.at[part(step - 1)],
                far_in.at[part(step - 1)],
                sems,
                spot.half + step,
                spot.peer(step),
            )

        order = list(range(1, spot.half)) + [0]
        for step in order:
            near_out[part(step), :] = gathered(spot.chip_at(step) * 2 + 1 - spot.core).astype(
                jnp.bfloat16
            )
            near_copy(step).start()
        joint_tree.near_to_far()
        for step in order:
            near_copy(step).wait()
            own = gathered(spot.chip_at(step) * 2 + spot.core)
            own = own + near_in[part(step), :].astype(jnp.float32)
            if step > 0:
                far_out[part(step - 1), :] = own.astype(jnp.bfloat16)
                far_copy(step).start()
        for step in range(1, spot.half):
            far_copy(step).wait()
            own = own + far_in[part(step - 1), :].astype(jnp.float32)
        grad_embedded = own[: latents_ref.shape[0]].astype(jnp.bfloat16)
        small_sum[5:6, :] = column_sum(grad_embedded)
        embed_rows = embed_ref.shape[0]
        embed_flat[:embed_rows, :] = lead_dot(latents_ref[...], grad_embedded).astype(jnp.bfloat16)
        small = jnp.concatenate([early_ref[...], small_sum[...]], axis=0)
        rest = embed_flat.shape[0] - embed_rows - small.shape[0]
        if rest:
            small = jnp.concatenate([small, jnp.zeros((rest, width), jnp.float32)], axis=0)
        embed_flat[embed_rows:, :] = small.astype(jnp.bfloat16)
        embed_tree.start()
        latent_grad_ref[...] = trail_dot(grad_embedded, embed_ref[...]).astype(jnp.bfloat16)
        joint_tree.far_to_deep()
        embed_tree.near_to_far()
        joint_tree.deep_to_layer()
        embed_tree.far_to_deep()
        joint_tree.part_to_half()
        embed_tree.deep_to_layer()
        joint_tree.finish()
        embed_tree.part_to_half()
        embed_tree.finish()


def leave(
    grad_query_t,
    grad_key,
    grad_value,
    stream,
    empty,
    low,
    grad_middle,
    gain,
    joint_weight,
    slot_place,
    latents,
    embed_weight,
    early_small,
):
    splits, layers = lax.axis_size("seq"), lax.axis_size("dp")
    rows, width = stream.shape
    slots = slot_place.shape[0]
    capacity = slots // splits
    half = splits // 2
    block = min(256, rows)
    row_block = pl.BlockSpec((block, width), lambda i: (i, 0))
    lane_block = pl.BlockSpec((width, block), lambda i: (0, i))
    joint_rows = padded(3 * width, splits * 16)
    embed_rows = padded(embed_weight.shape[0] + early_small.shape[0] + 8, splits * 16)
    return pl.pallas_call(
        leave_kernel,
        grid=(rows // block,),
        in_specs=[
            lane_block,
            row_block,
            row_block,
            row_block,
            pl.BlockSpec((block, 1), lambda i: (i, 0)),
            row_block,
            row_block,
            whole((1, width)),
            whole((width, 3 * width)),
            whole((slots, 1)),
            whole(latents.shape),
            whole(embed_weight.shape),
            whole(early_small.shape),
        ],
        out_specs=[
            whole(latents.shape),
            pl.BlockSpec(memory_space=pl.ANY),
            pl.BlockSpec(memory_space=pl.ANY),
        ],
        out_shape=[
            jax.ShapeDtypeStruct(latents.shape, jnp.bfloat16),
            jax.ShapeDtypeStruct((joint_rows, width), jnp.bfloat16),
            jax.ShapeDtypeStruct((embed_rows, width), jnp.bfloat16),
        ],
        scratch_shapes=[
            pltpu.VMEM((3 * width, width), jnp.float32),
            pltpu.VMEM((8, width), jnp.float32),
            pltpu.VMEM((rows, width), jnp.bfloat16),
            pltpu.VMEM((joint_rows, width), jnp.bfloat16),
            pltpu.VMEM((embed_rows, width), jnp.bfloat16),
            pltpu.VMEM((half * capacity, width), jnp.bfloat16),
            pltpu.VMEM((half * capacity, width), jnp.bfloat16),
            pltpu.VMEM((max(half - 1, 1) * capacity, width), jnp.bfloat16),
            pltpu.VMEM((max(half - 1, 1) * capacity, width), jnp.bfloat16),
            pltpu.SemaphoreType.DMA((2, splits)),
        ]
        + TreeSum.scratch(joint_rows, width, False, splits, layers)
        + TreeSum.scratch(embed_rows, width, False, splits, layers),
        compiler_params=pltpu.CompilerParams(
            vmem_limit_bytes=VMEM_LIMIT, collective_id=2, has_side_effects=True
        ),
        cost_estimate=pl.CostEstimate(
            flops=2 * rows * width * (slots + 6 * width),
            bytes_accessed=20 * rows * width,
            transcendentals=0,
        ),
        name="leave",
    )(
        grad_query_t,
        grad_key,
        grad_value,
        stream,
        empty,
        low,
        grad_middle,
        gain[None, :],
        joint_weight,
        slot_place[:, None],
        latents,
        embed_weight,
        early_small,
    )


def body(
    latents,
    clip_ids,
    restore,
    counts,
    embed_weight,
    embed_bias,
    mask_token,
    first_gain,
    first_shift,
    joint_weight,
    query_bias,
    value_bias,
    output_weight,
    output_bias,
    second_gain,
    second_shift,
    expand_weight,
    expand_bias,
    contract_weight,
    contract_bias,
    cotangent,
):
    splits = lax.axis_size("seq")
    seq_index = lax.axis_index("seq")
    capacity = latents.shape[0]
    clip_count, clip_share, model_width = cotangent.shape
    sharers = splits // clip_count
    rows = clip_count * clip_share
    own_clip = seq_index % clip_count
    first_place = (seq_index // clip_count) * rows
    exchange_groups = [[s * clip_count + c for c in range(clip_count)] for s in range(sharers)]
    clip_groups = [[s * clip_count + c for s in range(sharers)] for c in range(clip_count)]

    def to_clips(blocks):
        return lax.all_to_all(
            blocks,
            "seq",
            split_axis=0,
            concat_axis=0,
            tiled=True,
            axis_index_groups=exchange_groups if sharers > 1 else None,
        )

    live = jnp.arange(capacity, dtype=jnp.int32)[None, :] < counts[:, None]
    mine = live & ((clip_ids % clip_count).reshape(splits, capacity) == own_clip)
    slot_place = jnp.where(mine, restore.reshape(splits, capacity) - first_place, -1)
    slot_place = jnp.pad(
        slot_place, ((0, 0), (0, padded(capacity, 16) - capacity)), constant_values=-1
    ).reshape(-1)

    stream, empty, first_low, query_t, keys, key_t, values, value_t = enter(
        latents,
        embed_weight,
        embed_bias,
        slot_place,
        first_place,
        rows,
        mask_token,
        first_gain,
        first_shift,
        joint_weight,
        query_bias,
        value_bias,
    )
    cotangent, keys = lax.optimization_barrier((cotangent, keys))
    grad_output = to_clips(cotangent).reshape(rows, model_width)
    if sharers > 1:
        keys = lax.all_gather(keys, "seq", axis=0, tiled=True, axis_index_groups=clip_groups)
        values = lax.all_gather(values, "seq", axis=0, tiled=True, axis_index_groups=clip_groups)
        key_t, value_t = keys.T, values.T
    mixed_t, exact_t, total, raised = attend(keys, query_t, value_t)
    (
        decoded_rows,
        grad_middle,
        grad_attended_t,
        early_flat,
        early_small,
    ) = middle_block(
        stream,
        mixed_t,
        grad_output,
        output_weight,
        output_bias,
        second_gain,
        second_shift,
        expand_weight,
        expand_bias,
        contract_weight,
        contract_bias,
        padded(2 * expand_weight.shape[1] + model_width, splits * lax.axis_size("dp") * 16),
    )
    grad_query_t, grad_key, grad_value, early_sum, decoded = attend_back(
        raised,
        total,
        values,
        key_t,
        query_t,
        exact_t,
        grad_attended_t,
        early_flat,
        decoded_rows.reshape(clip_count, clip_share, model_width),
    )
    if sharers > 1:
        grad_key, grad_value = (
            lax.psum_scatter(
                side, "seq", scatter_dimension=0, tiled=True, axis_index_groups=clip_groups
            )
            for side in (grad_key, grad_value)
        )
    latent_grad, joint_sum, embed_sum = leave(
        grad_query_t,
        grad_key,
        grad_value,
        stream,
        empty,
        first_low,
        grad_middle,
        first_gain,
        joint_weight,
        slot_place,
        latents,
        embed_weight,
        early_small,
    )

    def columns(stack):
        return jnp.concatenate(jnp.split(stack, stack.shape[0] // model_width, axis=0), axis=1)

    hidden_width = expand_weight.shape[1]
    chunks = hidden_width // model_width
    grad_expand = columns(early_sum[:hidden_width])
    grad_contract = early_sum[hidden_width : 2 * hidden_width]
    grad_output_weight = early_sum[2 * hidden_width : 2 * hidden_width + model_width]
    grad_expand, grad_contract, grad_output_weight = (
        summed.astype(jnp.float32) for summed in (grad_expand, grad_contract, grad_output_weight)
    )
    grad_joint_weight = columns(joint_sum.astype(jnp.float32))
    at = embed_weight.shape[0]
    grad_embed_weight = embed_sum[:at].astype(jnp.float32)
    small = embed_sum[at:].astype(jnp.float32)
    grad_expand_bias = small[:chunks].reshape(-1)
    grad_contract_bias, grad_output_bias, grad_second_gain, grad_second_shift = small[
        chunks : chunks + 4
    ]
    (
        grad_mask,
        grad_first_gain,
        grad_first_shift,
        grad_query_bias,
        grad_value_bias,
        grad_embed_bias,
    ) = small[chunks + 4 : chunks + 10]
    return (
        decoded,
        latent_grad,
        grad_embed_weight,
        grad_embed_bias,
        grad_mask,
        grad_first_gain,
        grad_first_shift,
        grad_joint_weight,
        grad_query_bias,
        grad_value_bias,
        grad_output_weight,
        grad_output_bias,
        grad_second_gain,
        grad_second_shift,
        grad_expand,
        grad_expand_bias,
        grad_contract,
        grad_contract_bias,
    )


def solution(mesh):
    placed = (
        (P(("dp", "seq"), None),) + (P("dp"),) * 3 + (P(),) * 16 + (P("dp", "seq", None),)
    )
    return jax.shard_map(
        body,
        mesh=mesh,
        in_specs=placed,
        out_specs=(P("dp", "seq", None), P(("dp", "seq"), None)) + (P(),) * 16,
        check_vma=False,
    )
```

```python
from functools import partial
import math

import jax
import jax.numpy as jnp
from jax import lax
from jax.experimental import pallas as pl
from jax.experimental.pallas import tpu as pltpu
from jax.sharding import PartitionSpec as P

HEADS = 16
HEAD_DIM = 32
PACK = 128 // HEAD_DIM
VMEM_LIMIT = 56 * 1024 * 1024
SAFE_SCORE = 80.0
MESH = pl.DeviceIdType.MESH
LOG2E = math.log2(math.e)
QUERY_SCALE = LOG2E * HEAD_DIM ** (-0.5)


epsilon = 1e-06


EMBED_BIAS, MASK, FIRST_GAIN, FIRST_SHIFT, QUERY_BIAS, VALUE_BIAS = range(6)
OUTPUT_BIAS, SECOND_GAIN, SECOND_SHIFT, CONTRACT_BIAS, EXPAND_BIAS = range(6, 11)


def whole(shape):
    return pl.BlockSpec(shape, lambda *_: (0,) * len(shape))


def turned(values):
    return values.astype(jnp.float32).T.astype(values.dtype)


def sinusoid(places, table_width):
    half_width = table_width // 2
    frequency = jnp.exp(-math.log(10000.0) * jnp.arange(half_width, dtype=jnp.float32) / half_width)
    angles = places.astype(jnp.float32)[:, None] * frequency[None, :]
    return jnp.concatenate([jnp.sin(angles), jnp.cos(angles)], axis=1)


def plain_dot(left, right):
    return jnp.dot(left, right, preferred_element_type=jnp.float32)


def lead_dot(left, right):
    return lax.dot_general(
        left, right, (((0,), (0,)), ((), ())), preferred_element_type=jnp.float32
    )


def trail_dot(left, right):
    return lax.dot_general(
        left, right, (((1,), (1,)), ((), ())), preferred_element_type=jnp.float32
    )


def column_sum(values):
    return jnp.sum(values.astype(jnp.float32), axis=0, keepdims=True)


def row_mean(values):
    return jnp.mean(values, axis=-1, keepdims=True)


def normalize(values):
    center = values - row_mean(values)
    scale = lax.rsqrt(row_mean(center * center) + epsilon)
    return center * scale, scale


def normalize_back(grad, normed, scale):
    return scale * (grad - row_mean(grad) - normed * row_mean(grad * normed))


class Spot:
    def __init__(self):
        self.layers, self.splits = lax.axis_size("dp"), lax.axis_size("seq")
        self.half = self.splits // 2
        self.layer, self.index = lax.axis_index("dp"), lax.axis_index("seq")
        self.core, self.chip = self.index % 2, self.index // 2

    def sibling(self):
        return (self.layer, self.chip * 2 + (1 - self.core))

    def chip_at(self, step):
        return (self.chip + step) % self.half

    def layer_at(self, step):
        return (self.layer + step) % self.layers

    def peer(self, step):
        return (self.layer, self.chip_at(step) * 2 + self.core)

    def above(self, step):
        return (self.layer_at(step), self.index)

    def meet(self, others):
        barrier = pltpu.get_barrier_semaphore()
        for other in others:
            pl.semaphore_signal(barrier, inc=1, device_id=other, device_id_type=MESH)
        return len(others)

    def tree(self, layers=True):
        others = [self.sibling()] + [self.peer(step) for step in range(1, self.half)]
        if layers:
            others += [self.above(step) for step in range(1, self.layers)]
        return others


def padded(rows, unit):
    return -(-rows // unit) * unit


def span_of(start, size):
    return pl.ds(pl.multiple_of(start, 16), size)


def send(source, target, sems, at, device):
    return pltpu.make_async_remote_copy(
        src_ref=source,
        dst_ref=target,
        send_sem=sems.at[0, at],
        recv_sem=sems.at[1, at],
        device_id=device,
        device_id_type=MESH,
    )


class TreeSum:
    def __init__(self, spot, source, result, refs, scatter):
        (
            self.near,
            self.near_sum,
            self.far,
            self.far_sum,
            self.deep,
            self.done,
            self.sems,
            self.local,
        ) = refs
        self.spot, self.source, self.result, self.scatter = spot, source, result, scatter
        self.part = self.far_sum.shape[0]
        self.piece = self.done.shape[0]

    @staticmethod
    def scratch(rows, width, scatter, splits, layers):
        half = splits // 2
        part = rows // splits
        piece = part // layers if scatter else part
        low = jnp.bfloat16
        return [
            pltpu.VMEM((half * part, width), low),
            pltpu.VMEM((half * part, width), low),
            pltpu.VMEM((max(half - 1, 1) * part, width), low),
            pltpu.VMEM((part, width), low),
            pltpu.VMEM((layers * piece, width), low),
            pltpu.VMEM((piece, width), low),
            pltpu.SemaphoreType.DMA((2, 2 + 2 * half + 2 * layers)),
            pltpu.SemaphoreType.DMA((2,)),
        ]

    def near_copy(self):
        spot = self.spot
        rows = spot.half * self.part
        return send(
            self.source.at[span_of((1 - spot.core) * rows, rows)],
            self.near,
            self.sems,
            0,
            spot.sibling(),
        )

    def own_copy(self):
        rows = self.spot.half * self.part
        return pltpu.make_async_copy(
            self.source.at[span_of(self.spot.core * rows, rows)], self.near_sum, self.local.at[0]
        )

    def far_copy(self, step):
        return send(
            self.near_sum.at[span_of(self.spot.chip_at(step) * self.part, self.part)],
            self.far.at[span_of((step - 1) * self.part, self.part)],
            self.sems,
            1 + step,
            self.spot.peer(step),
        )

    def deep_copy(self, step):
        spot = self.spot
        if self.scatter:
            source = self.far_sum.at[span_of(spot.layer_at(step) * self.piece, self.piece)]
        else:
            source = self.far_sum
        return send(
            source,
            self.deep.at[span_of(spot.layer * self.piece, self.piece)],
            self.sems,
            1 + spot.half + step,
            spot.above(step),
        )

    def place(self, core, chip, layer=None):
        spot = self.spot
        start = (core * spot.half + chip) * self.part
        if layer is None:
            return span_of(start, self.part)
        return span_of(start + layer * self.piece, self.piece)

    def done_copy(self):
        spot = self.spot
        layer = spot.layer if self.scatter else None
        return pltpu.make_async_copy(
            self.done, self.result.at[self.place(spot.core, spot.chip, layer)], self.local.at[1]
        )

    def layer_copy(self, step, arriving):
        spot = self.spot
        layer = spot.layer_at(-step) if arriving else spot.layer
        return send(
            self.done,
            self.result.at[self.place(spot.core, spot.chip, layer)],
            self.sems,
            1 + spot.half + spot.layers + step,
            spot.above(step),
        )

    def part_copy(self, step, arriving):
        spot = self.spot
        place = self.place(spot.core, spot.chip_at(-step) if arriving else spot.chip)
        return send(
            self.result.at[place] if self.scatter else self.done,
            self.result.at[place],
            self.sems,
            1 + spot.half + 2 * spot.layers + step,
            spot.peer(step),
        )

    def half_copy(self, arriving):
        spot = self.spot
        rows = spot.half * self.part
        core = 1 - spot.core if arriving else spot.core
        place = span_of(core * rows, rows)
        return send(
            self.result.at[place], self.result.at[place], self.sems, 1, spot.sibling()
        )

    def start(self):
        self.own_copy().start()
        self.near_copy().start()

    def near_to_far(self):
        self.own_copy().wait()
        self.near_copy().wait()
        unit = self.part
        while unit > 160 and unit % 32 == 0:
            unit //= 2

        def add(at, _):
            rows = span_of(at * unit, unit)
            self.near_sum[rows, :] = (
                self.near_sum[rows, :].astype(jnp.float32) + self.near[rows, :].astype(jnp.float32)
            ).astype(jnp.bfloat16)
            return 0

        lax.fori_loop(0, self.spot.half * (self.part // unit), add, 0)
        for step in range(1, self.spot.half):
            self.far_copy(step).start()

    def far_to_deep(self):
        spot = self.spot
        for step in range(1, spot.half):
            self.far_copy(step).wait()
        unit = self.part
        while unit > 160 and unit % 32 == 0:
            unit //= 2

        def add(at, _):
            start = at * unit
            total = self.near_sum[span_of(spot.chip * self.part + start, unit), :].astype(
                jnp.float32
            )
            for step in range(1, spot.half):
                total = total + self.far[span_of((step - 1) * self.part + start, unit), :].astype(
                    jnp.float32
                )
            self.far_sum[span_of(start, unit), :] = total.astype(jnp.bfloat16)
            return 0

        lax.fori_loop(0, self.part // unit, add, 0)
        for step in range(1, spot.layers):
            self.deep_copy(step).start()
        own = self.far_sum[...]
        if self.scatter:
            own = self.far_sum[span_of(spot.layer * self.piece, self.piece), :]
        self.deep[span_of(spot.layer * self.piece, self.piece), :] = own

    def deep_to_layer(self):
        spot = self.spot
        for step in range(1, spot.layers):
            self.deep_copy(step).wait_send()
        for step in range(1, spot.layers):
            send(
                self.done,
                self.deep.at[span_of(spot.layer_at(-step) * self.piece, self.piece)],
                self.sems,
                1 + spot.half + step,
                spot.above(step),
            ).wait_recv()
        total = self.deep[: self.piece, :].astype(jnp.float32)
        for layer in range(1, spot.layers):
            total = total + self.deep[layer * self.piece : (layer + 1) * self.piece, :].astype(
                jnp.float32
            )
        self.done[...] = total.astype(jnp.bfloat16)
        self.done_copy().start()
        if self.scatter:
            for step in range(1, spot.layers):
                self.layer_copy(step, False).start()
        else:
            for step in range(1, spot.half):
                self.part_copy(step, False).start()

    def layer_to_part(self):
        spot = self.spot
        if not self.scatter:
            return
        self.done_copy().wait()
        for step in range(1, spot.layers):
            self.layer_copy(step, False).wait_send()
        for step in range(1, spot.layers):
            self.layer_copy(step, True).wait_recv()
        for step in range(1, spot.half):
            self.part_copy(step, False).start()

    def part_to_half(self):
        spot = self.spot
        if not self.scatter:
            self.done_copy().wait()
        for step in range(1, spot.half):
            self.part_copy(step, False).wait_send()
        for step in range(1, spot.half):
            self.part_copy(step, True).wait_recv()
        self.half_copy(False).start()

    def finish(self):
        self.half_copy(False).wait_send()
        self.half_copy(True).wait_recv()


def enter_kernel(
    latents_ref,
    embed_ref,
    slot_ref,
    coarse_ref,
    fine_ref,
    joint_ref,
    *refs,
):
    (
        stream_ref,
        empty_ref,
        normed_ref,
        query_t_ref,
        key_ref,
        key_t_ref,
        value_ref,
        value_t_ref,
        vector_ref,
        latents_out_ref,
        embedded_ref,
        slot_row,
        sems,
    ) = refs[-13:]
    vector_refs = refs[:-13]
    block, width = stream_ref.shape
    spot = Spot()
    capacity = embedded_ref.shape[0] // spot.splits

    def vector(row):
        return vector_ref[row : row + 1, :]

    @pl.when(pl.program_id(0) == 0)
    def _():
        count = spot.meet(spot.tree(False))
        at = 0
        for source in vector_refs:
            for start in range(0, source.shape[0], width):
                values = source[start : start + width].astype(jnp.float32)
                vector_ref[at : at + 1, :] = values.reshape(1, width)
                at += 1
        latents = latents_ref[...]
        rest = capacity - latents.shape[0]
        if rest:
            latents = jnp.concatenate(
                [latents.astype(jnp.float32), jnp.zeros((rest, latents.shape[1]), jnp.float32)],
                axis=0,
            ).astype(jnp.bfloat16)
        latents_out_ref[...] = latents
        embedded = plain_dot(latents, embed_ref[...]) + vector(EMBED_BIAS)

        def held(core, chip):
            return embedded_ref.at[span_of((chip * 2 + core) * capacity, capacity)]

        def share(at, core, chip, device):
            return send(held(core, chip), held(core, chip), sems, at, device)

        embedded_ref[span_of(spot.index * capacity, capacity), :] = embedded.astype(jnp.bfloat16)
        pl.semaphore_wait(pltpu.get_barrier_semaphore(), count)
        for step in range(1, spot.half):
            share(step, spot.core, spot.chip, spot.peer(step)).start()
        share(0, spot.core, spot.chip, spot.sibling()).start()
        for source in range(spot.splits):
            slot_row[:, source * capacity : (source + 1) * capacity] = slot_ref[
                source : source + 1, :capacity
            ]
        for step in range(1, spot.half):
            share(step, spot.core, spot.chip_at(-step), spot.peer(step)).wait_recv()
            share(spot.half + step, spot.core, spot.chip_at(-step), spot.sibling()).start()
        for step in range(1, spot.half):
            share(step, spot.core, spot.chip, spot.peer(step)).wait_send()
        share(0, spot.core, spot.chip, spot.sibling()).wait_send()
        share(0, 1 - spot.core, spot.chip, spot.sibling()).wait_recv()
        for step in range(1, spot.half):
            at = spot.half + step
            share(at, spot.core, spot.chip_at(-step), spot.sibling()).wait_send()
            share(at, 1 - spot.core, spot.chip_at(-step), spot.sibling()).wait_recv()

    place = lax.broadcasted_iota(jnp.int32, (block, 1), 0) + pl.program_id(0) * block
    fills = (place == slot_row[...]).astype(jnp.float32)
    empty = 1.0 - jnp.sum(fills, axis=1, keepdims=True)
    placed = plain_dot(fills.astype(jnp.bfloat16), embedded_ref[...])
    fine_rows = fine_ref.shape[0]
    half = width // 2
    fine_sin, fine_cos = fine_ref[:, :half], fine_ref[:, half:]
    tables = []
    for at in range(block // fine_rows):
        row = coarse_ref[0, at : at + 1, :]
        sin, cos = row[:, :half], row[:, half:]
        tables.append(
            jnp.concatenate(
                [sin * fine_cos + cos * fine_sin, cos * fine_cos - sin * fine_sin], axis=1
            )
        )
    stream = placed + empty * vector(MASK) + jnp.concatenate(tables, axis=0)
    stream_ref[...] = stream
    empty_ref[...] = empty
    normed, _ = normalize(stream)
    low = (normed * vector(FIRST_GAIN) + vector(FIRST_SHIFT)).astype(jnp.bfloat16)
    normed_ref[...] = low
    query = plain_dot(low, joint_ref[:, :width]) + vector(QUERY_BIAS)
    query_t_ref[...] = (query * QUERY_SCALE).T.astype(jnp.bfloat16)
    keys = plain_dot(low, joint_ref[:, width : 2 * width])
    key_ref[...] = keys.astype(jnp.bfloat16)
    key_t_ref[...] = keys.T.astype(jnp.bfloat16)
    values = plain_dot(low, joint_ref[:, 2 * width :]) + vector(VALUE_BIAS)
    value_ref[...] = values.astype(jnp.bfloat16)
    value_t_ref[...] = values.T.astype(jnp.bfloat16)


def enter(
    latents,
    embed_weight,
    slot_place,
    first_place,
    rows,
    vectors,
    joint_weight,
):
    splits = lax.axis_size("seq")
    width = embed_weight.shape[1]
    capacity = padded(latents.shape[0], 16)
    slots = splits * capacity
    vector_rows = sum(vector.shape[0] for vector in vectors) // width
    block = min(256, rows)
    fine_rows = min(32, block)
    fine = sinusoid(jnp.arange(fine_rows, dtype=jnp.int32), width)
    coarse = sinusoid(first_place + fine_rows * jnp.arange(rows // fine_rows, dtype=jnp.int32), width)
    row_block = pl.BlockSpec((block, width), lambda i: (i, 0))
    lane_block = pl.BlockSpec((width, block), lambda i: (0, i))
    low = jax.ShapeDtypeStruct((rows, width), jnp.bfloat16)
    low_t = jax.ShapeDtypeStruct((width, rows), jnp.bfloat16)
    return pl.pallas_call(
        enter_kernel,
        grid=(rows // block,),
        in_specs=[
            whole(latents.shape),
            whole(embed_weight.shape),
            whole(slot_place.shape),
            pl.BlockSpec((1, block // fine_rows, width), lambda i: (i, 0, 0)),
            whole(fine.shape),
            whole((width, 3 * width)),
        ]
        + [whole(vector.shape) for vector in vectors],
        out_specs=[
            row_block,
            pl.BlockSpec((block, 1), lambda i: (i, 0)),
            row_block,
            lane_block,
            row_block,
            lane_block,
            row_block,
            lane_block,
            whole((vector_rows, width)),
            whole((capacity, latents.shape[1])),
        ],
        out_shape=[
            jax.ShapeDtypeStruct((rows, width), jnp.float32),
            jax.ShapeDtypeStruct((rows, 1), jnp.float32),
            low,
            low_t,
            low,
            low_t,
            low,
            low_t,
            jax.ShapeDtypeStruct((vector_rows, width), jnp.float32),
            jax.ShapeDtypeStruct((capacity, latents.shape[1]), latents.dtype),
        ],
        scratch_shapes=[
            pltpu.VMEM((slots, width), jnp.bfloat16),
            pltpu.VMEM((1, slots), jnp.int32),
            pltpu.SemaphoreType.DMA((2, splits)),
        ],
        compiler_params=pltpu.CompilerParams(
            vmem_limit_bytes=VMEM_LIMIT, collective_id=0, has_side_effects=True
        ),
        cost_estimate=pl.CostEstimate(
            flops=2 * rows * width * (slots + 3 * width),
            bytes_accessed=20 * rows * width,
            transcendentals=0,
        ),
        name="enter",
    )(
        latents,
        embed_weight,
        slot_place,
        coarse.reshape(rows // block, block // fine_rows, width),
        fine,
        joint_weight,
        *vectors,
    )


def attend_kernel(
    key_ref, query_ref, value_ref, mixed_ref, exact_ref, total_ref, raised_ref, scores_ref, norm_ref
):
    span = key_ref.shape[0]
    block = query_ref.shape[1]
    slice_rows = min(256, span)
    slices = span // slice_rows
    query = query_ref[...]
    head_row = lax.broadcasted_iota(jnp.int32, query.shape, 0) // HEAD_DIM
    ones = jnp.ones((16, slice_rows), jnp.bfloat16)

    @pl.when(pl.program_id(1) == 0)
    def _():
        keys = key_ref[...].astype(jnp.float32)
        lane_head = lax.broadcasted_iota(jnp.int32, (128, 128), 0) // HEAD_DIM
        column = lax.broadcasted_iota(jnp.int32, (128, 128), 1)
        pick = (lane_head == column).astype(jnp.float32).astype(jnp.bfloat16)
        norms = plain_dot((keys * keys).astype(jnp.bfloat16), pick)
        norm_ref[...] = jnp.broadcast_to(jnp.max(norms, axis=0, keepdims=True), norm_ref.shape)

    squares = query.astype(jnp.float32)
    squares = squares * squares
    bound = jnp.zeros((1, 1), jnp.float32)
    for head in range(PACK):
        rows = slice(head * HEAD_DIM, (head + 1) * HEAD_DIM)
        longest = jnp.max(
            jnp.sum(squares[rows], axis=0, keepdims=True), axis=1, keepdims=True
        )
        bound = jnp.maximum(bound, longest * norm_ref[0:1, head : head + 1])
    small = bound[0, 0] * 1.02 < SAFE_SCORE**2

    def run(shifted):
        lag = slices if shifted else min(2, slices)
        steps = PACK * slices
        highest = {}
        own_query = partial_highest = mixed = None
        for now in range(steps + lag):
            if now < steps:
                head, at = divmod(now, slices)
                part = slice(at * slice_rows, (at + 1) * slice_rows)
                if at == 0:
                    own_query = jnp.where(head_row == head, query, jnp.zeros_like(query))
                    partial_highest = jnp.full((8, block), -jnp.inf, jnp.float32)
                scores = plain_dot(key_ref[part, :], own_query)
                scores_ref[now % (lag + 1)] = scores
                if shifted:
                    partial_highest = jnp.maximum(
                        partial_highest, jnp.max(scores.reshape(slice_rows // 8, 8, block), axis=0)
                    )
                    if at == slices - 1:
                        highest[head] = jnp.max(partial_highest, axis=0, keepdims=True)
            if now >= lag:
                head, at = divmod(now - lag, slices)
                rows = slice(head * HEAD_DIM, (head + 1) * HEAD_DIM)
                part = slice(at * slice_rows, (at + 1) * slice_rows)
                scores = scores_ref[(now - lag) % (lag + 1)]
                if shifted:
                    scores = scores - highest[head]
                raised = jnp.exp2(scores).astype(jnp.bfloat16)
                raised_ref[head, part, :] = raised
                term = plain_dot(jnp.concatenate([value_ref[rows, part], ones], axis=0), raised)
                mixed = term if at == 0 else mixed + term
                if at == slices - 1:
                    total = mixed[HEAD_DIM : HEAD_DIM + 1]
                    total_ref[0, head : head + 1, :] = total
                    mean = mixed[:HEAD_DIM] / total
                    exact_ref[rows, :] = mean
                    mixed_ref[rows, :] = mean.astype(jnp.bfloat16)

    @pl.when(small)
    def _():
        run(False)

    @pl.when(jnp.logical_not(small))
    def _():
        run(True)


def attend(keys, query_t, value_t):
    width, rows = query_t.shape
    span = keys.shape[0]
    block = min(512, rows)
    groups = width // 128
    lane_block = pl.BlockSpec((128, block), lambda g, i: (g, i))
    return pl.pallas_call(
        attend_kernel,
        grid=(groups, rows // block),
        in_specs=[
            pl.BlockSpec((span, 128), lambda g, i: (0, g)),
            lane_block,
            pl.BlockSpec((128, span), lambda g, i: (g, 0)),
        ],
        out_specs=[
            lane_block,
            lane_block,
            pl.BlockSpec((1, 8, block), lambda g, i: (g, 0, i)),
            pl.BlockSpec((PACK, span, block), lambda g, i: (g, 0, i)),
        ],
        out_shape=[
            jax.ShapeDtypeStruct((width, rows), jnp.bfloat16),
            jax.ShapeDtypeStruct((width, rows), jnp.float32),
            jax.ShapeDtypeStruct((groups, 8, rows), jnp.float32),
            jax.ShapeDtypeStruct((HEADS, span, rows), jnp.bfloat16),
        ],
        scratch_shapes=[
            pltpu.VMEM((span // min(256, span) + 1, min(256, span), block), jnp.float32),
            pltpu.VMEM((8, 128), jnp.float32),
        ],
        compiler_params=pltpu.CompilerParams(vmem_limit_bytes=VMEM_LIMIT),
        cost_estimate=pl.CostEstimate(
            flops=HEADS * span * rows * 512,
            bytes_accessed=2 * HEADS * span * rows,
            transcendentals=HEADS * span * rows,
        ),
        name="attend",
    )(keys, query_t, value_t)


def middle_kernel(
    stream_ref,
    mixed_ref,
    cotangent_ref,
    output_ref,
    expand_ref,
    contract_ref,
    vector_ref,
    decoded_ref,
    grad_middle_ref,
    grad_attended_ref,
    flat_ref,
    small_ref,
    expand_sum,
    contract_sum,
    output_sum,
    small_sum,
):
    width = stream_ref.shape[1]
    chunks = expand_ref.shape[1] // width

    def vector(row):
        return vector_ref[row : row + 1, :]

    @pl.when(pl.program_id(0) == 0)
    def _():
        expand_sum[...] = jnp.zeros_like(expand_sum)
        contract_sum[...] = jnp.zeros_like(contract_sum)
        output_sum[...] = jnp.zeros_like(output_sum)
        small_sum[...] = jnp.zeros_like(small_sum)

    mixed_t = mixed_ref[...]
    cotangent = cotangent_ref[...]
    middle = (
        stream_ref[...]
        + plain_dot(turned(mixed_t), output_ref[...])
        + vector(OUTPUT_BIAS)
    )
    normed, scale = normalize(middle)
    gain = vector(SECOND_GAIN)
    low = (normed * gain + vector(SECOND_SHIFT)).astype(jnp.bfloat16)
    low_t = turned(low)
    output = middle + vector(CONTRACT_BIAS)
    grad_normed = jnp.zeros_like(middle)
    for chunk in range(chunks):
        part = slice(chunk * width, (chunk + 1) * width)
        hidden = plain_dot(low, expand_ref[:, part]) + vector(EXPAND_BIAS + chunk)
        below = 0.5 + 0.5 * lax.erf(hidden * math.sqrt(0.5))
        slope = below + hidden * jnp.exp(-0.5 * hidden * hidden) * (1.0 / math.sqrt(2 * math.pi))
        active = (hidden * below).astype(jnp.bfloat16)
        grad_hidden = (trail_dot(cotangent, contract_ref[part, :]) * slope).astype(jnp.bfloat16)
        output = output + plain_dot(active, contract_ref[part, :])
        grad_normed = grad_normed + trail_dot(grad_hidden, expand_ref[:, part])
        contract_sum[part, :] += plain_dot(turned(active), cotangent)
        expand_sum[part, :] += plain_dot(low_t, grad_hidden)
        small_sum[chunk : chunk + 1, :] += column_sum(grad_hidden)
    decoded_ref[...] = output.astype(jnp.bfloat16)
    grad_middle = cotangent.astype(jnp.float32) + normalize_back(grad_normed * gain, normed, scale)
    grad_middle_ref[...] = grad_middle
    branch = grad_middle.astype(jnp.bfloat16)
    grad_attended_ref[...] = trail_dot(output_ref[...], branch).astype(jnp.bfloat16)
    output_sum[...] += plain_dot(mixed_t, branch)
    small_sum[chunks : chunks + 1, :] += column_sum(cotangent)
    small_sum[chunks + 1 : chunks + 2, :] += column_sum(branch)
    small_sum[chunks + 2 : chunks + 3, :] += column_sum(grad_normed * normed)
    small_sum[chunks + 3 : chunks + 4, :] += column_sum(grad_normed)

    @pl.when(pl.program_id(0) == pl.num_programs(0) - 1)
    def _():
        at = 0
        for total in (expand_sum, contract_sum, output_sum):
            flat_ref[at : at + total.shape[0], :] = total[...].astype(flat_ref.dtype)
            at += total.shape[0]
        if at < flat_ref.shape[0]:
            flat_ref[at:, :] = jnp.zeros((flat_ref.shape[0] - at, width), flat_ref.dtype)
        small_ref[...] = small_sum[...]


def middle_block(
    stream,
    mixed_t,
    cotangent,
    output_weight,
    expand_weight,
    contract_weight,
    vectors,
    flat_rows,
):
    rows, width = stream.shape
    hidden = expand_weight.shape[1]
    block = min(256, rows)
    row_block = pl.BlockSpec((block, width), lambda i: (i, 0))
    lane_block = pl.BlockSpec((width, block), lambda i: (0, i))
    small_rows = hidden // width + 4
    return pl.pallas_call(
        middle_kernel,
        grid=(rows // block,),
        in_specs=[
            row_block,
            lane_block,
            row_block,
            whole((width, width)),
            whole((width, hidden)),
            whole((hidden, width)),
            whole(vectors.shape),
        ],
        out_specs=[
            row_block,
            row_block,
            lane_block,
            whole((flat_rows, width)),
            whole((small_rows, width)),
        ],
        out_shape=[
            jax.ShapeDtypeStruct((rows, width), jnp.bfloat16),
            jax.ShapeDtypeStruct((rows, width), jnp.float32),
            jax.ShapeDtypeStruct((width, rows), jnp.bfloat16),
            jax.ShapeDtypeStruct((flat_rows, width), jnp.bfloat16),
            jax.ShapeDtypeStruct((small_rows, width), jnp.float32),
        ],
        scratch_shapes=[
            pltpu.VMEM((hidden, width), jnp.float32),
            pltpu.VMEM((hidden, width), jnp.float32),
            pltpu.VMEM((width, width), jnp.float32),
            pltpu.VMEM((small_rows, width), jnp.float32),
        ],
        compiler_params=pltpu.CompilerParams(vmem_limit_bytes=VMEM_LIMIT),
        cost_estimate=pl.CostEstimate(
            flops=2 * rows * width * (6 * hidden + 3 * width),
            bytes_accessed=16 * rows * width,
            transcendentals=2 * rows * hidden,
        ),
        name="middle",
    )(
        stream,
        mixed_t,
        cotangent,
        output_weight,
        expand_weight,
        contract_weight,
        vectors,
    )


def attend_back_kernel(
    steps,
    raised_ref,
    total_ref,
    value_ref,
    key_ref,
    query_ref,
    exact_ref,
    grad_ref,
    flat_ref,
    rows_ref,
    latents_ref,
    grad_query_ref,
    grad_key_ref,
    grad_value_ref,
    summed_ref,
    decoded_ref,
    gathered_ref,
    key_sum,
    value_sum,
    exchange_sems,
    exchange_local,
    gather_sems,
    gather_local,
    *sum_refs,
):
    spot = Spot()
    tree = TreeSum(spot, flat_ref, summed_ref, sum_refs, True)
    clips, share = decoded_ref.shape[0], decoded_ref.shape[1]
    mine, part = spot.index % clips, spot.index // clips

    def member(step):
        return (mine + step) % clips

    def exchange(step):
        return send(
            rows_ref.at[span_of(member(step) * share, share)],
            decoded_ref.at[mine],
            exchange_sems,
            step,
            (spot.layer, part * clips + member(step)),
        )

    def own_rows():
        return pltpu.make_async_copy(
            rows_ref.at[span_of(mine * share, share)], decoded_ref.at[mine], exchange_local
        )

    capacity = latents_ref.shape[0]

    def held(core, chip):
        return gathered_ref.at[span_of((chip * 2 + core) * capacity, capacity)]

    def share_own(at, device):
        return send(latents_ref, held(spot.core, spot.chip), gather_sems, at, device)

    def pass_on(at, core, step):
        place = held(core, spot.chip_at(-step))
        return send(place, place, gather_sems, at, spot.sibling())

    def keep_own():
        return pltpu.make_async_copy(latents_ref, held(spot.core, spot.chip), gather_local)

    step_now = pl.program_id(0) * pl.num_programs(1) + pl.program_id(1)

    def at_step(fraction):
        return pl.when(step_now == fraction * steps // 32)

    @at_step(0)
    def _():
        others = spot.tree() + [
            (spot.layer, part * clips + member(step)) for step in range(1, clips)
        ]
        count = spot.meet(others)
        pl.semaphore_wait(pltpu.get_barrier_semaphore(), count)
        tree.start()

    @at_step(2)
    def _():
        tree.near_to_far()

    @at_step(8)
    def _():
        tree.far_to_deep()
        own_rows().start()
        for step in range(1, clips):
            exchange(step).start()
        keep_own().start()
        for step in range(1, spot.half):
            share_own(step, spot.peer(step)).start()
        share_own(0, spot.sibling()).start()

    @at_step(12)
    def _():
        tree.deep_to_layer()

    @at_step(16)
    def _():
        tree.layer_to_part()

    @at_step(21)
    def _():
        for step in range(1, spot.half):
            pass_on(step, spot.core, step).wait_recv()
            pass_on(spot.half + step, spot.core, step).start()

    @at_step(26)
    def _():
        tree.part_to_half()

    @at_step(31)
    def _():
        tree.finish()
        own_rows().wait()
        for step in range(1, clips):
            exchange(step).wait_send()
        for step in range(1, clips):
            send(
                rows_ref.at[span_of(mine * share, share)],
                decoded_ref.at[member(-step)],
                exchange_sems,
                step,
                (spot.layer, part * clips + member(step)),
            ).wait_recv()
        keep_own().wait()
        for step in range(1, spot.half):
            share_own(step, spot.peer(step)).wait_send()
        share_own(0, spot.sibling()).wait_send()
        pass_on(0, 1 - spot.core, 0).wait_recv()
        for step in range(1, spot.half):
            pass_on(spot.half + step, spot.core, step).wait_send()
            pass_on(spot.half + step, 1 - spot.core, step).wait_recv()

    @pl.when(pl.program_id(1) == 0)
    def _():
        key_sum[...] = jnp.zeros_like(key_sum)
        value_sum[...] = jnp.zeros_like(value_sum)

    block = query_ref.shape[1]
    head_row = lax.broadcasted_iota(jnp.int32, (128, block), 0) // HEAD_DIM
    head_col = lax.broadcasted_iota(jnp.int32, (block, 128), 1) // HEAD_DIM
    inverse = 1.0 / total_ref[0, 0:PACK]
    inverse = jnp.concatenate(
        [jnp.broadcast_to(inverse[h : h + 1], (HEAD_DIM, block)) for h in range(PACK)], axis=0
    )
    grad_low = (grad_ref[...].astype(jnp.float32) * inverse).astype(jnp.bfloat16)
    grad = grad_low.astype(jnp.float32)
    inner = grad * exact_ref[...]
    grad_turned = grad.T.astype(jnp.bfloat16)
    query_turned = turned(query_ref[...])
    span = value_ref.shape[0]
    slice_rows = min(256, span)
    units = [(head, at) for head in range(PACK) for at in range(0, span, slice_rows)]
    lag = 2
    weights = {}
    grad_query = None
    for now in range(len(units) + lag):
        if now < len(units):
            head, at = units[now]
            own_grad = jnp.where(head_row == head, grad_low, jnp.zeros_like(grad_low))
            weights[now] = plain_dot(value_ref[at : at + slice_rows, :], own_grad)
        if now >= lag:
            head, at = units[now - lag]
            rows = slice(head * HEAD_DIM, (head + 1) * HEAD_DIM)
            part = slice(at, at + slice_rows)
            row_inner = jnp.sum(inner[rows], axis=0, keepdims=True)
            raised = raised_ref[head, part, :]
            grad_scores = raised * (weights.pop(now - lag) - row_inner).astype(jnp.bfloat16)
            value_sum[part, :] += plain_dot(
                raised, jnp.where(head_col == head, grad_turned, jnp.zeros_like(grad_turned))
            )
            key_sum[part, :] += plain_dot(
                grad_scores, jnp.where(head_col == head, query_turned, jnp.zeros_like(query_turned))
            )
            term = plain_dot(key_ref[rows, part], grad_scores)
            grad_query = term if at == 0 else grad_query + term
            if at + slice_rows == span:
                grad_query_ref[rows, :] = (grad_query * HEAD_DIM ** (-0.5)).astype(jnp.bfloat16)

    @pl.when(pl.program_id(1) == pl.num_programs(1) - 1)
    def _():
        grad_key_ref[...] = (key_sum[...] * (1.0 / LOG2E)).astype(jnp.bfloat16)
        grad_value_ref[...] = value_sum[...].astype(jnp.bfloat16)


def attend_back(raised, total, values, key_t, query_t, exact_t, grad_t, flat, decoded_rows, latents):
    splits, layers = lax.axis_size("seq"), lax.axis_size("dp")
    clips, share, _ = decoded_rows.shape
    width, rows = query_t.shape
    span = values.shape[0]
    block = min(256, rows)
    groups = width // 128
    lane_block = pl.BlockSpec((128, block), lambda g, i: (g, i))
    return pl.pallas_call(
        partial(attend_back_kernel, groups * (rows // block)),
        grid=(groups, rows // block),
        in_specs=[
            pl.BlockSpec((PACK, span, block), lambda g, i: (g, 0, i)),
            pl.BlockSpec((1, 8, block), lambda g, i: (g, 0, i)),
            pl.BlockSpec((span, 128), lambda g, i: (0, g)),
            pl.BlockSpec((128, span), lambda g, i: (g, 0)),
            lane_block,
            lane_block,
            lane_block,
            pl.BlockSpec(memory_space=pl.ANY),
            pl.BlockSpec(memory_space=pl.ANY),
            pl.BlockSpec(memory_space=pl.ANY),
        ],
        out_specs=[
            lane_block,
            pl.BlockSpec((span, 128), lambda g, i: (0, g)),
            pl.BlockSpec((span, 128), lambda g, i: (0, g)),
            pl.BlockSpec(memory_space=pl.ANY),
            pl.BlockSpec(memory_space=pl.ANY),
            pl.BlockSpec(memory_space=pl.ANY),
        ],
        out_shape=[
            jax.ShapeDtypeStruct((width, rows), jnp.bfloat16),
            jax.ShapeDtypeStruct((span, width), jnp.bfloat16),
            jax.ShapeDtypeStruct((span, width), jnp.bfloat16),
            jax.ShapeDtypeStruct(flat.shape, flat.dtype),
            jax.ShapeDtypeStruct(decoded_rows.shape, decoded_rows.dtype),
            jax.ShapeDtypeStruct((splits * latents.shape[0], latents.shape[1]), latents.dtype),
        ],
        scratch_shapes=[
            pltpu.VMEM((span, 128), jnp.float32),
            pltpu.VMEM((span, 128), jnp.float32),
            pltpu.SemaphoreType.DMA((2, clips)),
            pltpu.SemaphoreType.DMA,
            pltpu.SemaphoreType.DMA((2, splits)),
            pltpu.SemaphoreType.DMA,
        ]
        + TreeSum.scratch(flat.shape[0], flat.shape[1], True, splits, layers),
        compiler_params=pltpu.CompilerParams(
            vmem_limit_bytes=VMEM_LIMIT, collective_id=1, has_side_effects=True
        ),
        cost_estimate=pl.CostEstimate(
            flops=HEADS * span * rows * 1024,
            bytes_accessed=2 * HEADS * span * rows,
            transcendentals=0,
        ),
        name="attend_back",
    )(raised, total, values, key_t, query_t, exact_t, grad_t, flat, decoded_rows.reshape(clips * share, width), latents)


def leave_kernel(
    grad_query_ref,
    grad_key_ref,
    grad_value_ref,
    stream_ref,
    empty_ref,
    low_ref,
    grad_middle_ref,
    vector_ref,
    joint_ref,
    slot_ref,
    latents_ref,
    embed_ref,
    early_ref,
    latent_grad_ref,
    joint_total_ref,
    embed_total_ref,
    joint_sum,
    small_sum,
    grad_all,
    joint_flat,
    embed_flat,
    back_all,
    near_in,
    far_out,
    far_in,
    sems,
    *sum_refs,
):
    block, width = stream_ref.shape
    step_now = pl.program_id(0)
    spot = Spot()
    capacity = back_all.shape[0] // spot.splits
    others = spot.tree()

    @pl.when(step_now == 0)
    def _():
        spot.meet(others)
        joint_sum[...] = jnp.zeros_like(joint_sum)
        small_sum[...] = jnp.zeros_like(small_sum)

    normed, scale = normalize(stream_ref[...])
    low_t = turned(low_ref[...])
    sides = [turned(grad_query_ref[...]), grad_key_ref[...], grad_value_ref[...]]
    grad_normed = jnp.zeros_like(normed)
    for at, side in enumerate(sides):
        grad_normed = grad_normed + trail_dot(side, joint_ref[:, at * width : (at + 1) * width])
        joint_sum[at * width : (at + 1) * width, :] += plain_dot(low_t, side)
    grad_stream = grad_middle_ref[...] + normalize_back(
        grad_normed * vector_ref[FIRST_GAIN : FIRST_GAIN + 1, :], normed, scale
    )
    grad_all[pl.ds(pl.multiple_of(step_now * block, block), block), :] = grad_stream.astype(
        jnp.bfloat16
    )
    small_sum[0:1, :] += column_sum(empty_ref[...] * grad_stream)
    small_sum[1:2, :] += column_sum(grad_normed * normed)
    small_sum[2:3, :] += column_sum(grad_normed)
    small_sum[3:4, :] += column_sum(sides[0])
    small_sum[4:5, :] += column_sum(sides[2])

    @pl.when(step_now == pl.num_programs(0) - 1)
    def _():
        count = len(sum_refs) // 2
        joint_tree = TreeSum(spot, joint_flat, joint_total_ref, sum_refs[:count], False)
        embed_tree = TreeSum(spot, embed_flat, embed_total_ref, sum_refs[count:], False)
        joint_flat[...] = joint_sum[...].astype(jnp.bfloat16)
        pl.semaphore_wait(pltpu.get_barrier_semaphore(), len(others))
        joint_tree.start()
        place = lax.broadcasted_iota(jnp.int32, (1, grad_all.shape[0]), 1)

        def gathered(owner):
            slots = slot_ref[pl.ds(owner, 1), :].astype(jnp.float32)
            slots = jnp.broadcast_to(slots, (8, slots.shape[1])).T[:capacity, 0:1]
            takes = (slots.astype(jnp.int32) == place).astype(jnp.float32).astype(jnp.bfloat16)
            return plain_dot(takes, grad_all[...])

        def rows_of(owner):
            return span_of(owner * capacity, capacity)

        def part(at):
            return pl.ds(at * capacity, capacity)

        def near_copy(step):
            owner = spot.chip_at(step) * 2 + 1 - spot.core
            return send(
                back_all.at[rows_of(owner)], near_in.at[part(step)], sems, step, spot.sibling()
            )

        def far_copy(step):
            return send(
                far_out.at[part(step - 1)],
                far_in.at[part(step - 1)],
                sems,
                spot.half + step,
                spot.peer(step),
            )

        order = list(range(1, spot.half)) + [0]
        for step in order:
            owner = spot.chip_at(step) * 2 + 1 - spot.core
            back_all[rows_of(owner), :] = gathered(owner).astype(jnp.bfloat16)
            near_copy(step).start()
        joint_tree.near_to_far()
        for step in order:
            owner = spot.chip_at(step) * 2 + spot.core
            own = gathered(owner)
            back_all[rows_of(owner), :] = own.astype(jnp.bfloat16)
            near_copy(step).wait()
            own = own + near_in[part(step), :].astype(jnp.float32)
            if step > 0:
                far_out[part(step - 1), :] = own.astype(jnp.bfloat16)
                far_copy(step).start()
        embed_rows = embed_ref.shape[0]
        embed_flat[:embed_rows, :] = lead_dot(latents_ref[...], back_all[...]).astype(jnp.bfloat16)
        small_sum[5:6, :] = column_sum(back_all[...])
        small = jnp.concatenate([early_ref[...], small_sum[...]], axis=0)
        rest = embed_flat.shape[0] - embed_rows - small.shape[0]
        if rest:
            small = jnp.concatenate([small, jnp.zeros((rest, width), jnp.float32)], axis=0)
        embed_flat[embed_rows:, :] = small.astype(jnp.bfloat16)
        embed_tree.start()
        joint_tree.far_to_deep()
        embed_tree.near_to_far()
        for step in range(1, spot.half):
            far_copy(step).wait()
            own = own + far_in[part(step - 1), :].astype(jnp.float32)
        grad_embedded = own[: latent_grad_ref.shape[0]].astype(jnp.bfloat16)
        latent_grad_ref[...] = trail_dot(grad_embedded, embed_ref[...]).astype(jnp.bfloat16)
        joint_tree.deep_to_layer()
        embed_tree.far_to_deep()
        joint_tree.part_to_half()
        embed_tree.deep_to_layer()
        joint_tree.finish()
        embed_tree.part_to_half()
        embed_tree.finish()


def leave(
    grad_query_t,
    grad_key,
    grad_value,
    stream,
    empty,
    low,
    grad_middle,
    vectors,
    joint_weight,
    slot_place,
    latents_all,
    embed_weight,
    early_small,
    own_rows,
):
    splits, layers = lax.axis_size("seq"), lax.axis_size("dp")
    rows, width = stream.shape
    slots = latents_all.shape[0]
    latent_shape = (own_rows, latents_all.shape[1])
    capacity = slots // splits
    half = splits // 2
    block = min(256, rows)
    row_block = pl.BlockSpec((block, width), lambda i: (i, 0))
    lane_block = pl.BlockSpec((width, block), lambda i: (0, i))
    joint_rows = padded(3 * width, splits * 16)
    embed_rows = padded(embed_weight.shape[0] + early_small.shape[0] + 8, splits * 16)
    return pl.pallas_call(
        leave_kernel,
        grid=(rows // block,),
        in_specs=[
            lane_block,
            row_block,
            row_block,
            row_block,
            pl.BlockSpec((block, 1), lambda i: (i, 0)),
            row_block,
            row_block,
            whole(vectors.shape),
            whole((width, 3 * width)),
            whole(slot_place.shape),
            pl.BlockSpec(latents_all.shape, lambda i: (0, 0), pipeline_mode=pl.Buffered(1)),
            whole(embed_weight.shape),
            whole(early_small.shape),
        ],
        out_specs=[
            whole(latent_shape),
            pl.BlockSpec(memory_space=pl.ANY),
            pl.BlockSpec(memory_space=pl.ANY),
        ],
        out_shape=[
            jax.ShapeDtypeStruct(latent_shape, jnp.bfloat16),
            jax.ShapeDtypeStruct((joint_rows, width), jnp.bfloat16),
            jax.ShapeDtypeStruct((embed_rows, width), jnp.bfloat16),
        ],
        scratch_shapes=[
            pltpu.VMEM((3 * width, width), jnp.float32),
            pltpu.VMEM((8, width), jnp.float32),
            pltpu.VMEM((rows, width), jnp.bfloat16),
            pltpu.VMEM((joint_rows, width), jnp.bfloat16),
            pltpu.VMEM((embed_rows, width), jnp.bfloat16),
            pltpu.VMEM((slots, width), jnp.bfloat16),
            pltpu.VMEM((half * capacity, width), jnp.bfloat16),
            pltpu.VMEM((max(half - 1, 1) * capacity, width), jnp.bfloat16),
            pltpu.VMEM((max(half - 1, 1) * capacity, width), jnp.bfloat16),
            pltpu.SemaphoreType.DMA((2, splits)),
        ]
        + TreeSum.scratch(joint_rows, width, False, splits, layers)
        + TreeSum.scratch(embed_rows, width, False, splits, layers),
        compiler_params=pltpu.CompilerParams(
            vmem_limit_bytes=VMEM_LIMIT, collective_id=2, has_side_effects=True
        ),
        cost_estimate=pl.CostEstimate(
            flops=2 * rows * width * (slots + 6 * width),
            bytes_accessed=20 * rows * width,
            transcendentals=0,
        ),
        name="leave",
    )(
        grad_query_t,
        grad_key,
        grad_value,
        stream,
        empty,
        low,
        grad_middle,
        vectors,
        joint_weight,
        slot_place,
        latents_all,
        embed_weight,
        early_small,
    )


def finish_kernel(
    expand_ref,
    contract_ref,
    output_ref,
    joint_ref,
    embed_ref,
    small_ref,
    expand_out,
    contract_out,
    output_out,
    joint_out,
    embed_out,
    *small_outs,
):
    for source, target in (
        (expand_ref, expand_out),
        (contract_ref, contract_out),
        (output_ref, output_out),
        (joint_ref, joint_out),
        (embed_ref, embed_out),
    ):
        target[...] = source[...].astype(jnp.float32)
    small = small_ref[...].astype(jnp.float32)
    width = small.shape[1]
    at = 0
    for target in small_outs:
        for start in range(0, target.shape[0], width):
            target[start : start + width] = small[at]
            at += 1


def finish(early_sum, joint_sum, embed_sum, hidden, embed_rows, small_sizes):
    width = early_sum.shape[1]
    chunks = hidden // width
    square = (width, width)
    embed_block = (embed_rows // chunks, width)
    sides = joint_sum.shape[0] // width
    return pl.pallas_call(
        finish_kernel,
        grid=(chunks,),
        in_specs=[
            pl.BlockSpec(square, lambda i: (i, 0)),
            pl.BlockSpec(square, lambda i: (chunks + i, 0)),
            pl.BlockSpec(square, lambda i: (2 * chunks, 0)),
            pl.BlockSpec(square, lambda i: (jnp.minimum(i, sides - 1), 0)),
            pl.BlockSpec(embed_block, lambda i: (i, 0)),
            pl.BlockSpec((16, width), lambda i: (embed_rows // 16, 0)),
        ],
        out_specs=[
            pl.BlockSpec(square, lambda i: (0, i)),
            pl.BlockSpec(square, lambda i: (i, 0)),
            pl.BlockSpec(square, lambda i: (0, 0)),
            pl.BlockSpec(square, lambda i: (0, jnp.minimum(i, sides - 1))),
            pl.BlockSpec(embed_block, lambda i: (i, 0)),
        ]
        + [whole((size,)) for size in small_sizes],
        out_shape=[
            jax.ShapeDtypeStruct((width, hidden), jnp.float32),
            jax.ShapeDtypeStruct((hidden, width), jnp.float32),
            jax.ShapeDtypeStruct(square, jnp.float32),
            jax.ShapeDtypeStruct((width, sides * width), jnp.float32),
            jax.ShapeDtypeStruct((embed_rows, width), jnp.float32),
        ]
        + [jax.ShapeDtypeStruct((size,), jnp.float32) for size in small_sizes],
        compiler_params=pltpu.CompilerParams(vmem_limit_bytes=VMEM_LIMIT),
        cost_estimate=pl.CostEstimate(
            flops=0, bytes_accessed=12 * width * (hidden + width), transcendentals=0
        ),
        name="finish",
    )(early_sum, early_sum, early_sum, joint_sum, embed_sum, embed_sum)


def body(
    latents,
    clip_ids,
    restore,
    counts,
    embed_weight,
    embed_bias,
    mask_token,
    first_gain,
    first_shift,
    joint_weight,
    query_bias,
    value_bias,
    output_weight,
    output_bias,
    second_gain,
    second_shift,
    expand_weight,
    expand_bias,
    contract_weight,
    contract_bias,
    cotangent,
):
    splits = lax.axis_size("seq")
    seq_index = lax.axis_index("seq")
    capacity = latents.shape[0]
    clip_count, clip_share, model_width = cotangent.shape
    sharers = splits // clip_count
    rows = clip_count * clip_share
    own_clip = seq_index % clip_count
    first_place = (seq_index // clip_count) * rows
    exchange_groups = [[s * clip_count + c for c in range(clip_count)] for s in range(sharers)]
    clip_groups = [[s * clip_count + c for s in range(sharers)] for c in range(clip_count)]

    def to_clips(blocks):
        return lax.all_to_all(
            blocks,
            "seq",
            split_axis=0,
            concat_axis=0,
            tiled=True,
            axis_index_groups=exchange_groups if sharers > 1 else None,
        )

    live = jnp.arange(capacity, dtype=jnp.int32)[None, :] < counts[:, None]
    mine = live & ((clip_ids % clip_count).reshape(splits, capacity) == own_clip)
    slot_place = jnp.where(mine, restore.reshape(splits, capacity) - first_place, -1)
    slot_place = jnp.pad(
        slot_place, ((0, 0), (0, padded(capacity, 128) - capacity)), constant_values=-1
    )
    (
        stream,
        empty,
        first_low,
        query_t,
        keys,
        key_t,
        values,
        value_t,
        vectors,
        latents,
    ) = enter(
        latents,
        embed_weight,
        slot_place,
        first_place,
        rows,
        [
            embed_bias,
            mask_token,
            first_gain,
            first_shift,
            query_bias,
            value_bias,
            output_bias,
            second_gain,
            second_shift,
            contract_bias,
            expand_bias,
        ],
        joint_weight,
    )
    cotangent, keys = lax.optimization_barrier((cotangent, keys))
    grad_output = to_clips(cotangent).reshape(rows, model_width)
    if sharers > 1:
        keys = lax.all_gather(keys, "seq", axis=0, tiled=True, axis_index_groups=clip_groups)
        values = lax.all_gather(values, "seq", axis=0, tiled=True, axis_index_groups=clip_groups)
        key_t, value_t = keys.T, values.T
    mixed_t, exact_t, total, raised = attend(keys, query_t, value_t)
    (
        decoded_rows,
        grad_middle,
        grad_attended_t,
        early_flat,
        early_small,
    ) = middle_block(
        stream,
        mixed_t,
        grad_output,
        output_weight,
        expand_weight,
        contract_weight,
        vectors,
        padded(2 * expand_weight.shape[1] + model_width, splits * lax.axis_size("dp") * 16),
    )
    grad_query_t, grad_key, grad_value, early_sum, decoded, latents_all = attend_back(
        raised,
        total,
        values,
        key_t,
        query_t,
        exact_t,
        grad_attended_t,
        early_flat,
        decoded_rows.reshape(clip_count, clip_share, model_width),
        latents,
    )
    if sharers > 1:
        grad_key, grad_value = (
            lax.psum_scatter(
                side, "seq", scatter_dimension=0, tiled=True, axis_index_groups=clip_groups
            )
            for side in (grad_key, grad_value)
        )
    latent_grad, joint_sum, embed_sum = leave(
        grad_query_t,
        grad_key,
        grad_value,
        stream,
        empty,
        first_low,
        grad_middle,
        vectors,
        joint_weight,
        slot_place,
        latents_all,
        embed_weight,
        early_small,
        capacity,
    )
    hidden_width = expand_weight.shape[1]
    (
        grad_expand,
        grad_contract,
        grad_output_weight,
        grad_joint_weight,
        grad_embed_weight,
        grad_expand_bias,
        grad_contract_bias,
        grad_output_bias,
        grad_second_gain,
        grad_second_shift,
        grad_mask,
        grad_first_gain,
        grad_first_shift,
        grad_query_bias,
        grad_value_bias,
        grad_embed_bias,
    ) = finish(
        early_sum,
        joint_sum,
        embed_sum,
        hidden_width,
        embed_weight.shape[0],
        [hidden_width] + [model_width] * 10,
    )
    return (
        decoded,
        latent_grad,
        grad_embed_weight,
        grad_embed_bias,
        grad_mask,
        grad_first_gain,
        grad_first_shift,
        grad_joint_weight,
        grad_query_bias,
        grad_value_bias,
        grad_output_weight,
        grad_output_bias,
        grad_second_gain,
        grad_second_shift,
        grad_expand,
        grad_expand_bias,
        grad_contract,
        grad_contract_bias,
    )


def solution(mesh):
    placed = (
        (P(("dp", "seq"), None),) + (P("dp"),) * 3 + (P(),) * 16 + (P("dp", "seq", None),)
    )
    return jax.shard_map(
        body,
        mesh=mesh,
        in_specs=placed,
        out_specs=(P("dp", "seq", None), P(("dp", "seq"), None)) + (P(),) * 16,
        check_vma=False,
    )
```

```python
from functools import partial
import math

import jax
import jax.numpy as jnp
from jax import lax
from jax.experimental import pallas as pl
from jax.experimental.pallas import tpu as pltpu
from jax.sharding import PartitionSpec as P

HEADS = 16
HEAD_DIM = 32
PACK = 128 // HEAD_DIM
VMEM_LIMIT = 56 * 1024 * 1024
SAFE_SCORE = 80.0
MESH = pl.DeviceIdType.MESH
LOG2E = math.log2(math.e)
QUERY_SCALE = LOG2E * HEAD_DIM ** (-0.5)


epsilon = 1e-06


EMBED_BIAS, MASK, FIRST_GAIN, FIRST_SHIFT, QUERY_BIAS, VALUE_BIAS = range(6)
OUTPUT_BIAS, SECOND_GAIN, SECOND_SHIFT, CONTRACT_BIAS, EXPAND_BIAS = range(6, 11)


def whole(shape):
    return pl.BlockSpec(shape, lambda *_: (0,) * len(shape))


def turned(values):
    return values.astype(jnp.float32).T.astype(values.dtype)


def sinusoid(places, table_width):
    half_width = table_width // 2
    frequency = jnp.exp(-math.log(10000.0) * jnp.arange(half_width, dtype=jnp.float32) / half_width)
    angles = places.astype(jnp.float32)[:, None] * frequency[None, :]
    return jnp.concatenate([jnp.sin(angles), jnp.cos(angles)], axis=1)


def plain_dot(left, right):
    return jnp.dot(left, right, preferred_element_type=jnp.float32)


def lead_dot(left, right):
    return lax.dot_general(
        left, right, (((0,), (0,)), ((), ())), preferred_element_type=jnp.float32
    )


def trail_dot(left, right):
    return lax.dot_general(
        left, right, (((1,), (1,)), ((), ())), preferred_element_type=jnp.float32
    )


def column_sum(values):
    return jnp.sum(values.astype(jnp.float32), axis=0, keepdims=True)


def row_mean(values):
    return jnp.mean(values, axis=-1, keepdims=True)


def normalize(values):
    center = values - row_mean(values)
    scale = lax.rsqrt(row_mean(center * center) + epsilon)
    return center * scale, scale


def normalize_back(grad, normed, scale):
    return scale * (grad - row_mean(grad) - normed * row_mean(grad * normed))


class Spot:
    def __init__(self):
        self.layers, self.splits = lax.axis_size("dp"), lax.axis_size("seq")
        self.half = self.splits // 2
        self.layer, self.index = lax.axis_index("dp"), lax.axis_index("seq")
        self.core, self.chip = self.index % 2, self.index // 2

    def sibling(self):
        return (self.layer, self.chip * 2 + (1 - self.core))

    def chip_at(self, step):
        return (self.chip + step) % self.half

    def layer_at(self, step):
        return (self.layer + step) % self.layers

    def peer(self, step):
        return (self.layer, self.chip_at(step) * 2 + self.core)

    def above(self, step):
        return (self.layer_at(step), self.index)

    def meet(self, others):
        barrier = pltpu.get_barrier_semaphore()
        for other in others:
            pl.semaphore_signal(barrier, inc=1, device_id=other, device_id_type=MESH)
        return len(others)

    def tree(self, layers=True):
        others = [self.sibling()] + [self.peer(step) for step in range(1, self.half)]
        if layers:
            others += [self.above(step) for step in range(1, self.layers)]
        return others


def padded(rows, unit):
    return -(-rows // unit) * unit


def span_of(start, size):
    return pl.ds(pl.multiple_of(start, 16), size)


def send(source, target, sems, at, device):
    return pltpu.make_async_remote_copy(
        src_ref=source,
        dst_ref=target,
        send_sem=sems.at[0, at],
        recv_sem=sems.at[1, at],
        device_id=device,
        device_id_type=MESH,
    )


class TreeSum:
    def __init__(self, spot, source, result, refs, scatter):
        (
            self.near,
            self.near_sum,
            self.far,
            self.far_sum,
            self.deep,
            self.done,
            self.sems,
            self.local,
        ) = refs
        self.spot, self.source, self.result, self.scatter = spot, source, result, scatter
        self.part = self.far_sum.shape[0]
        self.piece = self.done.shape[0]

    @staticmethod
    def scratch(rows, width, scatter, splits, layers):
        half = splits // 2
        part = rows // splits
        piece = part // layers if scatter else part
        low = jnp.bfloat16
        return [
            pltpu.VMEM((half * part, width), low),
            pltpu.VMEM((half * part, width), low),
            pltpu.VMEM((max(half - 1, 1) * part, width), low),
            pltpu.VMEM((part, width), low),
            pltpu.VMEM((layers * piece, width), low),
            pltpu.VMEM((piece, width), low),
            pltpu.SemaphoreType.DMA((2, 2 + 2 * half + 2 * layers)),
            pltpu.SemaphoreType.DMA((2,)),
        ]

    def near_copy(self):
        spot = self.spot
        rows = spot.half * self.part
        return send(
            self.source.at[span_of((1 - spot.core) * rows, rows)],
            self.near,
            self.sems,
            0,
            spot.sibling(),
        )

    def own_copy(self):
        rows = self.spot.half * self.part
        return pltpu.make_async_copy(
            self.source.at[span_of(self.spot.core * rows, rows)], self.near_sum, self.local.at[0]
        )

    def far_copy(self, step):
        return send(
            self.near_sum.at[span_of(self.spot.chip_at(step) * self.part, self.part)],
            self.far.at[span_of((step - 1) * self.part, self.part)],
            self.sems,
            1 + step,
            self.spot.peer(step),
        )

    def deep_copy(self, step):
        spot = self.spot
        if self.scatter:
            source = self.far_sum.at[span_of(spot.layer_at(step) * self.piece, self.piece)]
        else:
            source = self.far_sum
        return send(
            source,
            self.deep.at[span_of(spot.layer * self.piece, self.piece)],
            self.sems,
            1 + spot.half + step,
            spot.above(step),
        )

    def place(self, core, chip, layer=None):
        spot = self.spot
        start = (core * spot.half + chip) * self.part
        if layer is None:
            return span_of(start, self.part)
        return span_of(start + layer * self.piece, self.piece)

    def done_copy(self):
        spot = self.spot
        layer = spot.layer if self.scatter else None
        return pltpu.make_async_copy(
            self.done, self.result.at[self.place(spot.core, spot.chip, layer)], self.local.at[1]
        )

    def layer_copy(self, step, arriving):
        spot = self.spot
        layer = spot.layer_at(-step) if arriving else spot.layer
        return send(
            self.done,
            self.result.at[self.place(spot.core, spot.chip, layer)],
            self.sems,
            1 + spot.half + spot.layers + step,
            spot.above(step),
        )

    def part_copy(self, step, arriving):
        spot = self.spot
        place = self.place(spot.core, spot.chip_at(-step) if arriving else spot.chip)
        return send(
            self.result.at[place] if self.scatter else self.done,
            self.result.at[place],
            self.sems,
            1 + spot.half + 2 * spot.layers + step,
            spot.peer(step),
        )

    def half_copy(self, arriving):
        spot = self.spot
        rows = spot.half * self.part
        core = 1 - spot.core if arriving else spot.core
        place = span_of(core * rows, rows)
        return send(
            self.result.at[place], self.result.at[place], self.sems, 1, spot.sibling()
        )

    def start(self):
        self.own_copy().start()
        self.near_copy().start()

    def near_to_far(self):
        self.own_copy().wait()
        self.near_copy().wait()
        unit = self.part
        while unit > 160 and unit % 32 == 0:
            unit //= 2

        def add(at, _):
            rows = span_of(at * unit, unit)
            self.near_sum[rows, :] = (
                self.near_sum[rows, :].astype(jnp.float32) + self.near[rows, :].astype(jnp.float32)
            ).astype(jnp.bfloat16)
            return 0

        lax.fori_loop(0, self.spot.half * (self.part // unit), add, 0)
        for step in range(1, self.spot.half):
            self.far_copy(step).start()

    def far_to_deep(self):
        spot = self.spot
        for step in range(1, spot.half):
            self.far_copy(step).wait()
        unit = self.part
        while unit > 160 and unit % 32 == 0:
            unit //= 2

        def add(at, _):
            start = at * unit
            total = self.near_sum[span_of(spot.chip * self.part + start, unit), :].astype(
                jnp.float32
            )
            for step in range(1, spot.half):
                total = total + self.far[span_of((step - 1) * self.part + start, unit), :].astype(
                    jnp.float32
                )
            self.far_sum[span_of(start, unit), :] = total.astype(jnp.bfloat16)
            return 0

        lax.fori_loop(0, self.part // unit, add, 0)
        for step in range(1, spot.layers):
            self.deep_copy(step).start()
        own = self.far_sum[...]
        if self.scatter:
            own = self.far_sum[span_of(spot.layer * self.piece, self.piece), :]
        self.deep[span_of(spot.layer * self.piece, self.piece), :] = own

    def deep_to_layer(self):
        spot = self.spot
        for step in range(1, spot.layers):
            self.deep_copy(step).wait_send()
        for step in range(1, spot.layers):
            send(
                self.done,
                self.deep.at[span_of(spot.layer_at(-step) * self.piece, self.piece)],
                self.sems,
                1 + spot.half + step,
                spot.above(step),
            ).wait_recv()
        total = self.deep[: self.piece, :].astype(jnp.float32)
        for layer in range(1, spot.layers):
            total = total + self.deep[layer * self.piece : (layer + 1) * self.piece, :].astype(
                jnp.float32
            )
        self.done[...] = total.astype(jnp.bfloat16)
        self.done_copy().start()
        if self.scatter:
            for step in range(1, spot.layers):
                self.layer_copy(step, False).start()
        else:
            for step in range(1, spot.half):
                self.part_copy(step, False).start()

    def layer_to_part(self):
        spot = self.spot
        if not self.scatter:
            return
        self.done_copy().wait()
        for step in range(1, spot.layers):
            self.layer_copy(step, False).wait_send()
        for step in range(1, spot.layers):
            self.layer_copy(step, True).wait_recv()
        for step in range(1, spot.half):
            self.part_copy(step, False).start()

    def part_to_half(self):
        spot = self.spot
        if not self.scatter:
            self.done_copy().wait()
        for step in range(1, spot.half):
            self.part_copy(step, False).wait_send()
        for step in range(1, spot.half):
            self.part_copy(step, True).wait_recv()
        self.half_copy(False).start()

    def finish(self):
        self.half_copy(False).wait_send()
        self.half_copy(True).wait_recv()


def enter_kernel(
    latents_ref,
    embed_ref,
    slot_ref,
    coarse_ref,
    fine_ref,
    joint_ref,
    *refs,
):
    (
        stream_ref,
        empty_ref,
        normed_ref,
        query_t_ref,
        key_ref,
        key_t_ref,
        value_ref,
        value_t_ref,
        vector_ref,
        latents_out_ref,
        embedded_ref,
        slot_row,
        sems,
    ) = refs[-13:]
    vector_refs = refs[:-13]
    block, width = stream_ref.shape
    spot = Spot()
    capacity = embedded_ref.shape[0] // spot.splits

    def vector(row):
        return vector_ref[row : row + 1, :]

    @pl.when(pl.program_id(0) == 0)
    def _():
        count = spot.meet(spot.tree(False))
        at = 0
        for source in vector_refs:
            for start in range(0, source.shape[0], width):
                values = source[start : start + width].astype(jnp.float32)
                vector_ref[at : at + 1, :] = values.reshape(1, width)
                at += 1
        latents = latents_ref[...]
        rest = capacity - latents.shape[0]
        if rest:
            latents = jnp.concatenate(
                [latents.astype(jnp.float32), jnp.zeros((rest, latents.shape[1]), jnp.float32)],
                axis=0,
            ).astype(jnp.bfloat16)
        latents_out_ref[...] = latents
        embedded = plain_dot(latents, embed_ref[...]) + vector(EMBED_BIAS)

        def held(core, chip):
            return embedded_ref.at[span_of((chip * 2 + core) * capacity, capacity)]

        def share(at, core, chip, device):
            return send(held(core, chip), held(core, chip), sems, at, device)

        embedded_ref[span_of(spot.index * capacity, capacity), :] = embedded.astype(jnp.bfloat16)
        pl.semaphore_wait(pltpu.get_barrier_semaphore(), count)
        for step in range(1, spot.half):
            share(step, spot.core, spot.chip, spot.peer(step)).start()
        share(0, spot.core, spot.chip, spot.sibling()).start()
        for source in range(spot.splits):
            slot_row[:, source * capacity : (source + 1) * capacity] = slot_ref[
                source : source + 1, :capacity
            ]
        for step in range(1, spot.half):
            share(step, spot.core, spot.chip_at(-step), spot.peer(step)).wait_recv()
            share(spot.half + step, spot.core, spot.chip_at(-step), spot.sibling()).start()
        for step in range(1, spot.half):
            share(step, spot.core, spot.chip, spot.peer(step)).wait_send()
        share(0, spot.core, spot.chip, spot.sibling()).wait_send()
        share(0, 1 - spot.core, spot.chip, spot.sibling()).wait_recv()
        for step in range(1, spot.half):
            at = spot.half + step
            share(at, spot.core, spot.chip_at(-step), spot.sibling()).wait_send()
            share(at, 1 - spot.core, spot.chip_at(-step), spot.sibling()).wait_recv()

    place = lax.broadcasted_iota(jnp.int32, (block, 1), 0) + pl.program_id(0) * block
    fills = (place == slot_row[...]).astype(jnp.float32)
    empty = 1.0 - jnp.sum(fills, axis=1, keepdims=True)
    placed = plain_dot(fills.astype(jnp.bfloat16), embedded_ref[...])
    fine_rows = fine_ref.shape[0]
    half = width // 2
    fine_sin, fine_cos = fine_ref[:, :half], fine_ref[:, half:]
    tables = []
    for at in range(block // fine_rows):
        row = coarse_ref[0, at : at + 1, :]
        sin, cos = row[:, :half], row[:, half:]
        tables.append(
            jnp.concatenate(
                [sin * fine_cos + cos * fine_sin, cos * fine_cos - sin * fine_sin], axis=1
            )
        )
    stream = placed + empty * vector(MASK) + jnp.concatenate(tables, axis=0)
    stream_ref[...] = stream
    empty_ref[...] = empty
    normed, _ = normalize(stream)
    low = (normed * vector(FIRST_GAIN) + vector(FIRST_SHIFT)).astype(jnp.bfloat16)
    normed_ref[...] = low
    query = plain_dot(low, joint_ref[:, :width]) + vector(QUERY_BIAS)
    query_t_ref[...] = (query * QUERY_SCALE).T.astype(jnp.bfloat16)
    keys = plain_dot(low, joint_ref[:, width : 2 * width])
    key_ref[...] = keys.astype(jnp.bfloat16)
    key_t_ref[...] = keys.T.astype(jnp.bfloat16)
    values = plain_dot(low, joint_ref[:, 2 * width :]) + vector(VALUE_BIAS)
    value_ref[...] = values.astype(jnp.bfloat16)
    value_t_ref[...] = values.T.astype(jnp.bfloat16)


def enter(
    latents,
    embed_weight,
    slot_place,
    first_place,
    rows,
    vectors,
    joint_weight,
):
    splits = lax.axis_size("seq")
    width = embed_weight.shape[1]
    capacity = padded(latents.shape[0], 16)
    slots = splits * capacity
    vector_rows = sum(vector.shape[0] for vector in vectors) // width
    block = min(256, rows)
    fine_rows = min(32, block)
    fine = sinusoid(jnp.arange(fine_rows, dtype=jnp.int32), width)
    coarse = sinusoid(first_place + fine_rows * jnp.arange(rows // fine_rows, dtype=jnp.int32), width)
    row_block = pl.BlockSpec((block, width), lambda i: (i, 0))
    lane_block = pl.BlockSpec((width, block), lambda i: (0, i))
    low = jax.ShapeDtypeStruct((rows, width), jnp.bfloat16)
    low_t = jax.ShapeDtypeStruct((width, rows), jnp.bfloat16)
    return pl.pallas_call(
        enter_kernel,
        grid=(rows // block,),
        in_specs=[
            whole(latents.shape),
            whole(embed_weight.shape),
            whole(slot_place.shape),
            pl.BlockSpec((1, block // fine_rows, width), lambda i: (i, 0, 0)),
            whole(fine.shape),
            whole((width, 3 * width)),
        ]
        + [whole(vector.shape) for vector in vectors],
        out_specs=[
            row_block,
            pl.BlockSpec((block, 1), lambda i: (i, 0)),
            row_block,
            lane_block,
            row_block,
            lane_block,
            row_block,
            lane_block,
            whole((vector_rows, width)),
            whole((capacity, latents.shape[1])),
        ],
        out_shape=[
            jax.ShapeDtypeStruct((rows, width), jnp.float32),
            jax.ShapeDtypeStruct((rows, 1), jnp.float32),
            low,
            low_t,
            low,
            low_t,
            low,
            low_t,
            jax.ShapeDtypeStruct((vector_rows, width), jnp.float32),
            jax.ShapeDtypeStruct((capacity, latents.shape[1]), latents.dtype),
        ],
        scratch_shapes=[
            pltpu.VMEM((slots, width), jnp.bfloat16),
            pltpu.VMEM((1, slots), jnp.int32),
            pltpu.SemaphoreType.DMA((2, splits)),
        ],
        compiler_params=pltpu.CompilerParams(
            vmem_limit_bytes=VMEM_LIMIT, collective_id=0, has_side_effects=True
        ),
        cost_estimate=pl.CostEstimate(
            flops=2 * rows * width * (slots + 3 * width),
            bytes_accessed=20 * rows * width,
            transcendentals=0,
        ),
        name="enter",
    )(
        latents,
        embed_weight,
        slot_place,
        coarse.reshape(rows // block, block // fine_rows, width),
        fine,
        joint_weight,
        *vectors,
    )


def attend_kernel(
    key_ref, query_ref, value_ref, mixed_ref, exact_ref, total_ref, raised_ref, scores_ref, norm_ref
):
    span = key_ref.shape[0]
    block = query_ref.shape[1]
    slice_rows = min(256, span)
    slices = span // slice_rows
    query = query_ref[...]
    head_row = lax.broadcasted_iota(jnp.int32, query.shape, 0) // HEAD_DIM
    ones = jnp.ones((16, slice_rows), jnp.bfloat16)

    @pl.when(pl.program_id(1) == 0)
    def _():
        keys = key_ref[...].astype(jnp.float32)
        lane_head = lax.broadcasted_iota(jnp.int32, (128, 128), 0) // HEAD_DIM
        column = lax.broadcasted_iota(jnp.int32, (128, 128), 1)
        pick = (lane_head == column).astype(jnp.float32).astype(jnp.bfloat16)
        norms = plain_dot((keys * keys).astype(jnp.bfloat16), pick)
        norm_ref[...] = jnp.broadcast_to(jnp.max(norms, axis=0, keepdims=True), norm_ref.shape)

    squares = query.astype(jnp.float32)
    squares = squares * squares
    bound = jnp.zeros((1, 1), jnp.float32)
    for head in range(PACK):
        rows = slice(head * HEAD_DIM, (head + 1) * HEAD_DIM)
        longest = jnp.max(
            jnp.sum(squares[rows], axis=0, keepdims=True), axis=1, keepdims=True
        )
        bound = jnp.maximum(bound, longest * norm_ref[0:1, head : head + 1])
    small = bound[0, 0] * 1.02 < SAFE_SCORE**2

    def run(shifted):
        lag = slices if shifted else min(2, slices)
        steps = PACK * slices
        highest, held = {}, {}
        own_query = partial_highest = mixed = None
        for now in range(steps + lag):
            if now < steps:
                head, at = divmod(now, slices)
                part = slice(at * slice_rows, (at + 1) * slice_rows)
                if at == 0:
                    own_query = jnp.where(head_row == head, query, jnp.zeros_like(query))
                    partial_highest = jnp.full((8, block), -jnp.inf, jnp.float32)
                scores = plain_dot(key_ref[part, :], own_query)
                held[now] = scores
                if shifted:
                    partial_highest = jnp.maximum(
                        partial_highest, jnp.max(scores.reshape(slice_rows // 8, 8, block), axis=0)
                    )
                    if at == slices - 1:
                        highest[head] = jnp.max(partial_highest, axis=0, keepdims=True)
            if now >= lag:
                head, at = divmod(now - lag, slices)
                rows = slice(head * HEAD_DIM, (head + 1) * HEAD_DIM)
                part = slice(at * slice_rows, (at + 1) * slice_rows)
                scores = held.pop(now - lag)
                if shifted:
                    scores = scores - highest[head]
                raised = jnp.exp2(scores).astype(jnp.bfloat16)
                raised_ref[head, part, :] = raised
                term = plain_dot(jnp.concatenate([value_ref[rows, part], ones], axis=0), raised)
                mixed = term if at == 0 else mixed + term
                if at == slices - 1:
                    total = mixed[HEAD_DIM : HEAD_DIM + 1]
                    total_ref[0, head : head + 1, :] = total
                    mean = mixed[:HEAD_DIM] / total
                    exact_ref[rows, :] = mean
                    mixed_ref[rows, :] = mean.astype(jnp.bfloat16)

    @pl.when(small)
    def _():
        run(False)

    @pl.when(jnp.logical_not(small))
    def _():
        run(True)


def attend(keys, query_t, value_t):
    width, rows = query_t.shape
    span = keys.shape[0]
    block = min(512, rows)
    groups = width // 128
    lane_block = pl.BlockSpec((128, block), lambda g, i: (g, i))
    return pl.pallas_call(
        attend_kernel,
        grid=(groups, rows // block),
        in_specs=[
            pl.BlockSpec((span, 128), lambda g, i: (0, g)),
            lane_block,
            pl.BlockSpec((128, span), lambda g, i: (g, 0)),
        ],
        out_specs=[
            lane_block,
            lane_block,
            pl.BlockSpec((1, 8, block), lambda g, i: (g, 0, i)),
            pl.BlockSpec((PACK, span, block), lambda g, i: (g, 0, i)),
        ],
        out_shape=[
            jax.ShapeDtypeStruct((width, rows), jnp.bfloat16),
            jax.ShapeDtypeStruct((width, rows), jnp.float32),
            jax.ShapeDtypeStruct((groups, 8, rows), jnp.float32),
            jax.ShapeDtypeStruct((HEADS, span, rows), jnp.bfloat16),
        ],
        scratch_shapes=[
            pltpu.VMEM((span // min(256, span) + 1, min(256, span), block), jnp.float32),
            pltpu.VMEM((8, 128), jnp.float32),
        ],
        compiler_params=pltpu.CompilerParams(vmem_limit_bytes=VMEM_LIMIT),
        cost_estimate=pl.CostEstimate(
            flops=HEADS * span * rows * 512,
            bytes_accessed=2 * HEADS * span * rows,
            transcendentals=HEADS * span * rows,
        ),
        name="attend",
    )(keys, query_t, value_t)


def middle_kernel(
    stream_ref,
    mixed_ref,
    cotangent_ref,
    output_ref,
    expand_ref,
    contract_ref,
    vector_ref,
    decoded_ref,
    grad_middle_ref,
    grad_attended_ref,
    flat_ref,
    small_ref,
    expand_sum,
    contract_sum,
    output_sum,
    small_sum,
):
    width = stream_ref.shape[1]
    chunks = expand_ref.shape[1] // width

    def vector(row):
        return vector_ref[row : row + 1, :]

    @pl.when(pl.program_id(0) == 0)
    def _():
        expand_sum[...] = jnp.zeros_like(expand_sum)
        contract_sum[...] = jnp.zeros_like(contract_sum)
        output_sum[...] = jnp.zeros_like(output_sum)
        small_sum[...] = jnp.zeros_like(small_sum)

    mixed_t = mixed_ref[...]
    cotangent = cotangent_ref[...]
    middle = (
        stream_ref[...]
        + lead_dot(mixed_t, output_ref[...])
        + vector(OUTPUT_BIAS)
    )
    normed, scale = normalize(middle)
    gain = vector(SECOND_GAIN)
    low = (normed * gain + vector(SECOND_SHIFT)).astype(jnp.bfloat16)
    low_t = turned(low)
    output = middle + vector(CONTRACT_BIAS)
    grad_normed = jnp.zeros_like(middle)
    for chunk in range(chunks):
        part = slice(chunk * width, (chunk + 1) * width)
        hidden = plain_dot(low, expand_ref[:, part]) + vector(EXPAND_BIAS + chunk)
        below = 0.5 + 0.5 * lax.erf(hidden * math.sqrt(0.5))
        slope = below + hidden * jnp.exp(-0.5 * hidden * hidden) * (1.0 / math.sqrt(2 * math.pi))
        active = (hidden * below).astype(jnp.bfloat16)
        grad_hidden = (trail_dot(cotangent, contract_ref[part, :]) * slope).astype(jnp.bfloat16)
        output = output + plain_dot(active, contract_ref[part, :])
        grad_normed = grad_normed + trail_dot(grad_hidden, expand_ref[:, part])
        contract_sum[part, :] += lead_dot(active, cotangent)
        expand_sum[part, :] += plain_dot(low_t, grad_hidden)
        small_sum[chunk : chunk + 1, :] += column_sum(grad_hidden)
    decoded_ref[...] = output.astype(jnp.bfloat16)
    grad_middle = cotangent.astype(jnp.float32) + normalize_back(grad_normed * gain, normed, scale)
    grad_middle_ref[...] = grad_middle
    branch = grad_middle.astype(jnp.bfloat16)
    grad_attended_ref[...] = trail_dot(output_ref[...], branch).astype(jnp.bfloat16)
    output_sum[...] += plain_dot(mixed_t, branch)
    small_sum[chunks : chunks + 1, :] += column_sum(cotangent)
    small_sum[chunks + 1 : chunks + 2, :] += column_sum(branch)
    small_sum[chunks + 2 : chunks + 3, :] += column_sum(grad_normed * normed)
    small_sum[chunks + 3 : chunks + 4, :] += column_sum(grad_normed)

    @pl.when(pl.program_id(0) == pl.num_programs(0) - 1)
    def _():
        at = 0
        for total in (expand_sum, contract_sum, output_sum):
            flat_ref[at : at + total.shape[0], :] = total[...].astype(flat_ref.dtype)
            at += total.shape[0]
        if at < flat_ref.shape[0]:
            flat_ref[at:, :] = jnp.zeros((flat_ref.shape[0] - at, width), flat_ref.dtype)
        small_ref[...] = small_sum[...]


def middle_block(
    stream,
    mixed_t,
    cotangent,
    output_weight,
    expand_weight,
    contract_weight,
    vectors,
    flat_rows,
):
    rows, width = stream.shape
    hidden = expand_weight.shape[1]
    block = min(256, rows)
    row_block = pl.BlockSpec((block, width), lambda i: (i, 0))
    lane_block = pl.BlockSpec((width, block), lambda i: (0, i))
    small_rows = hidden // width + 4
    return pl.pallas_call(
        middle_kernel,
        grid=(rows // block,),
        in_specs=[
            row_block,
            lane_block,
            row_block,
            whole((width, width)),
            whole((width, hidden)),
            whole((hidden, width)),
            whole(vectors.shape),
        ],
        out_specs=[
            row_block,
            row_block,
            lane_block,
            whole((flat_rows, width)),
            whole((small_rows, width)),
        ],
        out_shape=[
            jax.ShapeDtypeStruct((rows, width), jnp.bfloat16),
            jax.ShapeDtypeStruct((rows, width), jnp.float32),
            jax.ShapeDtypeStruct((width, rows), jnp.bfloat16),
            jax.ShapeDtypeStruct((flat_rows, width), jnp.bfloat16),
            jax.ShapeDtypeStruct((small_rows, width), jnp.float32),
        ],
        scratch_shapes=[
            pltpu.VMEM((hidden, width), jnp.float32),
            pltpu.VMEM((hidden, width), jnp.float32),
            pltpu.VMEM((width, width), jnp.float32),
            pltpu.VMEM((small_rows, width), jnp.float32),
        ],
        compiler_params=pltpu.CompilerParams(vmem_limit_bytes=VMEM_LIMIT),
        cost_estimate=pl.CostEstimate(
            flops=2 * rows * width * (6 * hidden + 3 * width),
            bytes_accessed=16 * rows * width,
            transcendentals=2 * rows * hidden,
        ),
        name="middle",
    )(
        stream,
        mixed_t,
        cotangent,
        output_weight,
        expand_weight,
        contract_weight,
        vectors,
    )


def attend_back_kernel(
    steps,
    raised_ref,
    total_ref,
    value_ref,
    key_ref,
    query_ref,
    exact_ref,
    grad_ref,
    flat_ref,
    rows_ref,
    latents_ref,
    grad_query_ref,
    grad_key_ref,
    grad_value_ref,
    summed_ref,
    decoded_ref,
    gathered_ref,
    key_sum,
    value_sum,
    exchange_sems,
    exchange_local,
    gather_sems,
    gather_local,
    *sum_refs,
):
    spot = Spot()
    tree = TreeSum(spot, flat_ref, summed_ref, sum_refs, True)
    clips, share = decoded_ref.shape[0], decoded_ref.shape[1]
    mine, part = spot.index % clips, spot.index // clips

    def member(step):
        return (mine + step) % clips

    def exchange(step):
        return send(
            rows_ref.at[span_of(member(step) * share, share)],
            decoded_ref.at[mine],
            exchange_sems,
            step,
            (spot.layer, part * clips + member(step)),
        )

    def own_rows():
        return pltpu.make_async_copy(
            rows_ref.at[span_of(mine * share, share)], decoded_ref.at[mine], exchange_local
        )

    capacity = latents_ref.shape[0]

    def held(core, chip):
        return gathered_ref.at[span_of((chip * 2 + core) * capacity, capacity)]

    def share_own(at, device):
        return send(latents_ref, held(spot.core, spot.chip), gather_sems, at, device)

    def pass_on(at, core, step):
        place = held(core, spot.chip_at(-step))
        return send(place, place, gather_sems, at, spot.sibling())

    def keep_own():
        return pltpu.make_async_copy(latents_ref, held(spot.core, spot.chip), gather_local)

    step_now = pl.program_id(0) * pl.num_programs(1) + pl.program_id(1)

    def at_step(fraction):
        return pl.when(step_now == fraction * steps // 32)

    @at_step(0)
    def _():
        others = spot.tree() + [
            (spot.layer, part * clips + member(step)) for step in range(1, clips)
        ]
        count = spot.meet(others)
        pl.semaphore_wait(pltpu.get_barrier_semaphore(), count)
        tree.start()

    @at_step(4)
    def _():
        tree.near_to_far()

    @at_step(11)
    def _():
        tree.far_to_deep()
        own_rows().start()
        for step in range(1, clips):
            exchange(step).start()
        keep_own().start()
        for step in range(1, spot.half):
            share_own(step, spot.peer(step)).start()
        share_own(0, spot.sibling()).start()

    @at_step(15)
    def _():
        tree.deep_to_layer()

    @at_step(19)
    def _():
        tree.layer_to_part()

    @at_step(24)
    def _():
        for step in range(1, spot.half):
            pass_on(step, spot.core, step).wait_recv()
            pass_on(spot.half + step, spot.core, step).start()

    @at_step(29)
    def _():
        tree.part_to_half()

    @at_step(31)
    def _():
        tree.finish()
        own_rows().wait()
        for step in range(1, clips):
            exchange(step).wait_send()
        for step in range(1, clips):
            send(
                rows_ref.at[span_of(mine * share, share)],
                decoded_ref.at[member(-step)],
                exchange_sems,
                step,
                (spot.layer, part * clips + member(step)),
            ).wait_recv()
        keep_own().wait()
        for step in range(1, spot.half):
            share_own(step, spot.peer(step)).wait_send()
        share_own(0, spot.sibling()).wait_send()
        pass_on(0, 1 - spot.core, 0).wait_recv()
        for step in range(1, spot.half):
            pass_on(spot.half + step, spot.core, step).wait_send()
            pass_on(spot.half + step, 1 - spot.core, step).wait_recv()

    @pl.when(pl.program_id(1) == 0)
    def _():
        key_sum[...] = jnp.zeros_like(key_sum)
        value_sum[...] = jnp.zeros_like(value_sum)

    block = query_ref.shape[1]
    head_row = lax.broadcasted_iota(jnp.int32, (128, block), 0) // HEAD_DIM
    head_col = lax.broadcasted_iota(jnp.int32, (block, 128), 1) // HEAD_DIM
    inverse = 1.0 / total_ref[0, 0:PACK]
    inverse = jnp.concatenate(
        [jnp.broadcast_to(inverse[h : h + 1], (HEAD_DIM, block)) for h in range(PACK)], axis=0
    )
    grad_low = (grad_ref[...].astype(jnp.float32) * inverse).astype(jnp.bfloat16)
    grad = grad_low.astype(jnp.float32)
    inner = grad * exact_ref[...]
    grad_turned = grad.T.astype(jnp.bfloat16)
    query_turned = turned(query_ref[...])
    span = value_ref.shape[0]
    slice_rows = min(256, span)
    units = [(head, at) for head in range(PACK) for at in range(0, span, slice_rows)]
    lag = 2
    weights = {}
    grad_query = None
    for now in range(len(units) + lag):
        if now < len(units):
            head, at = units[now]
            own_grad = jnp.where(head_row == head, grad_low, jnp.zeros_like(grad_low))
            weights[now] = plain_dot(value_ref[at : at + slice_rows, :], own_grad)
        if now >= lag:
            head, at = units[now - lag]
            rows = slice(head * HEAD_DIM, (head + 1) * HEAD_DIM)
            part = slice(at, at + slice_rows)
            row_inner = jnp.sum(inner[rows], axis=0, keepdims=True)
            raised = raised_ref[head, part, :]
            grad_scores = raised * (weights.pop(now - lag) - row_inner).astype(jnp.bfloat16)
            value_sum[part, :] += plain_dot(
                raised, jnp.where(head_col == head, grad_turned, jnp.zeros_like(grad_turned))
            )
            key_sum[part, :] += plain_dot(
                grad_scores, jnp.where(head_col == head, query_turned, jnp.zeros_like(query_turned))
            )
            term = plain_dot(key_ref[rows, part], grad_scores)
            grad_query = term if at == 0 else grad_query + term
            if at + slice_rows == span:
                grad_query_ref[rows, :] = (grad_query * HEAD_DIM ** (-0.5)).astype(jnp.bfloat16)

    @pl.when(pl.program_id(1) == pl.num_programs(1) - 1)
    def _():
        grad_key_ref[...] = (key_sum[...] * (1.0 / LOG2E)).astype(jnp.bfloat16)
        grad_value_ref[...] = value_sum[...].astype(jnp.bfloat16)


def attend_back(raised, total, values, key_t, query_t, exact_t, grad_t, flat, decoded_rows, latents):
    splits, layers = lax.axis_size("seq"), lax.axis_size("dp")
    clips, share, _ = decoded_rows.shape
    width, rows = query_t.shape
    span = values.shape[0]
    block = min(256, rows)
    groups = width // 128
    lane_block = pl.BlockSpec((128, block), lambda g, i: (g, i))
    return pl.pallas_call(
        partial(attend_back_kernel, groups * (rows // block)),
        grid=(groups, rows // block),
        in_specs=[
            pl.BlockSpec((PACK, span, block), lambda g, i: (g, 0, i)),
            pl.BlockSpec((1, 8, block), lambda g, i: (g, 0, i)),
            pl.BlockSpec((span, 128), lambda g, i: (0, g)),
            pl.BlockSpec((128, span), lambda g, i: (g, 0)),
            lane_block,
            lane_block,
            lane_block,
            pl.BlockSpec(memory_space=pl.ANY),
            pl.BlockSpec(memory_space=pl.ANY),
            pl.BlockSpec(memory_space=pl.ANY),
        ],
        out_specs=[
            lane_block,
            pl.BlockSpec((span, 128), lambda g, i: (0, g)),
            pl.BlockSpec((span, 128), lambda g, i: (0, g)),
            pl.BlockSpec(memory_space=pl.ANY),
            pl.BlockSpec(memory_space=pl.ANY),
            pl.BlockSpec(memory_space=pl.ANY),
        ],
        out_shape=[
            jax.ShapeDtypeStruct((width, rows), jnp.bfloat16),
            jax.ShapeDtypeStruct((span, width), jnp.bfloat16),
            jax.ShapeDtypeStruct((span, width), jnp.bfloat16),
            jax.ShapeDtypeStruct(flat.shape, flat.dtype),
            jax.ShapeDtypeStruct(decoded_rows.shape, decoded_rows.dtype),
            jax.ShapeDtypeStruct((splits * latents.shape[0], latents.shape[1]), latents.dtype),
        ],
        scratch_shapes=[
            pltpu.VMEM((span, 128), jnp.float32),
            pltpu.VMEM((span, 128), jnp.float32),
            pltpu.SemaphoreType.DMA((2, clips)),
            pltpu.SemaphoreType.DMA,
            pltpu.SemaphoreType.DMA((2, splits)),
            pltpu.SemaphoreType.DMA,
        ]
        + TreeSum.scratch(flat.shape[0], flat.shape[1], True, splits, layers),
        compiler_params=pltpu.CompilerParams(
            vmem_limit_bytes=VMEM_LIMIT, collective_id=1, has_side_effects=True
        ),
        cost_estimate=pl.CostEstimate(
            flops=HEADS * span * rows * 1024,
            bytes_accessed=2 * HEADS * span * rows,
            transcendentals=0,
        ),
        name="attend_back",
    )(raised, total, values, key_t, query_t, exact_t, grad_t, flat, decoded_rows.reshape(clips * share, width), latents)


def leave_kernel(
    grad_query_ref,
    grad_key_ref,
    grad_value_ref,
    stream_ref,
    empty_ref,
    low_ref,
    grad_middle_ref,
    vector_ref,
    joint_ref,
    slot_ref,
    latents_ref,
    embed_ref,
    early_ref,
    latent_grad_ref,
    joint_total_ref,
    embed_total_ref,
    joint_sum,
    small_sum,
    grad_all,
    joint_flat,
    embed_flat,
    back_all,
    near_in,
    far_out,
    far_in,
    latents_all,
    sems,
    local,
    *sum_refs,
):
    block, width = stream_ref.shape
    step_now = pl.program_id(0)
    spot = Spot()
    capacity = back_all.shape[0] // spot.splits
    others = spot.tree()
    blocks = pl.num_programs(0) // 2
    count = len(sum_refs) // 2
    joint_tree = TreeSum(spot, joint_flat, joint_total_ref, sum_refs[:count], True)
    embed_tree = TreeSum(spot, embed_flat, embed_total_ref, sum_refs[count:], False)

    def load_latents():
        return pltpu.make_async_copy(latents_ref, latents_all, local)

    @pl.when(step_now == 0)
    def _():
        spot.meet(others)
        load_latents().start()
        joint_sum[...] = jnp.zeros_like(joint_sum)
        small_sum[...] = jnp.zeros_like(small_sum)

    @pl.when(step_now < blocks)
    def _():
        low_t = turned(low_ref[...])
        sides = [turned(grad_query_ref[...]), grad_key_ref[...], grad_value_ref[...]]
        for at, side in enumerate(sides):
            joint_sum[at * width : (at + 1) * width, :] += plain_dot(low_t, side)
        small_sum[3:4, :] += column_sum(sides[0])
        small_sum[4:5, :] += column_sum(sides[2])

    @pl.when(step_now == blocks - 1)
    def _():
        rows = joint_sum.shape[0]
        joint_flat[:rows, :] = joint_sum[...].astype(jnp.bfloat16)
        if joint_flat.shape[0] > rows:
            joint_flat[rows:, :] = jnp.zeros(
                (joint_flat.shape[0] - rows, width), jnp.bfloat16
            )
        pl.semaphore_wait(pltpu.get_barrier_semaphore(), len(others))
        joint_tree.start()

    @pl.when(step_now == blocks + blocks // 4)
    def _():
        joint_tree.near_to_far()

    @pl.when(step_now >= blocks)
    def _():
        normed, scale = normalize(stream_ref[...])
        sides = [turned(grad_query_ref[...]), grad_key_ref[...], grad_value_ref[...]]
        grad_normed = jnp.zeros_like(normed)
        for at, side in enumerate(sides):
            grad_normed = grad_normed + trail_dot(
                side, joint_ref[:, at * width : (at + 1) * width]
            )
        grad_stream = grad_middle_ref[...] + normalize_back(
            grad_normed * vector_ref[FIRST_GAIN : FIRST_GAIN + 1, :], normed, scale
        )
        grad_all[pl.ds(pl.multiple_of((step_now - blocks) * block, block), block), :] = (
            grad_stream.astype(jnp.bfloat16)
        )
        small_sum[0:1, :] += column_sum(empty_ref[...] * grad_stream)
        small_sum[1:2, :] += column_sum(grad_normed * normed)
        small_sum[2:3, :] += column_sum(grad_normed)

    @pl.when(step_now == pl.num_programs(0) - 1)
    def _():
        place = lax.broadcasted_iota(jnp.int32, (1, grad_all.shape[0]), 1)

        def gathered(owner):
            slots = slot_ref[pl.ds(owner, 1), :].astype(jnp.float32)
            slots = jnp.broadcast_to(slots, (8, slots.shape[1])).T[:capacity, 0:1]
            takes = (slots.astype(jnp.int32) == place).astype(jnp.float32).astype(jnp.bfloat16)
            return plain_dot(takes, grad_all[...])

        def rows_of(owner):
            return span_of(owner * capacity, capacity)

        def part(at):
            return pl.ds(at * capacity, capacity)

        def near_copy(step):
            owner = spot.chip_at(step) * 2 + 1 - spot.core
            return send(
                back_all.at[rows_of(owner)], near_in.at[part(step)], sems, step, spot.sibling()
            )

        def far_copy(step):
            return send(
                far_out.at[part(step - 1)],
                far_in.at[part(step - 1)],
                sems,
                spot.half + step,
                spot.peer(step),
            )

        for step in list(range(1, spot.half)) + [0]:
            owner = spot.chip_at(step) * 2 + 1 - spot.core
            back_all[rows_of(owner), :] = gathered(owner).astype(jnp.bfloat16)
            near_copy(step).start()
            owner = spot.chip_at(step) * 2 + spot.core
            own = gathered(owner)
            back_all[rows_of(owner), :] = own.astype(jnp.bfloat16)
            near_copy(step).wait()
            own = own + near_in[part(step), :].astype(jnp.float32)
            if step > 0:
                far_out[part(step - 1), :] = own.astype(jnp.bfloat16)
                far_copy(step).start()
            if step == 1:
                joint_tree.far_to_deep()
        load_latents().wait()
        embed_rows = embed_ref.shape[0]
        embed_flat[:embed_rows, :] = lead_dot(latents_all[...], back_all[...]).astype(jnp.bfloat16)
        small_sum[5:6, :] = column_sum(back_all[...])
        small = jnp.concatenate([early_ref[...], small_sum[...]], axis=0)
        rest = embed_flat.shape[0] - embed_rows - small.shape[0]
        if rest:
            small = jnp.concatenate([small, jnp.zeros((rest, width), jnp.float32)], axis=0)
        embed_flat[embed_rows:, :] = small.astype(jnp.bfloat16)
        embed_tree.start()
        joint_tree.deep_to_layer()
        embed_tree.near_to_far()
        joint_tree.layer_to_part()
        embed_tree.far_to_deep()
        for step in range(1, spot.half):
            far_copy(step).wait()
            own = own + far_in[part(step - 1), :].astype(jnp.float32)
        grad_embedded = own[: latent_grad_ref.shape[0]].astype(jnp.bfloat16)
        latent_grad_ref[...] = trail_dot(grad_embedded, embed_ref[...]).astype(jnp.bfloat16)
        joint_tree.part_to_half()
        embed_tree.deep_to_layer()
        joint_tree.finish()
        embed_tree.part_to_half()
        embed_tree.finish()


def leave(
    grad_query_t,
    grad_key,
    grad_value,
    stream,
    empty,
    low,
    grad_middle,
    vectors,
    joint_weight,
    slot_place,
    latents_all,
    embed_weight,
    early_small,
    own_rows,
):
    splits, layers = lax.axis_size("seq"), lax.axis_size("dp")
    rows, width = stream.shape
    slots = latents_all.shape[0]
    latent_shape = (own_rows, latents_all.shape[1])
    capacity = slots // splits
    half = splits // 2
    block = min(256, rows)
    blocks = rows // block
    row_block = pl.BlockSpec((block, width), lambda i: (i % blocks, 0))
    first_block = pl.BlockSpec((block, width), lambda i: (jnp.minimum(i, blocks - 1), 0))
    later_block = pl.BlockSpec((block, width), lambda i: (jnp.maximum(i - blocks, 0), 0))
    lane_block = pl.BlockSpec((width, block), lambda i: (0, i % blocks))
    joint_rows = padded(3 * width, splits * layers * 16)
    embed_rows = padded(embed_weight.shape[0] + early_small.shape[0] + 8, splits * 16)
    return pl.pallas_call(
        leave_kernel,
        grid=(2 * blocks,),
        in_specs=[
            lane_block,
            row_block,
            row_block,
            later_block,
            pl.BlockSpec((block, 1), lambda i: (jnp.maximum(i - blocks, 0), 0)),
            first_block,
            later_block,
            whole(vectors.shape),
            whole((width, 3 * width)),
            whole(slot_place.shape),
            pl.BlockSpec(memory_space=pl.ANY),
            whole(embed_weight.shape),
            whole(early_small.shape),
        ],
        out_specs=[
            whole(latent_shape),
            pl.BlockSpec(memory_space=pl.ANY),
            pl.BlockSpec(memory_space=pl.ANY),
        ],
        out_shape=[
            jax.ShapeDtypeStruct(latent_shape, jnp.bfloat16),
            jax.ShapeDtypeStruct((joint_rows, width), jnp.bfloat16),
            jax.ShapeDtypeStruct((embed_rows, width), jnp.bfloat16),
        ],
        scratch_shapes=[
            pltpu.VMEM((3 * width, width), jnp.float32),
            pltpu.VMEM((8, width), jnp.float32),
            pltpu.VMEM((rows, width), jnp.bfloat16),
            pltpu.VMEM((joint_rows, width), jnp.bfloat16),
            pltpu.VMEM((embed_rows, width), jnp.bfloat16),
            pltpu.VMEM((slots, width), jnp.bfloat16),
            pltpu.VMEM((half * capacity, width), jnp.bfloat16),
            pltpu.VMEM((max(half - 1, 1) * capacity, width), jnp.bfloat16),
            pltpu.VMEM((max(half - 1, 1) * capacity, width), jnp.bfloat16),
            pltpu.VMEM(latents_all.shape, latents_all.dtype),
            pltpu.SemaphoreType.DMA((2, splits)),
            pltpu.SemaphoreType.DMA,
        ]
        + TreeSum.scratch(joint_rows, width, True, splits, layers)
        + TreeSum.scratch(embed_rows, width, False, splits, layers),
        compiler_params=pltpu.CompilerParams(
            vmem_limit_bytes=VMEM_LIMIT, collective_id=2, has_side_effects=True
        ),
        cost_estimate=pl.CostEstimate(
            flops=2 * rows * width * (slots + 6 * width),
            bytes_accessed=20 * rows * width,
            transcendentals=0,
        ),
        name="leave",
    )(
        grad_query_t,
        grad_key,
        grad_value,
        stream,
        empty,
        low,
        grad_middle,
        vectors,
        joint_weight,
        slot_place,
        latents_all,
        embed_weight,
        early_small,
    )


def finish_kernel(
    expand_ref,
    contract_ref,
    output_ref,
    joint_ref,
    embed_ref,
    small_ref,
    expand_out,
    contract_out,
    output_out,
    joint_out,
    embed_out,
    *small_outs,
):
    for source, target in (
        (expand_ref, expand_out),
        (contract_ref, contract_out),
        (output_ref, output_out),
        (joint_ref, joint_out),
        (embed_ref, embed_out),
    ):
        target[...] = source[...].astype(jnp.float32)
    small = small_ref[...].astype(jnp.float32)
    width = small.shape[1]
    at = 0
    for target in small_outs:
        for start in range(0, target.shape[0], width):
            target[start : start + width] = small[at]
            at += 1


def finish(early_sum, joint_sum, embed_sum, hidden, embed_rows, small_sizes):
    width = early_sum.shape[1]
    chunks = hidden // width
    square = (width, width)
    embed_block = (embed_rows // chunks, width)
    sides = 3
    return pl.pallas_call(
        finish_kernel,
        grid=(chunks,),
        in_specs=[
            pl.BlockSpec(square, lambda i: (i, 0)),
            pl.BlockSpec(square, lambda i: (chunks + i, 0)),
            pl.BlockSpec(square, lambda i: (2 * chunks, 0)),
            pl.BlockSpec(square, lambda i: (jnp.minimum(i, sides - 1), 0)),
            pl.BlockSpec(embed_block, lambda i: (i, 0)),
            pl.BlockSpec((16, width), lambda i: (embed_rows // 16, 0)),
        ],
        out_specs=[
            pl.BlockSpec(square, lambda i: (0, i)),
            pl.BlockSpec(square, lambda i: (i, 0)),
            pl.BlockSpec(square, lambda i: (0, 0)),
            pl.BlockSpec(square, lambda i: (0, jnp.minimum(i, sides - 1))),
            pl.BlockSpec(embed_block, lambda i: (i, 0)),
        ]
        + [whole((size,)) for size in small_sizes],
        out_shape=[
            jax.ShapeDtypeStruct((width, hidden), jnp.float32),
            jax.ShapeDtypeStruct((hidden, width), jnp.float32),
            jax.ShapeDtypeStruct(square, jnp.float32),
            jax.ShapeDtypeStruct((width, sides * width), jnp.float32),
            jax.ShapeDtypeStruct((embed_rows, width), jnp.float32),
        ]
        + [jax.ShapeDtypeStruct((size,), jnp.float32) for size in small_sizes],
        compiler_params=pltpu.CompilerParams(vmem_limit_bytes=VMEM_LIMIT),
        cost_estimate=pl.CostEstimate(
            flops=0, bytes_accessed=12 * width * (hidden + width), transcendentals=0
        ),
        name="finish",
    )(early_sum, early_sum, early_sum, joint_sum, embed_sum, embed_sum)


def body(
    latents,
    clip_ids,
    restore,
    counts,
    embed_weight,
    embed_bias,
    mask_token,
    first_gain,
    first_shift,
    joint_weight,
    query_bias,
    value_bias,
    output_weight,
    output_bias,
    second_gain,
    second_shift,
    expand_weight,
    expand_bias,
    contract_weight,
    contract_bias,
    cotangent,
):
    splits = lax.axis_size("seq")
    seq_index = lax.axis_index("seq")
    capacity = latents.shape[0]
    clip_count, clip_share, model_width = cotangent.shape
    sharers = splits // clip_count
    rows = clip_count * clip_share
    own_clip = seq_index % clip_count
    first_place = (seq_index // clip_count) * rows
    exchange_groups = [[s * clip_count + c for c in range(clip_count)] for s in range(sharers)]
    clip_groups = [[s * clip_count + c for s in range(sharers)] for c in range(clip_count)]

    def to_clips(blocks):
        return lax.all_to_all(
            blocks,
            "seq",
            split_axis=0,
            concat_axis=0,
            tiled=True,
            axis_index_groups=exchange_groups if sharers > 1 else None,
        )

    live = jnp.arange(capacity, dtype=jnp.int32)[None, :] < counts[:, None]
    mine = live & ((clip_ids % clip_count).reshape(splits, capacity) == own_clip)
    slot_place = jnp.where(mine, restore.reshape(splits, capacity) - first_place, -1)
    slot_place = jnp.pad(
        slot_place, ((0, 0), (0, padded(capacity, 128) - capacity)), constant_values=-1
    )
    (
        stream,
        empty,
        first_low,
        query_t,
        keys,
        key_t,
        values,
        value_t,
        vectors,
        latents,
    ) = enter(
        latents,
        embed_weight,
        slot_place,
        first_place,
        rows,
        [
            embed_bias,
            mask_token,
            first_gain,
            first_shift,
            query_bias,
            value_bias,
            output_bias,
            second_gain,
            second_shift,
            contract_bias,
            expand_bias,
        ],
        joint_weight,
    )
    cotangent, keys = lax.optimization_barrier((cotangent, keys))
    grad_output = to_clips(cotangent).reshape(rows, model_width)
    if sharers > 1:
        keys = lax.all_gather(keys, "seq", axis=0, tiled=True, axis_index_groups=clip_groups)
        values = lax.all_gather(values, "seq", axis=0, tiled=True, axis_index_groups=clip_groups)
        key_t, value_t = keys.T, values.T
    mixed_t, exact_t, total, raised = attend(keys, query_t, value_t)
    (
        decoded_rows,
        grad_middle,
        grad_attended_t,
        early_flat,
        early_small,
    ) = middle_block(
        stream,
        mixed_t,
        grad_output,
        output_weight,
        expand_weight,
        contract_weight,
        vectors,
        padded(2 * expand_weight.shape[1] + model_width, splits * lax.axis_size("dp") * 16),
    )
    grad_query_t, grad_key, grad_value, early_sum, decoded, latents_all = attend_back(
        raised,
        total,
        values,
        key_t,
        query_t,
        exact_t,
        grad_attended_t,
        early_flat,
        decoded_rows.reshape(clip_count, clip_share, model_width),
        latents,
    )
    if sharers > 1:
        grad_key, grad_value = (
            lax.psum_scatter(
                side, "seq", scatter_dimension=0, tiled=True, axis_index_groups=clip_groups
            )
            for side in (grad_key, grad_value)
        )
    latent_grad, joint_sum, embed_sum = leave(
        grad_query_t,
        grad_key,
        grad_value,
        stream,
        empty,
        first_low,
        grad_middle,
        vectors,
        joint_weight,
        slot_place,
        latents_all,
        embed_weight,
        early_small,
        capacity,
    )
    hidden_width = expand_weight.shape[1]
    (
        grad_expand,
        grad_contract,
        grad_output_weight,
        grad_joint_weight,
        grad_embed_weight,
        grad_expand_bias,
        grad_contract_bias,
        grad_output_bias,
        grad_second_gain,
        grad_second_shift,
        grad_mask,
        grad_first_gain,
        grad_first_shift,
        grad_query_bias,
        grad_value_bias,
        grad_embed_bias,
    ) = finish(
        early_sum,
        joint_sum,
        embed_sum,
        hidden_width,
        embed_weight.shape[0],
        [hidden_width] + [model_width] * 10,
    )
    return (
        decoded,
        latent_grad,
        grad_embed_weight,
        grad_embed_bias,
        grad_mask,
        grad_first_gain,
        grad_first_shift,
        grad_joint_weight,
        grad_query_bias,
        grad_value_bias,
        grad_output_weight,
        grad_output_bias,
        grad_second_gain,
        grad_second_shift,
        grad_expand,
        grad_expand_bias,
        grad_contract,
        grad_contract_bias,
    )


def solution(mesh):
    placed = (
        (P(("dp", "seq"), None),) + (P("dp"),) * 3 + (P(),) * 16 + (P("dp", "seq", None),)
    )
    return jax.shard_map(
        body,
        mesh=mesh,
        in_specs=placed,
        out_specs=(P("dp", "seq", None), P(("dp", "seq"), None)) + (P(),) * 16,
        check_vma=False,
    )
```

```python
from functools import partial
import math

import jax
import jax.numpy as jnp
from jax import lax
from jax.experimental import pallas as pl
from jax.experimental.pallas import tpu as pltpu
from jax.sharding import PartitionSpec as P

HEADS = 16
HEAD_DIM = 32
PACK = 128 // HEAD_DIM
VMEM_LIMIT = 56 * 1024 * 1024
SAFE_SCORE = 80.0
MESH = pl.DeviceIdType.MESH
LOG2E = math.log2(math.e)
QUERY_SCALE = LOG2E * HEAD_DIM ** (-0.5)


epsilon = 1e-06


EMBED_BIAS, MASK, FIRST_GAIN, FIRST_SHIFT, QUERY_BIAS, VALUE_BIAS = range(6)
OUTPUT_BIAS, SECOND_GAIN, SECOND_SHIFT, CONTRACT_BIAS, EXPAND_BIAS = range(6, 11)


def whole(shape):
    return pl.BlockSpec(shape, lambda *_: (0,) * len(shape))


def turned(values):
    return values.astype(jnp.float32).T.astype(values.dtype)


def sinusoid(places, table_width):
    half_width = table_width // 2
    frequency = jnp.exp(-math.log(10000.0) * jnp.arange(half_width, dtype=jnp.float32) / half_width)
    angles = places.astype(jnp.float32)[:, None] * frequency[None, :]
    return jnp.concatenate([jnp.sin(angles), jnp.cos(angles)], axis=1)


def plain_dot(left, right):
    return jnp.dot(left, right, preferred_element_type=jnp.float32)


def lead_dot(left, right):
    return lax.dot_general(
        left, right, (((0,), (0,)), ((), ())), preferred_element_type=jnp.float32
    )


def trail_dot(left, right):
    return lax.dot_general(
        left, right, (((1,), (1,)), ((), ())), preferred_element_type=jnp.float32
    )


def column_sum(values):
    return jnp.sum(values.astype(jnp.float32), axis=0, keepdims=True)


def row_mean(values):
    return jnp.mean(values, axis=-1, keepdims=True)


def normalize(values):
    center = values - row_mean(values)
    scale = lax.rsqrt(row_mean(center * center) + epsilon)
    return center * scale, scale


def normalize_back(grad, normed, scale):
    return scale * (grad - row_mean(grad) - normed * row_mean(grad * normed))


class Spot:
    def __init__(self):
        self.layers, self.splits = lax.axis_size("dp"), lax.axis_size("seq")
        self.half = self.splits // 2
        self.layer, self.index = lax.axis_index("dp"), lax.axis_index("seq")
        self.core, self.chip = self.index % 2, self.index // 2

    def sibling(self):
        return (self.layer, self.chip * 2 + (1 - self.core))

    def chip_at(self, step):
        return (self.chip + step) % self.half

    def layer_at(self, step):
        return (self.layer + step) % self.layers

    def peer(self, step):
        return (self.layer, self.chip_at(step) * 2 + self.core)

    def above(self, step):
        return (self.layer_at(step), self.index)

    def routes(self):
        if self.half != 4:
            steps = range(1, self.half)
            return (
                [self.chip_at(-step) for step in steps],
                [self.peer(step) for step in steps],
                [self.chip for _ in steps],
            )
        across, up = self.chip % 2, self.chip // 2
        beside = up * 2 + 1 - across
        above = (1 - up) * 2 + across
        first = beside * (1 - self.core) + above * self.core
        second = above * (1 - self.core) + beside * self.core
        return (
            [first, second, 3 - self.chip],
            [(self.layer, chip * 2 + self.core) for chip in (first, second, second)],
            [self.chip, self.chip, first],
        )

    def passed_on(self, at):
        return self.half == 4 and at == 2

    def sibling_turn(self, at):
        return [1, 0, 2][at] if self.half == 4 else at

    def meet(self, others):
        barrier = pltpu.get_barrier_semaphore()
        for other in others:
            pl.semaphore_signal(barrier, inc=1, device_id=other, device_id_type=MESH)
        return len(others)

    def tree(self, layers=True):
        others = [self.sibling()] + [self.peer(step) for step in range(1, self.half)]
        if layers:
            others += [self.above(step) for step in range(1, self.layers)]
        return others


def padded(rows, unit):
    return -(-rows // unit) * unit


def span_of(start, size):
    return pl.ds(pl.multiple_of(start, 16), size)


def send(source, target, sems, at, device):
    return pltpu.make_async_remote_copy(
        src_ref=source,
        dst_ref=target,
        send_sem=sems.at[0, at],
        recv_sem=sems.at[1, at],
        device_id=device,
        device_id_type=MESH,
    )


class TreeSum:
    def __init__(self, spot, source, result, refs, scatter):
        (
            self.near,
            self.near_sum,
            self.far,
            self.far_sum,
            self.deep,
            self.done,
            self.sems,
            self.local,
        ) = refs
        self.spot, self.source, self.result, self.scatter = spot, source, result, scatter
        self.part = self.far_sum.shape[0]
        self.piece = self.done.shape[0]

    @staticmethod
    def scratch(rows, width, scatter, splits, layers):
        half = splits // 2
        part = rows // splits
        piece = part // layers if scatter else part
        low = jnp.bfloat16
        return [
            pltpu.VMEM((half * part, width), low),
            pltpu.VMEM((half * part, width), low),
            pltpu.VMEM((max(half - 1, 1) * part, width), low),
            pltpu.VMEM((part, width), low),
            pltpu.VMEM((layers * piece, width), low),
            pltpu.VMEM((piece, width), low),
            pltpu.SemaphoreType.DMA((2, 2 + 2 * half + 2 * layers)),
            pltpu.SemaphoreType.DMA((2,)),
        ]

    def near_copy(self):
        spot = self.spot
        rows = spot.half * self.part
        return send(
            self.source.at[span_of((1 - spot.core) * rows, rows)],
            self.near,
            self.sems,
            0,
            spot.sibling(),
        )

    def own_copy(self):
        rows = self.spot.half * self.part
        return pltpu.make_async_copy(
            self.source.at[span_of(self.spot.core * rows, rows)], self.near_sum, self.local.at[0]
        )

    def far_copy(self, step):
        return send(
            self.near_sum.at[span_of(self.spot.chip_at(step) * self.part, self.part)],
            self.far.at[span_of((step - 1) * self.part, self.part)],
            self.sems,
            1 + step,
            self.spot.peer(step),
        )

    def deep_copy(self, step):
        spot = self.spot
        if self.scatter:
            source = self.far_sum.at[span_of(spot.layer_at(step) * self.piece, self.piece)]
        else:
            source = self.far_sum
        return send(
            source,
            self.deep.at[span_of(spot.layer * self.piece, self.piece)],
            self.sems,
            1 + spot.half + step,
            spot.above(step),
        )

    def place(self, core, chip, layer=None):
        spot = self.spot
        start = (core * spot.half + chip) * self.part
        if layer is None:
            return span_of(start, self.part)
        return span_of(start + layer * self.piece, self.piece)

    def done_copy(self):
        spot = self.spot
        layer = spot.layer if self.scatter else None
        return pltpu.make_async_copy(
            self.done, self.result.at[self.place(spot.core, spot.chip, layer)], self.local.at[1]
        )

    def layer_copy(self, step, arriving):
        spot = self.spot
        layer = spot.layer_at(-step) if arriving else spot.layer
        return send(
            self.done,
            self.result.at[self.place(spot.core, spot.chip, layer)],
            self.sems,
            1 + spot.half + spot.layers + step,
            spot.above(step),
        )

    def part_copy(self, step, arriving):
        spot = self.spot
        place = self.place(spot.core, spot.chip_at(-step) if arriving else spot.chip)
        return send(
            self.result.at[place] if self.scatter else self.done,
            self.result.at[place],
            self.sems,
            1 + spot.half + 2 * spot.layers + step,
            spot.peer(step),
        )

    def half_copy(self, arriving):
        spot = self.spot
        rows = spot.half * self.part
        core = 1 - spot.core if arriving else spot.core
        place = span_of(core * rows, rows)
        return send(
            self.result.at[place], self.result.at[place], self.sems, 1, spot.sibling()
        )

    def start(self):
        self.own_copy().start()
        self.near_copy().start()

    def near_to_far(self):
        self.own_copy().wait()
        self.near_copy().wait()
        unit = self.part
        while unit > 160 and unit % 32 == 0:
            unit //= 2

        def add(at, _):
            rows = span_of(at * unit, unit)
            self.near_sum[rows, :] = (
                self.near_sum[rows, :].astype(jnp.float32) + self.near[rows, :].astype(jnp.float32)
            ).astype(jnp.bfloat16)
            return 0

        lax.fori_loop(0, self.spot.half * (self.part // unit), add, 0)
        for step in range(1, self.spot.half):
            self.far_copy(step).start()

    def far_to_deep(self):
        spot = self.spot
        for step in range(1, spot.half):
            self.far_copy(step).wait()
        unit = self.part
        while unit > 160 and unit % 32 == 0:
            unit //= 2

        def add(at, _):
            start = at * unit
            total = self.near_sum[span_of(spot.chip * self.part + start, unit), :].astype(
                jnp.float32
            )
            for step in range(1, spot.half):
                total = total + self.far[span_of((step - 1) * self.part + start, unit), :].astype(
                    jnp.float32
                )
            self.far_sum[span_of(start, unit), :] = total.astype(jnp.bfloat16)
            return 0

        lax.fori_loop(0, self.part // unit, add, 0)
        for step in range(1, spot.layers):
            self.deep_copy(step).start()
        own = self.far_sum[...]
        if self.scatter:
            own = self.far_sum[span_of(spot.layer * self.piece, self.piece), :]
        self.deep[span_of(spot.layer * self.piece, self.piece), :] = own

    def deep_to_layer(self):
        spot = self.spot
        for step in range(1, spot.layers):
            self.deep_copy(step).wait_send()
        for step in range(1, spot.layers):
            send(
                self.done,
                self.deep.at[span_of(spot.layer_at(-step) * self.piece, self.piece)],
                self.sems,
                1 + spot.half + step,
                spot.above(step),
            ).wait_recv()
        total = self.deep[: self.piece, :].astype(jnp.float32)
        for layer in range(1, spot.layers):
            total = total + self.deep[layer * self.piece : (layer + 1) * self.piece, :].astype(
                jnp.float32
            )
        self.done[...] = total.astype(jnp.bfloat16)
        self.done_copy().start()
        if self.scatter:
            for step in range(1, spot.layers):
                self.layer_copy(step, False).start()
        else:
            for step in range(1, spot.half):
                self.part_copy(step, False).start()

    def layer_to_part(self):
        spot = self.spot
        if not self.scatter:
            return
        self.done_copy().wait()
        for step in range(1, spot.layers):
            self.layer_copy(step, False).wait_send()
        for step in range(1, spot.layers):
            self.layer_copy(step, True).wait_recv()
        for step in range(1, spot.half):
            self.part_copy(step, False).start()

    def part_to_half(self):
        spot = self.spot
        if not self.scatter:
            self.done_copy().wait()
        for step in range(1, spot.half):
            self.part_copy(step, False).wait_send()
        for step in range(1, spot.half):
            self.part_copy(step, True).wait_recv()
        self.half_copy(False).start()

    def finish(self):
        self.half_copy(False).wait_send()
        self.half_copy(True).wait_recv()


def enter_kernel(
    latents_ref,
    embed_ref,
    slot_ref,
    coarse_ref,
    fine_ref,
    joint_ref,
    *refs,
):
    (
        stream_ref,
        empty_ref,
        normed_ref,
        query_t_ref,
        key_ref,
        key_t_ref,
        value_ref,
        value_t_ref,
        vector_ref,
        latents_out_ref,
        embedded_ref,
        slot_row,
        sems,
    ) = refs[-13:]
    vector_refs = refs[:-13]
    block, width = stream_ref.shape
    spot = Spot()
    capacity = embedded_ref.shape[0] // spot.splits

    def vector(row):
        return vector_ref[row : row + 1, :]

    @pl.when(pl.program_id(0) == 0)
    def _():
        count = spot.meet(spot.tree(False))
        at = 0
        for source in vector_refs:
            for start in range(0, source.shape[0], width):
                values = source[start : start + width].astype(jnp.float32)
                vector_ref[at : at + 1, :] = values.reshape(1, width)
                at += 1
        latents = latents_ref[...]
        rest = capacity - latents.shape[0]
        if rest:
            latents = jnp.concatenate(
                [latents.astype(jnp.float32), jnp.zeros((rest, latents.shape[1]), jnp.float32)],
                axis=0,
            ).astype(jnp.bfloat16)
        latents_out_ref[...] = latents
        embedded = plain_dot(latents, embed_ref[...]) + vector(EMBED_BIAS)

        def held(core, chip):
            return embedded_ref.at[span_of((chip * 2 + core) * capacity, capacity)]

        def share(at, core, chip, device):
            return send(held(core, chip), held(core, chip), sems, at, device)

        embedded_ref[span_of(spot.index * capacity, capacity), :] = embedded.astype(jnp.bfloat16)
        pl.semaphore_wait(pltpu.get_barrier_semaphore(), count)
        sources, targets, sent = spot.routes()

        def far(at):
            return share(1 + at, spot.core, sent[at], targets[at])

        def near(at, core):
            return share(spot.half + 1 + at, core, sources[at], spot.sibling())

        turns = range(len(targets))
        for at in turns:
            if not spot.passed_on(at):
                far(at).start()
        share(0, spot.core, spot.chip, spot.sibling()).start()
        for source in range(spot.splits):
            slot_row[:, source * capacity : (source + 1) * capacity] = slot_ref[
                source : source + 1, :capacity
            ]
        for at in turns:
            share(1 + at, spot.core, sources[at], targets[at]).wait_recv()
            if at == 0 and spot.passed_on(2):
                far(2).start()
            near(at, spot.core).start()
        for at in turns:
            far(at).wait_send()
        share(0, spot.core, spot.chip, spot.sibling()).wait_send()
        share(0, 1 - spot.core, spot.chip, spot.sibling()).wait_recv()
        for at in turns:
            near(at, spot.core).wait_send()
            share(
                spot.half + 1 + at, 1 - spot.core, sources[spot.sibling_turn(at)], spot.sibling()
            ).wait_recv()

    place = lax.broadcasted_iota(jnp.int32, (block, 1), 0) + pl.program_id(0) * block
    fills = (place == slot_row[...]).astype(jnp.float32)
    empty = 1.0 - jnp.sum(fills, axis=1, keepdims=True)
    placed = plain_dot(fills.astype(jnp.bfloat16), embedded_ref[...])
    fine_rows = fine_ref.shape[0]
    half = width // 2
    fine_sin, fine_cos = fine_ref[:, :half], fine_ref[:, half:]
    tables = []
    for at in range(block // fine_rows):
        row = coarse_ref[0, at : at + 1, :]
        sin, cos = row[:, :half], row[:, half:]
        tables.append(
            jnp.concatenate(
                [sin * fine_cos + cos * fine_sin, cos * fine_cos - sin * fine_sin], axis=1
            )
        )
    stream = placed + empty * vector(MASK) + jnp.concatenate(tables, axis=0)
    stream_ref[...] = stream
    empty_ref[...] = empty
    normed, _ = normalize(stream)
    low = (normed * vector(FIRST_GAIN) + vector(FIRST_SHIFT)).astype(jnp.bfloat16)
    normed_ref[...] = low
    query = plain_dot(low, joint_ref[:, :width]) + vector(QUERY_BIAS)
    query_t_ref[...] = (query * QUERY_SCALE).T.astype(jnp.bfloat16)
    keys = plain_dot(low, joint_ref[:, width : 2 * width])
    key_ref[...] = keys.astype(jnp.bfloat16)
    key_t_ref[...] = keys.T.astype(jnp.bfloat16)
    values = plain_dot(low, joint_ref[:, 2 * width :]) + vector(VALUE_BIAS)
    value_ref[...] = values.astype(jnp.bfloat16)
    value_t_ref[...] = values.T.astype(jnp.bfloat16)


def enter(
    latents,
    embed_weight,
    slot_place,
    first_place,
    rows,
    vectors,
    joint_weight,
):
    splits = lax.axis_size("seq")
    width = embed_weight.shape[1]
    capacity = padded(latents.shape[0], 16)
    slots = splits * capacity
    vector_rows = sum(vector.shape[0] for vector in vectors) // width
    block = min(256, rows)
    fine_rows = min(32, block)
    fine = sinusoid(jnp.arange(fine_rows, dtype=jnp.int32), width)
    coarse = sinusoid(first_place + fine_rows * jnp.arange(rows // fine_rows, dtype=jnp.int32), width)
    row_block = pl.BlockSpec((block, width), lambda i: (i, 0))
    lane_block = pl.BlockSpec((width, block), lambda i: (0, i))
    low = jax.ShapeDtypeStruct((rows, width), jnp.bfloat16)
    low_t = jax.ShapeDtypeStruct((width, rows), jnp.bfloat16)
    return pl.pallas_call(
        enter_kernel,
        grid=(rows // block,),
        in_specs=[
            whole(latents.shape),
            whole(embed_weight.shape),
            whole(slot_place.shape),
            pl.BlockSpec((1, block // fine_rows, width), lambda i: (i, 0, 0)),
            whole(fine.shape),
            whole((width, 3 * width)),
        ]
        + [whole(vector.shape) for vector in vectors],
        out_specs=[
            row_block,
            pl.BlockSpec((block, 1), lambda i: (i, 0)),
            row_block,
            lane_block,
            row_block,
            lane_block,
            row_block,
            lane_block,
            whole((vector_rows, width)),
            whole((capacity, latents.shape[1])),
        ],
        out_shape=[
            jax.ShapeDtypeStruct((rows, width), jnp.float32),
            jax.ShapeDtypeStruct((rows, 1), jnp.float32),
            low,
            low_t,
            low,
            low_t,
            low,
            low_t,
            jax.ShapeDtypeStruct((vector_rows, width), jnp.float32),
            jax.ShapeDtypeStruct((capacity, latents.shape[1]), latents.dtype),
        ],
        scratch_shapes=[
            pltpu.VMEM((slots, width), jnp.bfloat16),
            pltpu.VMEM((1, slots), jnp.int32),
            pltpu.SemaphoreType.DMA((2, splits)),
        ],
        compiler_params=pltpu.CompilerParams(
            vmem_limit_bytes=VMEM_LIMIT, collective_id=0, has_side_effects=True
        ),
        cost_estimate=pl.CostEstimate(
            flops=2 * rows * width * (slots + 3 * width),
            bytes_accessed=20 * rows * width,
            transcendentals=0,
        ),
        name="enter",
    )(
        latents,
        embed_weight,
        slot_place,
        coarse.reshape(rows // block, block // fine_rows, width),
        fine,
        joint_weight,
        *vectors,
    )


def attend_kernel(
    key_ref, query_ref, value_ref, mixed_ref, exact_ref, total_ref, raised_ref, scores_ref, norm_ref
):
    span = key_ref.shape[0]
    block = query_ref.shape[1]
    slice_rows = min(256, span)
    slices = span // slice_rows
    query = query_ref[...]
    head_row = lax.broadcasted_iota(jnp.int32, query.shape, 0) // HEAD_DIM
    ones = jnp.ones((16, slice_rows), jnp.bfloat16)

    @pl.when(pl.program_id(1) == 0)
    def _():
        keys = key_ref[...].astype(jnp.float32)
        lane_head = lax.broadcasted_iota(jnp.int32, (128, 128), 0) // HEAD_DIM
        column = lax.broadcasted_iota(jnp.int32, (128, 128), 1)
        pick = (lane_head == column).astype(jnp.float32).astype(jnp.bfloat16)
        norms = plain_dot((keys * keys).astype(jnp.bfloat16), pick)
        norm_ref[...] = jnp.broadcast_to(jnp.max(norms, axis=0, keepdims=True), norm_ref.shape)

    squares = query.astype(jnp.float32)
    squares = squares * squares
    bound = jnp.zeros((1, 1), jnp.float32)
    for head in range(PACK):
        rows = slice(head * HEAD_DIM, (head + 1) * HEAD_DIM)
        longest = jnp.max(
            jnp.sum(squares[rows], axis=0, keepdims=True), axis=1, keepdims=True
        )
        bound = jnp.maximum(bound, longest * norm_ref[0:1, head : head + 1])
    small = bound[0, 0] * 1.02 < SAFE_SCORE**2

    def run(shifted):
        lag = slices if shifted else min(2, slices)
        steps = PACK * slices
        highest, held = {}, {}
        own_query = partial_highest = mixed = None
        for now in range(steps + lag):
            if now < steps:
                head, at = divmod(now, slices)
                part = slice(at * slice_rows, (at + 1) * slice_rows)
                if at == 0:
                    own_query = jnp.where(head_row == head, query, jnp.zeros_like(query))
                    partial_highest = jnp.full((8, block), -jnp.inf, jnp.float32)
                scores = plain_dot(key_ref[part, :], own_query)
                held[now] = scores
                if shifted:
                    partial_highest = jnp.maximum(
                        partial_highest, jnp.max(scores.reshape(slice_rows // 8, 8, block), axis=0)
                    )
                    if at == slices - 1:
                        highest[head] = jnp.max(partial_highest, axis=0, keepdims=True)
            if now >= lag:
                head, at = divmod(now - lag, slices)
                rows = slice(head * HEAD_DIM, (head + 1) * HEAD_DIM)
                part = slice(at * slice_rows, (at + 1) * slice_rows)
                scores = held.pop(now - lag)
                if shifted:
                    scores = scores - highest[head]
                raised = jnp.exp2(scores).astype(jnp.bfloat16)
                raised_ref[head, part, :] = raised
                term = plain_dot(jnp.concatenate([value_ref[rows, part], ones], axis=0), raised)
                mixed = term if at == 0 else mixed + term
                if at == slices - 1:
                    total = mixed[HEAD_DIM : HEAD_DIM + 1]
                    total_ref[0, head : head + 1, :] = total
                    mean = mixed[:HEAD_DIM] / total
                    exact_ref[rows, :] = mean
                    mixed_ref[rows, :] = mean.astype(jnp.bfloat16)

    @pl.when(small)
    def _():
        run(False)

    @pl.when(jnp.logical_not(small))
    def _():
        run(True)


def attend(keys, query_t, value_t):
    width, rows = query_t.shape
    span = keys.shape[0]
    block = min(512, rows)
    groups = width // 128
    lane_block = pl.BlockSpec((128, block), lambda g, i: (g, i))
    return pl.pallas_call(
        attend_kernel,
        grid=(groups, rows // block),
        in_specs=[
            pl.BlockSpec((span, 128), lambda g, i: (0, g)),
            lane_block,
            pl.BlockSpec((128, span), lambda g, i: (g, 0)),
        ],
        out_specs=[
            lane_block,
            lane_block,
            pl.BlockSpec((1, 8, block), lambda g, i: (g, 0, i)),
            pl.BlockSpec((PACK, span, block), lambda g, i: (g, 0, i)),
        ],
        out_shape=[
            jax.ShapeDtypeStruct((width, rows), jnp.bfloat16),
            jax.ShapeDtypeStruct((width, rows), jnp.float32),
            jax.ShapeDtypeStruct((groups, 8, rows), jnp.float32),
            jax.ShapeDtypeStruct((HEADS, span, rows), jnp.bfloat16),
        ],
        scratch_shapes=[
            pltpu.VMEM((span // min(256, span) + 1, min(256, span), block), jnp.float32),
            pltpu.VMEM((8, 128), jnp.float32),
        ],
        compiler_params=pltpu.CompilerParams(vmem_limit_bytes=VMEM_LIMIT),
        cost_estimate=pl.CostEstimate(
            flops=HEADS * span * rows * 512,
            bytes_accessed=2 * HEADS * span * rows,
            transcendentals=HEADS * span * rows,
        ),
        name="attend",
    )(keys, query_t, value_t)


def middle_kernel(
    stream_ref,
    mixed_ref,
    cotangent_ref,
    output_ref,
    expand_ref,
    contract_ref,
    vector_ref,
    decoded_ref,
    grad_middle_ref,
    grad_attended_ref,
    flat_ref,
    small_ref,
    expand_sum,
    contract_sum,
    output_sum,
    small_sum,
):
    width = stream_ref.shape[1]
    chunks = expand_ref.shape[1] // width

    def vector(row):
        return vector_ref[row : row + 1, :]

    @pl.when(pl.program_id(0) == 0)
    def _():
        expand_sum[...] = jnp.zeros_like(expand_sum)
        contract_sum[...] = jnp.zeros_like(contract_sum)
        output_sum[...] = jnp.zeros_like(output_sum)
        small_sum[...] = jnp.zeros_like(small_sum)

    mixed_t = mixed_ref[...]
    cotangent = cotangent_ref[...]
    middle = (
        stream_ref[...]
        + lead_dot(mixed_t, output_ref[...])
        + vector(OUTPUT_BIAS)
    )
    normed, scale = normalize(middle)
    gain = vector(SECOND_GAIN)
    low = (normed * gain + vector(SECOND_SHIFT)).astype(jnp.bfloat16)
    low_t = turned(low)
    output = middle + vector(CONTRACT_BIAS)
    grad_normed = jnp.zeros_like(middle)
    for chunk in range(chunks):
        part = slice(chunk * width, (chunk + 1) * width)
        hidden = plain_dot(low, expand_ref[:, part]) + vector(EXPAND_BIAS + chunk)
        below = 0.5 + 0.5 * lax.erf(hidden * math.sqrt(0.5))
        slope = below + hidden * jnp.exp(-0.5 * hidden * hidden) * (1.0 / math.sqrt(2 * math.pi))
        active = (hidden * below).astype(jnp.bfloat16)
        grad_hidden = (trail_dot(cotangent, contract_ref[part, :]) * slope).astype(jnp.bfloat16)
        output = output + plain_dot(active, contract_ref[part, :])
        grad_normed = grad_normed + trail_dot(grad_hidden, expand_ref[:, part])
        contract_sum[part, :] += lead_dot(active, cotangent)
        expand_sum[part, :] += plain_dot(low_t, grad_hidden)
        small_sum[chunk : chunk + 1, :] += column_sum(grad_hidden)
    decoded_ref[...] = output.astype(jnp.bfloat16)
    grad_middle = cotangent.astype(jnp.float32) + normalize_back(grad_normed * gain, normed, scale)
    grad_middle_ref[...] = grad_middle
    branch = grad_middle.astype(jnp.bfloat16)
    grad_attended_ref[...] = trail_dot(output_ref[...], branch).astype(jnp.bfloat16)
    output_sum[...] += plain_dot(mixed_t, branch)
    small_sum[chunks : chunks + 1, :] += column_sum(cotangent)
    small_sum[chunks + 1 : chunks + 2, :] += column_sum(branch)
    small_sum[chunks + 2 : chunks + 3, :] += column_sum(grad_normed * normed)
    small_sum[chunks + 3 : chunks + 4, :] += column_sum(grad_normed)

    @pl.when(pl.program_id(0) == pl.num_programs(0) - 1)
    def _():
        at = 0
        for total in (expand_sum, contract_sum, output_sum):
            flat_ref[at : at + total.shape[0], :] = total[...].astype(flat_ref.dtype)
            at += total.shape[0]
        if at < flat_ref.shape[0]:
            flat_ref[at:, :] = jnp.zeros((flat_ref.shape[0] - at, width), flat_ref.dtype)
        small_ref[...] = small_sum[...]


def middle_block(
    stream,
    mixed_t,
    cotangent,
    output_weight,
    expand_weight,
    contract_weight,
    vectors,
    flat_rows,
):
    rows, width = stream.shape
    hidden = expand_weight.shape[1]
    block = min(256, rows)
    row_block = pl.BlockSpec((block, width), lambda i: (i, 0))
    lane_block = pl.BlockSpec((width, block), lambda i: (0, i))
    small_rows = hidden // width + 4
    return pl.pallas_call(
        middle_kernel,
        grid=(rows // block,),
        in_specs=[
            row_block,
            lane_block,
            row_block,
            whole((width, width)),
            whole((width, hidden)),
            whole((hidden, width)),
            whole(vectors.shape),
        ],
        out_specs=[
            row_block,
            row_block,
            lane_block,
            whole((flat_rows, width)),
            whole((small_rows, width)),
        ],
        out_shape=[
            jax.ShapeDtypeStruct((rows, width), jnp.bfloat16),
            jax.ShapeDtypeStruct((rows, width), jnp.float32),
            jax.ShapeDtypeStruct((width, rows), jnp.bfloat16),
            jax.ShapeDtypeStruct((flat_rows, width), jnp.bfloat16),
            jax.ShapeDtypeStruct((small_rows, width), jnp.float32),
        ],
        scratch_shapes=[
            pltpu.VMEM((hidden, width), jnp.float32),
            pltpu.VMEM((hidden, width), jnp.float32),
            pltpu.VMEM((width, width), jnp.float32),
            pltpu.VMEM((small_rows, width), jnp.float32),
        ],
        compiler_params=pltpu.CompilerParams(vmem_limit_bytes=VMEM_LIMIT),
        cost_estimate=pl.CostEstimate(
            flops=2 * rows * width * (6 * hidden + 3 * width),
            bytes_accessed=16 * rows * width,
            transcendentals=2 * rows * hidden,
        ),
        name="middle",
    )(
        stream,
        mixed_t,
        cotangent,
        output_weight,
        expand_weight,
        contract_weight,
        vectors,
    )


def attend_back_kernel(
    steps,
    raised_ref,
    total_ref,
    value_ref,
    key_ref,
    query_ref,
    exact_ref,
    grad_ref,
    flat_ref,
    rows_ref,
    latents_ref,
    grad_query_ref,
    grad_key_ref,
    grad_value_ref,
    summed_ref,
    decoded_ref,
    gathered_ref,
    key_sum,
    value_sum,
    exchange_sems,
    exchange_local,
    gather_sems,
    gather_local,
    *sum_refs,
):
    spot = Spot()
    tree = TreeSum(spot, flat_ref, summed_ref, sum_refs, True)
    clips, share = decoded_ref.shape[0], decoded_ref.shape[1]
    mine, part = spot.index % clips, spot.index // clips

    def member(step):
        return (mine + step) % clips

    def exchange(step):
        return send(
            rows_ref.at[span_of(member(step) * share, share)],
            decoded_ref.at[mine],
            exchange_sems,
            step,
            (spot.layer, part * clips + member(step)),
        )

    def own_rows():
        return pltpu.make_async_copy(
            rows_ref.at[span_of(mine * share, share)], decoded_ref.at[mine], exchange_local
        )

    capacity = latents_ref.shape[0]

    def held(core, chip):
        return gathered_ref.at[span_of((chip * 2 + core) * capacity, capacity)]

    def share_own(at, device):
        return send(latents_ref, held(spot.core, spot.chip), gather_sems, at, device)

    def pass_on(at, core, step):
        place = held(core, spot.chip_at(-step))
        return send(place, place, gather_sems, at, spot.sibling())

    def keep_own():
        return pltpu.make_async_copy(latents_ref, held(spot.core, spot.chip), gather_local)

    step_now = pl.program_id(0) * pl.num_programs(1) + pl.program_id(1)

    def at_step(fraction):
        return pl.when(step_now == fraction * steps // 32)

    @at_step(0)
    def _():
        others = spot.tree() + [
            (spot.layer, part * clips + member(step)) for step in range(1, clips)
        ]
        count = spot.meet(others)
        pl.semaphore_wait(pltpu.get_barrier_semaphore(), count)
        tree.start()

    @at_step(4)
    def _():
        tree.near_to_far()

    @at_step(11)
    def _():
        tree.far_to_deep()
        own_rows().start()
        for step in range(1, clips):
            exchange(step).start()
        keep_own().start()
        for step in range(1, spot.half):
            share_own(step, spot.peer(step)).start()
        share_own(0, spot.sibling()).start()

    @at_step(15)
    def _():
        tree.deep_to_layer()

    @at_step(19)
    def _():
        tree.layer_to_part()

    @at_step(24)
    def _():
        for step in range(1, spot.half):
            pass_on(step, spot.core, step).wait_recv()
            pass_on(spot.half + step, spot.core, step).start()

    @at_step(29)
    def _():
        tree.part_to_half()

    @at_step(31)
    def _():
        tree.finish()
        own_rows().wait()
        for step in range(1, clips):
            exchange(step).wait_send()
        for step in range(1, clips):
            send(
                rows_ref.at[span_of(mine * share, share)],
                decoded_ref.at[member(-step)],
                exchange_sems,
                step,
                (spot.layer, part * clips + member(step)),
            ).wait_recv()
        keep_own().wait()
        for step in range(1, spot.half):
            share_own(step, spot.peer(step)).wait_send()
        share_own(0, spot.sibling()).wait_send()
        pass_on(0, 1 - spot.core, 0).wait_recv()
        for step in range(1, spot.half):
            pass_on(spot.half + step, spot.core, step).wait_send()
            pass_on(spot.half + step, 1 - spot.core, step).wait_recv()

    @pl.when(pl.program_id(1) == 0)
    def _():
        key_sum[...] = jnp.zeros_like(key_sum)
        value_sum[...] = jnp.zeros_like(value_sum)

    block = query_ref.shape[1]
    head_row = lax.broadcasted_iota(jnp.int32, (128, block), 0) // HEAD_DIM
    head_col = lax.broadcasted_iota(jnp.int32, (block, 128), 1) // HEAD_DIM
    inverse = 1.0 / total_ref[0, 0:PACK]
    inverse = jnp.concatenate(
        [jnp.broadcast_to(inverse[h : h + 1], (HEAD_DIM, block)) for h in range(PACK)], axis=0
    )
    grad_low = (grad_ref[...].astype(jnp.float32) * inverse).astype(jnp.bfloat16)
    grad = grad_low.astype(jnp.float32)
    inner = grad * exact_ref[...]
    grad_turned = grad.T.astype(jnp.bfloat16)
    query_turned = turned(query_ref[...])
    span = value_ref.shape[0]
    slice_rows = min(256, span)
    units = [(head, at) for head in range(PACK) for at in range(0, span, slice_rows)]
    lag = 2
    weights = {}
    grad_query = None
    for now in range(len(units) + lag):
        if now < len(units):
            head, at = units[now]
            own_grad = jnp.where(head_row == head, grad_low, jnp.zeros_like(grad_low))
            weights[now] = plain_dot(value_ref[at : at + slice_rows, :], own_grad)
        if now >= lag:
            head, at = units[now - lag]
            rows = slice(head * HEAD_DIM, (head + 1) * HEAD_DIM)
            part = slice(at, at + slice_rows)
            row_inner = jnp.sum(inner[rows], axis=0, keepdims=True)
            raised = raised_ref[head, part, :]
            grad_scores = raised * (weights.pop(now - lag) - row_inner).astype(jnp.bfloat16)
            value_sum[part, :] += plain_dot(
                raised, jnp.where(head_col == head, grad_turned, jnp.zeros_like(grad_turned))
            )
            key_sum[part, :] += plain_dot(
                grad_scores, jnp.where(head_col == head, query_turned, jnp.zeros_like(query_turned))
            )
            term = plain_dot(key_ref[rows, part], grad_scores)
            grad_query = term if at == 0 else grad_query + term
            if at + slice_rows == span:
                grad_query_ref[rows, :] = (grad_query * HEAD_DIM ** (-0.5)).astype(jnp.bfloat16)

    @pl.when(pl.program_id(1) == pl.num_programs(1) - 1)
    def _():
        grad_key_ref[...] = (key_sum[...] * (1.0 / LOG2E)).astype(jnp.bfloat16)
        grad_value_ref[...] = value_sum[...].astype(jnp.bfloat16)


def attend_back(raised, total, values, key_t, query_t, exact_t, grad_t, flat, decoded_rows, latents):
    splits, layers = lax.axis_size("seq"), lax.axis_size("dp")
    clips, share, _ = decoded_rows.shape
    width, rows = query_t.shape
    span = values.shape[0]
    block = min(256, rows)
    groups = width // 128
    lane_block = pl.BlockSpec((128, block), lambda g, i: (g, i))
    return pl.pallas_call(
        partial(attend_back_kernel, groups * (rows // block)),
        grid=(groups, rows // block),
        in_specs=[
            pl.BlockSpec((PACK, span, block), lambda g, i: (g, 0, i)),
            pl.BlockSpec((1, 8, block), lambda g, i: (g, 0, i)),
            pl.BlockSpec((span, 128), lambda g, i: (0, g)),
            pl.BlockSpec((128, span), lambda g, i: (g, 0)),
            lane_block,
            lane_block,
            lane_block,
            pl.BlockSpec(memory_space=pl.ANY),
            pl.BlockSpec(memory_space=pl.ANY),
            pl.BlockSpec(memory_space=pl.ANY),
        ],
        out_specs=[
            lane_block,
            pl.BlockSpec((span, 128), lambda g, i: (0, g)),
            pl.BlockSpec((span, 128), lambda g, i: (0, g)),
            pl.BlockSpec(memory_space=pl.ANY),
            pl.BlockSpec(memory_space=pl.ANY),
            pl.BlockSpec(memory_space=pl.ANY),
        ],
        out_shape=[
            jax.ShapeDtypeStruct((width, rows), jnp.bfloat16),
            jax.ShapeDtypeStruct((span, width), jnp.bfloat16),
            jax.ShapeDtypeStruct((span, width), jnp.bfloat16),
            jax.ShapeDtypeStruct(flat.shape, flat.dtype),
            jax.ShapeDtypeStruct(decoded_rows.shape, decoded_rows.dtype),
            jax.ShapeDtypeStruct((splits * latents.shape[0], latents.shape[1]), latents.dtype),
        ],
        scratch_shapes=[
            pltpu.VMEM((span, 128), jnp.float32),
            pltpu.VMEM((span, 128), jnp.float32),
            pltpu.SemaphoreType.DMA((2, clips)),
            pltpu.SemaphoreType.DMA,
            pltpu.SemaphoreType.DMA((2, splits)),
            pltpu.SemaphoreType.DMA,
        ]
        + TreeSum.scratch(flat.shape[0], flat.shape[1], True, splits, layers),
        compiler_params=pltpu.CompilerParams(
            vmem_limit_bytes=VMEM_LIMIT, collective_id=1, has_side_effects=True
        ),
        cost_estimate=pl.CostEstimate(
            flops=HEADS * span * rows * 1024,
            bytes_accessed=2 * HEADS * span * rows,
            transcendentals=0,
        ),
        name="attend_back",
    )(raised, total, values, key_t, query_t, exact_t, grad_t, flat, decoded_rows.reshape(clips * share, width), latents)


def leave_kernel(
    grad_query_ref,
    grad_key_ref,
    grad_value_ref,
    stream_ref,
    empty_ref,
    low_ref,
    grad_middle_ref,
    vector_ref,
    joint_ref,
    slot_ref,
    latents_ref,
    embed_ref,
    early_ref,
    latent_grad_ref,
    joint_total_ref,
    embed_total_ref,
    joint_sum,
    small_sum,
    grad_all,
    joint_flat,
    embed_flat,
    back_all,
    near_in,
    far_out,
    far_in,
    latents_all,
    sems,
    local,
    *sum_refs,
):
    block, width = stream_ref.shape
    step_now = pl.program_id(0)
    spot = Spot()
    capacity = back_all.shape[0] // spot.splits
    others = spot.tree()
    blocks = pl.num_programs(0) // 2
    count = len(sum_refs) // 2
    joint_tree = TreeSum(spot, joint_flat, joint_total_ref, sum_refs[:count], True)
    embed_tree = TreeSum(spot, embed_flat, embed_total_ref, sum_refs[count:], False)

    def load_latents():
        return pltpu.make_async_copy(latents_ref, latents_all, local)

    @pl.when(step_now == 0)
    def _():
        spot.meet(others)
        load_latents().start()
        joint_sum[...] = jnp.zeros_like(joint_sum)
        small_sum[...] = jnp.zeros_like(small_sum)

    @pl.when(step_now < blocks)
    def _():
        low_t = turned(low_ref[...])
        sides = [turned(grad_query_ref[...]), grad_key_ref[...], grad_value_ref[...]]
        for at, side in enumerate(sides):
            joint_sum[at * width : (at + 1) * width, :] += plain_dot(low_t, side)
        small_sum[3:4, :] += column_sum(sides[0])
        small_sum[4:5, :] += column_sum(sides[2])

    @pl.when(step_now == blocks - 1)
    def _():
        rows = joint_sum.shape[0]
        joint_flat[:rows, :] = joint_sum[...].astype(jnp.bfloat16)
        if joint_flat.shape[0] > rows:
            joint_flat[rows:, :] = jnp.zeros(
                (joint_flat.shape[0] - rows, width), jnp.bfloat16
            )
        pl.semaphore_wait(pltpu.get_barrier_semaphore(), len(others))
        joint_tree.start()

    @pl.when(step_now == blocks + blocks // 4)
    def _():
        joint_tree.near_to_far()

    @pl.when(step_now >= blocks)
    def _():
        normed, scale = normalize(stream_ref[...])
        sides = [turned(grad_query_ref[...]), grad_key_ref[...], grad_value_ref[...]]
        grad_normed = jnp.zeros_like(normed)
        for at, side in enumerate(sides):
            grad_normed = grad_normed + trail_dot(
                side, joint_ref[:, at * width : (at + 1) * width]
            )
        grad_stream = grad_middle_ref[...] + normalize_back(
            grad_normed * vector_ref[FIRST_GAIN : FIRST_GAIN + 1, :], normed, scale
        )
        grad_all[pl.ds(pl.multiple_of((step_now - blocks) * block, block), block), :] = (
            grad_stream.astype(jnp.bfloat16)
        )
        small_sum[0:1, :] += column_sum(empty_ref[...] * grad_stream)
        small_sum[1:2, :] += column_sum(grad_normed * normed)
        small_sum[2:3, :] += column_sum(grad_normed)

    @pl.when(step_now == pl.num_programs(0) - 1)
    def _():
        place = lax.broadcasted_iota(jnp.int32, (1, grad_all.shape[0]), 1)

        def gathered(owner):
            slots = slot_ref[pl.ds(owner, 1), :].astype(jnp.float32)
            slots = jnp.broadcast_to(slots, (8, slots.shape[1])).T[:capacity, 0:1]
            takes = (slots.astype(jnp.int32) == place).astype(jnp.float32).astype(jnp.bfloat16)
            return plain_dot(takes, grad_all[...])

        def rows_of(owner):
            return span_of(owner * capacity, capacity)

        def part(at):
            return pl.ds(at * capacity, capacity)

        def near_copy(step):
            owner = spot.chip_at(step) * 2 + 1 - spot.core
            return send(
                back_all.at[rows_of(owner)], near_in.at[part(step)], sems, step, spot.sibling()
            )

        def far_copy(step):
            return send(
                far_out.at[part(step - 1)],
                far_in.at[part(step - 1)],
                sems,
                spot.half + step,
                spot.peer(step),
            )

        for step in list(range(1, spot.half)) + [0]:
            owner = spot.chip_at(step) * 2 + 1 - spot.core
            back_all[rows_of(owner), :] = gathered(owner).astype(jnp.bfloat16)
            near_copy(step).start()
            owner = spot.chip_at(step) * 2 + spot.core
            own = gathered(owner)
            back_all[rows_of(owner), :] = own.astype(jnp.bfloat16)
            near_copy(step).wait()
            own = own + near_in[part(step), :].astype(jnp.float32)
            if step > 0:
                far_out[part(step - 1), :] = own.astype(jnp.bfloat16)
                far_copy(step).start()
            if step == 1:
                joint_tree.far_to_deep()
        load_latents().wait()
        embed_rows = embed_ref.shape[0]
        embed_flat[:embed_rows, :] = lead_dot(latents_all[...], back_all[...]).astype(jnp.bfloat16)
        small_sum[5:6, :] = column_sum(back_all[...])
        small = jnp.concatenate([early_ref[...], small_sum[...]], axis=0)
        rest = embed_flat.shape[0] - embed_rows - small.shape[0]
        if rest:
            small = jnp.concatenate([small, jnp.zeros((rest, width), jnp.float32)], axis=0)
        embed_flat[embed_rows:, :] = small.astype(jnp.bfloat16)
        embed_tree.start()
        joint_tree.deep_to_layer()
        embed_tree.near_to_far()
        joint_tree.layer_to_part()
        embed_tree.far_to_deep()
        for step in range(1, spot.half):
            far_copy(step).wait()
            own = own + far_in[part(step - 1), :].astype(jnp.float32)
        grad_embedded = own[: latent_grad_ref.shape[0]].astype(jnp.bfloat16)
        latent_grad_ref[...] = trail_dot(grad_embedded, embed_ref[...]).astype(jnp.bfloat16)
        joint_tree.part_to_half()
        embed_tree.deep_to_layer()
        joint_tree.finish()
        embed_tree.part_to_half()
        embed_tree.finish()


def leave(
    grad_query_t,
    grad_key,
    grad_value,
    stream,
    empty,
    low,
    grad_middle,
    vectors,
    joint_weight,
    slot_place,
    latents_all,
    embed_weight,
    early_small,
    own_rows,
):
    splits, layers = lax.axis_size("seq"), lax.axis_size("dp")
    rows, width = stream.shape
    slots = latents_all.shape[0]
    latent_shape = (own_rows, latents_all.shape[1])
    capacity = slots // splits
    half = splits // 2
    block = min(256, rows)
    blocks = rows // block
    row_block = pl.BlockSpec((block, width), lambda i: (i % blocks, 0))
    first_block = pl.BlockSpec((block, width), lambda i: (jnp.minimum(i, blocks - 1), 0))
    later_block = pl.BlockSpec((block, width), lambda i: (jnp.maximum(i - blocks, 0), 0))
    lane_block = pl.BlockSpec((width, block), lambda i: (0, i % blocks))
    joint_rows = padded(3 * width, splits * layers * 16)
    embed_rows = padded(embed_weight.shape[0] + early_small.shape[0] + 8, splits * 16)
    return pl.pallas_call(
        leave_kernel,
        grid=(2 * blocks,),
        in_specs=[
            lane_block,
            row_block,
            row_block,
            later_block,
            pl.BlockSpec((block, 1), lambda i: (jnp.maximum(i - blocks, 0), 0)),
            first_block,
            later_block,
            whole(vectors.shape),
            whole((width, 3 * width)),
            whole(slot_place.shape),
            pl.BlockSpec(memory_space=pl.ANY),
            whole(embed_weight.shape),
            whole(early_small.shape),
        ],
        out_specs=[
            whole(latent_shape),
            pl.BlockSpec(memory_space=pl.ANY),
            pl.BlockSpec(memory_space=pl.ANY),
        ],
        out_shape=[
            jax.ShapeDtypeStruct(latent_shape, jnp.bfloat16),
            jax.ShapeDtypeStruct((joint_rows, width), jnp.bfloat16),
            jax.ShapeDtypeStruct((embed_rows, width), jnp.bfloat16),
        ],
        scratch_shapes=[
            pltpu.VMEM((3 * width, width), jnp.float32),
            pltpu.VMEM((8, width), jnp.float32),
            pltpu.VMEM((rows, width), jnp.bfloat16),
            pltpu.VMEM((joint_rows, width), jnp.bfloat16),
            pltpu.VMEM((embed_rows, width), jnp.bfloat16),
            pltpu.VMEM((slots, width), jnp.bfloat16),
            pltpu.VMEM((half * capacity, width), jnp.bfloat16),
            pltpu.VMEM((max(half - 1, 1) * capacity, width), jnp.bfloat16),
            pltpu.VMEM((max(half - 1, 1) * capacity, width), jnp.bfloat16),
            pltpu.VMEM(latents_all.shape, latents_all.dtype),
            pltpu.SemaphoreType.DMA((2, splits)),
            pltpu.SemaphoreType.DMA,
        ]
        + TreeSum.scratch(joint_rows, width, True, splits, layers)
        + TreeSum.scratch(embed_rows, width, False, splits, layers),
        compiler_params=pltpu.CompilerParams(
            vmem_limit_bytes=VMEM_LIMIT, collective_id=2, has_side_effects=True
        ),
        cost_estimate=pl.CostEstimate(
            flops=2 * rows * width * (slots + 6 * width),
            bytes_accessed=20 * rows * width,
            transcendentals=0,
        ),
        name="leave",
    )(
        grad_query_t,
        grad_key,
        grad_value,
        stream,
        empty,
        low,
        grad_middle,
        vectors,
        joint_weight,
        slot_place,
        latents_all,
        embed_weight,
        early_small,
    )


def finish_kernel(
    expand_ref,
    contract_ref,
    output_ref,
    joint_ref,
    embed_ref,
    small_ref,
    expand_out,
    contract_out,
    output_out,
    joint_out,
    embed_out,
    *small_outs,
):
    for source, target in (
        (expand_ref, expand_out),
        (contract_ref, contract_out),
        (output_ref, output_out),
        (joint_ref, joint_out),
        (embed_ref, embed_out),
    ):
        target[...] = source[...].astype(jnp.float32)
    small = small_ref[...].astype(jnp.float32)
    width = small.shape[1]
    at = 0
    for target in small_outs:
        for start in range(0, target.shape[0], width):
            target[start : start + width] = small[at]
            at += 1


def finish(early_sum, joint_sum, embed_sum, hidden, embed_rows, small_sizes):
    width = early_sum.shape[1]
    chunks = hidden // width
    square = (width, width)
    embed_block = (embed_rows // chunks, width)
    sides = 3
    return pl.pallas_call(
        finish_kernel,
        grid=(chunks,),
        in_specs=[
            pl.BlockSpec(square, lambda i: (i, 0)),
            pl.BlockSpec(square, lambda i: (chunks + i, 0)),
            pl.BlockSpec(square, lambda i: (2 * chunks, 0)),
            pl.BlockSpec(square, lambda i: (jnp.minimum(i, sides - 1), 0)),
            pl.BlockSpec(embed_block, lambda i: (i, 0)),
            pl.BlockSpec((16, width), lambda i: (embed_rows // 16, 0)),
        ],
        out_specs=[
            pl.BlockSpec(square, lambda i: (0, i)),
            pl.BlockSpec(square, lambda i: (i, 0)),
            pl.BlockSpec(square, lambda i: (0, 0)),
            pl.BlockSpec(square, lambda i: (0, jnp.minimum(i, sides - 1))),
            pl.BlockSpec(embed_block, lambda i: (i, 0)),
        ]
        + [whole((size,)) for size in small_sizes],
        out_shape=[
            jax.ShapeDtypeStruct((width, hidden), jnp.float32),
            jax.ShapeDtypeStruct((hidden, width), jnp.float32),
            jax.ShapeDtypeStruct(square, jnp.float32),
            jax.ShapeDtypeStruct((width, sides * width), jnp.float32),
            jax.ShapeDtypeStruct((embed_rows, width), jnp.float32),
        ]
        + [jax.ShapeDtypeStruct((size,), jnp.float32) for size in small_sizes],
        compiler_params=pltpu.CompilerParams(vmem_limit_bytes=VMEM_LIMIT),
        cost_estimate=pl.CostEstimate(
            flops=0, bytes_accessed=12 * width * (hidden + width), transcendentals=0
        ),
        name="finish",
    )(early_sum, early_sum, early_sum, joint_sum, embed_sum, embed_sum)


def body(
    latents,
    clip_ids,
    restore,
    counts,
    embed_weight,
    embed_bias,
    mask_token,
    first_gain,
    first_shift,
    joint_weight,
    query_bias,
    value_bias,
    output_weight,
    output_bias,
    second_gain,
    second_shift,
    expand_weight,
    expand_bias,
    contract_weight,
    contract_bias,
    cotangent,
):
    splits = lax.axis_size("seq")
    seq_index = lax.axis_index("seq")
    capacity = latents.shape[0]
    clip_count, clip_share, model_width = cotangent.shape
    sharers = splits // clip_count
    rows = clip_count * clip_share
    own_clip = seq_index % clip_count
    first_place = (seq_index // clip_count) * rows
    exchange_groups = [[s * clip_count + c for c in range(clip_count)] for s in range(sharers)]
    clip_groups = [[s * clip_count + c for s in range(sharers)] for c in range(clip_count)]

    def to_clips(blocks):
        return lax.all_to_all(
            blocks,
            "seq",
            split_axis=0,
            concat_axis=0,
            tiled=True,
            axis_index_groups=exchange_groups if sharers > 1 else None,
        )

    live = jnp.arange(capacity, dtype=jnp.int32)[None, :] < counts[:, None]
    mine = live & ((clip_ids % clip_count).reshape(splits, capacity) == own_clip)
    slot_place = jnp.where(mine, restore.reshape(splits, capacity) - first_place, -1)
    slot_place = jnp.pad(
        slot_place, ((0, 0), (0, padded(capacity, 128) - capacity)), constant_values=-1
    )
    (
        stream,
        empty,
        first_low,
        query_t,
        keys,
        key_t,
        values,
        value_t,
        vectors,
        latents,
    ) = enter(
        latents,
        embed_weight,
        slot_place,
        first_place,
        rows,
        [
            embed_bias,
            mask_token,
            first_gain,
            first_shift,
            query_bias,
            value_bias,
            output_bias,
            second_gain,
            second_shift,
            contract_bias,
            expand_bias,
        ],
        joint_weight,
    )
    cotangent, keys = lax.optimization_barrier((cotangent, keys))
    grad_output = to_clips(cotangent).reshape(rows, model_width)
    if sharers > 1:
        keys = lax.all_gather(keys, "seq", axis=0, tiled=True, axis_index_groups=clip_groups)
        values = lax.all_gather(values, "seq", axis=0, tiled=True, axis_index_groups=clip_groups)
        key_t, value_t = keys.T, values.T
    mixed_t, exact_t, total, raised = attend(keys, query_t, value_t)
    (
        decoded_rows,
        grad_middle,
        grad_attended_t,
        early_flat,
        early_small,
    ) = middle_block(
        stream,
        mixed_t,
        grad_output,
        output_weight,
        expand_weight,
        contract_weight,
        vectors,
        padded(2 * expand_weight.shape[1] + model_width, splits * lax.axis_size("dp") * 16),
    )
    grad_query_t, grad_key, grad_value, early_sum, decoded, latents_all = attend_back(
        raised,
        total,
        values,
        key_t,
        query_t,
        exact_t,
        grad_attended_t,
        early_flat,
        decoded_rows.reshape(clip_count, clip_share, model_width),
        latents,
    )
    if sharers > 1:
        grad_key, grad_value = (
            lax.psum_scatter(
                side, "seq", scatter_dimension=0, tiled=True, axis_index_groups=clip_groups
            )
            for side in (grad_key, grad_value)
        )
    latent_grad, joint_sum, embed_sum = leave(
        grad_query_t,
        grad_key,
        grad_value,
        stream,
        empty,
        first_low,
        grad_middle,
        vectors,
        joint_weight,
        slot_place,
        latents_all,
        embed_weight,
        early_small,
        capacity,
    )
    hidden_width = expand_weight.shape[1]
    (
        grad_expand,
        grad_contract,
        grad_output_weight,
        grad_joint_weight,
        grad_embed_weight,
        grad_expand_bias,
        grad_contract_bias,
        grad_output_bias,
        grad_second_gain,
        grad_second_shift,
        grad_mask,
        grad_first_gain,
        grad_first_shift,
        grad_query_bias,
        grad_value_bias,
        grad_embed_bias,
    ) = finish(
        early_sum,
        joint_sum,
        embed_sum,
        hidden_width,
        embed_weight.shape[0],
        [hidden_width] + [model_width] * 10,
    )
    return (
        decoded,
        latent_grad,
        grad_embed_weight,
        grad_embed_bias,
        grad_mask,
        grad_first_gain,
        grad_first_shift,
        grad_joint_weight,
        grad_query_bias,
        grad_value_bias,
        grad_output_weight,
        grad_output_bias,
        grad_second_gain,
        grad_second_shift,
        grad_expand,
        grad_expand_bias,
        grad_contract,
        grad_contract_bias,
    )


def solution(mesh):
    placed = (
        (P(("dp", "seq"), None),) + (P("dp"),) * 3 + (P(),) * 16 + (P("dp", "seq", None),)
    )
    return jax.shard_map(
        body,
        mesh=mesh,
        in_specs=placed,
        out_specs=(P("dp", "seq", None), P(("dp", "seq"), None)) + (P(),) * 16,
        check_vma=False,
    )
```

```python
from functools import partial
import math

import jax
import jax.numpy as jnp
from jax import lax
from jax.experimental import pallas as pl
from jax.experimental.pallas import tpu as pltpu
from jax.sharding import PartitionSpec as P

HEADS = 16
HEAD_DIM = 32
PACK = 128 // HEAD_DIM
VMEM_LIMIT = 56 * 1024 * 1024
SAFE_SCORE = 80.0
MESH = pl.DeviceIdType.MESH
LOG2E = math.log2(math.e)
QUERY_SCALE = LOG2E * HEAD_DIM ** (-0.5)


epsilon = 1e-06


EMBED_BIAS, MASK, FIRST_GAIN, FIRST_SHIFT, QUERY_BIAS, VALUE_BIAS = range(6)
OUTPUT_BIAS, SECOND_GAIN, SECOND_SHIFT, CONTRACT_BIAS, EXPAND_BIAS = range(6, 11)


def whole(shape):
    return pl.BlockSpec(shape, lambda *_: (0,) * len(shape))


def turned(values):
    return values.astype(jnp.float32).T.astype(values.dtype)


def sinusoid(places, table_width):
    half_width = table_width // 2
    frequency = jnp.exp(-math.log(10000.0) * jnp.arange(half_width, dtype=jnp.float32) / half_width)
    angles = places.astype(jnp.float32)[:, None] * frequency[None, :]
    return jnp.concatenate([jnp.sin(angles), jnp.cos(angles)], axis=1)


def plain_dot(left, right):
    return jnp.dot(left, right, preferred_element_type=jnp.float32)


def lead_dot(left, right):
    return lax.dot_general(
        left, right, (((0,), (0,)), ((), ())), preferred_element_type=jnp.float32
    )


def trail_dot(left, right):
    return lax.dot_general(
        left, right, (((1,), (1,)), ((), ())), preferred_element_type=jnp.float32
    )


def column_sum(values):
    return jnp.sum(values.astype(jnp.float32), axis=0, keepdims=True)


def row_mean(values):
    return jnp.mean(values, axis=-1, keepdims=True)


def normalize(values):
    center = values - row_mean(values)
    scale = lax.rsqrt(row_mean(center * center) + epsilon)
    return center * scale, scale


def normalize_back(grad, normed, scale):
    return scale * (grad - row_mean(grad) - normed * row_mean(grad * normed))


class Spot:
    def __init__(self):
        self.layers, self.splits = lax.axis_size("dp"), lax.axis_size("seq")
        self.half = self.splits // 2
        self.layer, self.index = lax.axis_index("dp"), lax.axis_index("seq")
        self.core, self.chip = self.index % 2, self.index // 2

    def sibling(self):
        return (self.layer, self.chip * 2 + (1 - self.core))

    def chip_at(self, step):
        return (self.chip + step) % self.half

    def layer_at(self, step):
        return (self.layer + step) % self.layers

    def peer(self, step):
        return (self.layer, self.chip_at(step) * 2 + self.core)

    def above(self, step):
        return (self.layer_at(step), self.index)

    def routes(self):
        if self.half != 4:
            steps = range(1, self.half)
            return (
                [self.chip_at(-step) for step in steps],
                [self.peer(step) for step in steps],
                [self.chip for _ in steps],
            )
        across, up = self.chip % 2, self.chip // 2
        beside = up * 2 + 1 - across
        above = (1 - up) * 2 + across
        first = beside * (1 - self.core) + above * self.core
        second = above * (1 - self.core) + beside * self.core
        return (
            [first, second, 3 - self.chip],
            [(self.layer, chip * 2 + self.core) for chip in (first, second, second)],
            [self.chip, self.chip, first],
        )

    def passed_on(self, at):
        return self.half == 4 and at == 2

    def sibling_turn(self, at):
        return [1, 0, 2][at] if self.half == 4 else at

    def meet(self, others):
        barrier = pltpu.get_barrier_semaphore()
        for other in others:
            pl.semaphore_signal(barrier, inc=1, device_id=other, device_id_type=MESH)
        return len(others)

    def tree(self, layers=True):
        others = [self.sibling()] + [self.peer(step) for step in range(1, self.half)]
        if layers:
            others += [self.above(step) for step in range(1, self.layers)]
        return others


def padded(rows, unit):
    return -(-rows // unit) * unit


def span_of(start, size):
    return pl.ds(pl.multiple_of(start, 16), size)


def send(source, target, sems, at, device):
    return pltpu.make_async_remote_copy(
        src_ref=source,
        dst_ref=target,
        send_sem=sems.at[0, at],
        recv_sem=sems.at[1, at],
        device_id=device,
        device_id_type=MESH,
    )


class TreeSum:
    def __init__(self, spot, source, result, refs, scatter):
        (
            self.near,
            self.near_sum,
            self.far,
            self.far_sum,
            self.deep,
            self.done,
            self.sems,
            self.local,
        ) = refs
        self.spot, self.source, self.result, self.scatter = spot, source, result, scatter
        self.part = self.far_sum.shape[0]
        self.piece = self.done.shape[0]

    @staticmethod
    def scratch(rows, width, scatter, splits, layers):
        half = splits // 2
        part = rows // splits
        piece = part // layers if scatter else part
        low = jnp.bfloat16
        return [
            pltpu.VMEM((half * part, width), low),
            pltpu.VMEM((half * part, width), low),
            pltpu.VMEM((max(half - 1, 1) * part, width), low),
            pltpu.VMEM((part, width), low),
            pltpu.VMEM((layers * piece, width), low),
            pltpu.VMEM((piece, width), low),
            pltpu.SemaphoreType.DMA((2, 2 + 2 * half + 2 * layers)),
            pltpu.SemaphoreType.DMA((2,)),
        ]

    def near_copy(self):
        spot = self.spot
        rows = spot.half * self.part
        return send(
            self.source.at[span_of((1 - spot.core) * rows, rows)],
            self.near,
            self.sems,
            0,
            spot.sibling(),
        )

    def own_copy(self):
        rows = self.spot.half * self.part
        return pltpu.make_async_copy(
            self.source.at[span_of(self.spot.core * rows, rows)], self.near_sum, self.local.at[0]
        )

    def far_copy(self, step):
        return send(
            self.near_sum.at[span_of(self.spot.chip_at(step) * self.part, self.part)],
            self.far.at[span_of((step - 1) * self.part, self.part)],
            self.sems,
            1 + step,
            self.spot.peer(step),
        )

    def deep_copy(self, step):
        spot = self.spot
        if self.scatter:
            source = self.far_sum.at[span_of(spot.layer_at(step) * self.piece, self.piece)]
        else:
            source = self.far_sum
        return send(
            source,
            self.deep.at[span_of(spot.layer * self.piece, self.piece)],
            self.sems,
            1 + spot.half + step,
            spot.above(step),
        )

    def place(self, core, chip, layer=None):
        spot = self.spot
        start = (core * spot.half + chip) * self.part
        if layer is None:
            return span_of(start, self.part)
        return span_of(start + layer * self.piece, self.piece)

    def done_copy(self):
        spot = self.spot
        layer = spot.layer if self.scatter else None
        return pltpu.make_async_copy(
            self.done, self.result.at[self.place(spot.core, spot.chip, layer)], self.local.at[1]
        )

    def layer_copy(self, step, arriving):
        spot = self.spot
        layer = spot.layer_at(-step) if arriving else spot.layer
        return send(
            self.done,
            self.result.at[self.place(spot.core, spot.chip, layer)],
            self.sems,
            1 + spot.half + spot.layers + step,
            spot.above(step),
        )

    def part_copy(self, step, arriving):
        spot = self.spot
        place = self.place(spot.core, spot.chip_at(-step) if arriving else spot.chip)
        return send(
            self.result.at[place] if self.scatter else self.done,
            self.result.at[place],
            self.sems,
            1 + spot.half + 2 * spot.layers + step,
            spot.peer(step),
        )

    def half_copy(self, arriving):
        spot = self.spot
        rows = spot.half * self.part
        core = 1 - spot.core if arriving else spot.core
        place = span_of(core * rows, rows)
        return send(
            self.result.at[place], self.result.at[place], self.sems, 1, spot.sibling()
        )

    def start(self):
        self.own_copy().start()
        self.near_copy().start()

    def near_to_far(self):
        self.own_copy().wait()
        self.near_copy().wait()
        unit = self.part
        while unit > 160 and unit % 32 == 0:
            unit //= 2

        def add(at, _):
            rows = span_of(at * unit, unit)
            self.near_sum[rows, :] = (
                self.near_sum[rows, :].astype(jnp.float32) + self.near[rows, :].astype(jnp.float32)
            ).astype(jnp.bfloat16)
            return 0

        lax.fori_loop(0, self.spot.half * (self.part // unit), add, 0)
        for step in range(1, self.spot.half):
            self.far_copy(step).start()

    def far_to_deep(self):
        spot = self.spot
        for step in range(1, spot.half):
            self.far_copy(step).wait()
        unit = self.part
        while unit > 160 and unit % 32 == 0:
            unit //= 2

        def add(at, _):
            start = at * unit
            total = self.near_sum[span_of(spot.chip * self.part + start, unit), :].astype(
                jnp.float32
            )
            for step in range(1, spot.half):
                total = total + self.far[span_of((step - 1) * self.part + start, unit), :].astype(
                    jnp.float32
                )
            self.far_sum[span_of(start, unit), :] = total.astype(jnp.bfloat16)
            return 0

        lax.fori_loop(0, self.part // unit, add, 0)
        for step in range(1, spot.layers):
            self.deep_copy(step).start()
        own = self.far_sum[...]
        if self.scatter:
            own = self.far_sum[span_of(spot.layer * self.piece, self.piece), :]
        self.deep[span_of(spot.layer * self.piece, self.piece), :] = own

    def deep_to_layer(self):
        spot = self.spot
        for step in range(1, spot.layers):
            self.deep_copy(step).wait_send()
        for step in range(1, spot.layers):
            send(
                self.done,
                self.deep.at[span_of(spot.layer_at(-step) * self.piece, self.piece)],
                self.sems,
                1 + spot.half + step,
                spot.above(step),
            ).wait_recv()
        total = self.deep[: self.piece, :].astype(jnp.float32)
        for layer in range(1, spot.layers):
            total = total + self.deep[layer * self.piece : (layer + 1) * self.piece, :].astype(
                jnp.float32
            )
        self.done[...] = total.astype(jnp.bfloat16)
        self.done_copy().start()
        if self.scatter:
            for step in range(1, spot.layers):
                self.layer_copy(step, False).start()
        else:
            for step in range(1, spot.half):
                self.part_copy(step, False).start()

    def layer_to_part(self):
        spot = self.spot
        if not self.scatter:
            return
        self.done_copy().wait()
        for step in range(1, spot.layers):
            self.layer_copy(step, False).wait_send()
        for step in range(1, spot.layers):
            self.layer_copy(step, True).wait_recv()
        for step in range(1, spot.half):
            self.part_copy(step, False).start()

    def part_to_half(self):
        spot = self.spot
        if not self.scatter:
            self.done_copy().wait()
        for step in range(1, spot.half):
            self.part_copy(step, False).wait_send()
        for step in range(1, spot.half):
            self.part_copy(step, True).wait_recv()
        self.half_copy(False).start()

    def finish(self):
        self.half_copy(False).wait_send()
        self.half_copy(True).wait_recv()


def enter_kernel(
    latents_ref,
    embed_ref,
    slot_ref,
    coarse_ref,
    fine_ref,
    joint_ref,
    *refs,
):
    (
        stream_ref,
        empty_ref,
        normed_ref,
        query_t_ref,
        key_ref,
        key_t_ref,
        value_ref,
        value_t_ref,
        vector_ref,
        latents_out_ref,
        embedded_ref,
        slot_row,
        sems,
    ) = refs[-13:]
    vector_refs = refs[:-13]
    block, width = stream_ref.shape
    spot = Spot()
    capacity = embedded_ref.shape[0] // spot.splits

    def vector(row):
        return vector_ref[row : row + 1, :]

    @pl.when(pl.program_id(0) == 0)
    def _():
        count = spot.meet(spot.tree(False))
        at = 0
        for source in vector_refs:
            for start in range(0, source.shape[0], width):
                values = source[start : start + width].astype(jnp.float32)
                vector_ref[at : at + 1, :] = values.reshape(1, width)
                at += 1
        latents = latents_ref[...]
        rest = capacity - latents.shape[0]
        if rest:
            latents = jnp.concatenate(
                [latents.astype(jnp.float32), jnp.zeros((rest, latents.shape[1]), jnp.float32)],
                axis=0,
            ).astype(jnp.bfloat16)
        latents_out_ref[...] = latents
        embedded = plain_dot(latents, embed_ref[...]) + vector(EMBED_BIAS)

        def held(core, chip):
            return embedded_ref.at[span_of((chip * 2 + core) * capacity, capacity)]

        def share(at, core, chip, device):
            return send(held(core, chip), held(core, chip), sems, at, device)

        embedded_ref[span_of(spot.index * capacity, capacity), :] = embedded.astype(jnp.bfloat16)
        pl.semaphore_wait(pltpu.get_barrier_semaphore(), count)
        sources, targets, sent = spot.routes()

        def far(at):
            return share(1 + at, spot.core, sent[at], targets[at])

        def near(at, core):
            return share(spot.half + 1 + at, core, sources[at], spot.sibling())

        turns = range(len(targets))
        for at in turns:
            if not spot.passed_on(at):
                far(at).start()
        share(0, spot.core, spot.chip, spot.sibling()).start()
        for source in range(spot.splits):
            slot_row[:, source * capacity : (source + 1) * capacity] = slot_ref[
                source : source + 1, :capacity
            ]
        for at in turns:
            share(1 + at, spot.core, sources[at], targets[at]).wait_recv()
            if at == 0 and spot.passed_on(2):
                far(2).start()
            near(at, spot.core).start()
        for at in turns:
            far(at).wait_send()
        share(0, spot.core, spot.chip, spot.sibling()).wait_send()
        share(0, 1 - spot.core, spot.chip, spot.sibling()).wait_recv()
        for at in turns:
            near(at, spot.core).wait_send()
            share(
                spot.half + 1 + at, 1 - spot.core, sources[spot.sibling_turn(at)], spot.sibling()
            ).wait_recv()

    place = lax.broadcasted_iota(jnp.int32, (block, 1), 0) + pl.program_id(0) * block
    fills = (place == slot_row[...]).astype(jnp.float32)
    empty = 1.0 - jnp.sum(fills, axis=1, keepdims=True)
    placed = plain_dot(fills.astype(jnp.bfloat16), embedded_ref[...])
    fine_rows = fine_ref.shape[0]
    half = width // 2
    fine_sin, fine_cos = fine_ref[:, :half], fine_ref[:, half:]
    tables = []
    for at in range(block // fine_rows):
        row = coarse_ref[0, at : at + 1, :]
        sin, cos = row[:, :half], row[:, half:]
        tables.append(
            jnp.concatenate(
                [sin * fine_cos + cos * fine_sin, cos * fine_cos - sin * fine_sin], axis=1
            )
        )
    stream = placed + empty * vector(MASK) + jnp.concatenate(tables, axis=0)
    stream_ref[...] = stream
    empty_ref[...] = empty
    normed, _ = normalize(stream)
    low = (normed * vector(FIRST_GAIN) + vector(FIRST_SHIFT)).astype(jnp.bfloat16)
    normed_ref[...] = low
    query = plain_dot(low, joint_ref[:, :width]) + vector(QUERY_BIAS)
    query_t_ref[...] = (query * QUERY_SCALE).T.astype(jnp.bfloat16)
    keys = plain_dot(low, joint_ref[:, width : 2 * width])
    key_ref[...] = keys.astype(jnp.bfloat16)
    key_t_ref[...] = keys.T.astype(jnp.bfloat16)
    values = plain_dot(low, joint_ref[:, 2 * width :]) + vector(VALUE_BIAS)
    value_ref[...] = values.astype(jnp.bfloat16)
    value_t_ref[...] = values.T.astype(jnp.bfloat16)


def enter(
    latents,
    embed_weight,
    slot_place,
    first_place,
    rows,
    vectors,
    joint_weight,
):
    splits = lax.axis_size("seq")
    width = embed_weight.shape[1]
    capacity = padded(latents.shape[0], 16)
    slots = splits * capacity
    vector_rows = sum(vector.shape[0] for vector in vectors) // width
    block = min(512, rows)
    fine_rows = min(32, block)
    fine = sinusoid(jnp.arange(fine_rows, dtype=jnp.int32), width)
    coarse = sinusoid(first_place + fine_rows * jnp.arange(rows // fine_rows, dtype=jnp.int32), width)
    row_block = pl.BlockSpec((block, width), lambda i: (i, 0))
    lane_block = pl.BlockSpec((width, block), lambda i: (0, i))
    low = jax.ShapeDtypeStruct((rows, width), jnp.bfloat16)
    low_t = jax.ShapeDtypeStruct((width, rows), jnp.bfloat16)
    return pl.pallas_call(
        enter_kernel,
        grid=(rows // block,),
        in_specs=[
            whole(latents.shape),
            whole(embed_weight.shape),
            whole(slot_place.shape),
            pl.BlockSpec((1, block // fine_rows, width), lambda i: (i, 0, 0)),
            whole(fine.shape),
            whole((width, 3 * width)),
        ]
        + [whole(vector.shape) for vector in vectors],
        out_specs=[
            row_block,
            pl.BlockSpec((block, 1), lambda i: (i, 0)),
            row_block,
            lane_block,
            row_block,
            lane_block,
            row_block,
            lane_block,
            whole((vector_rows, width)),
            whole((capacity, latents.shape[1])),
        ],
        out_shape=[
            jax.ShapeDtypeStruct((rows, width), jnp.float32),
            jax.ShapeDtypeStruct((rows, 1), jnp.float32),
            low,
            low_t,
            low,
            low_t,
            low,
            low_t,
            jax.ShapeDtypeStruct((vector_rows, width), jnp.float32),
            jax.ShapeDtypeStruct((capacity, latents.shape[1]), latents.dtype),
        ],
        scratch_shapes=[
            pltpu.VMEM((slots, width), jnp.bfloat16),
            pltpu.VMEM((1, slots), jnp.int32),
            pltpu.SemaphoreType.DMA((2, splits)),
        ],
        compiler_params=pltpu.CompilerParams(
            vmem_limit_bytes=VMEM_LIMIT, collective_id=0, has_side_effects=True
        ),
        cost_estimate=pl.CostEstimate(
            flops=2 * rows * width * (slots + 3 * width),
            bytes_accessed=20 * rows * width,
            transcendentals=0,
        ),
        name="enter",
    )(
        latents,
        embed_weight,
        slot_place,
        coarse.reshape(rows // block, block // fine_rows, width),
        fine,
        joint_weight,
        *vectors,
    )


def attend_kernel(
    key_ref, query_ref, value_ref, mixed_ref, exact_ref, total_ref, raised_ref, scores_ref, norm_ref
):
    span = key_ref.shape[0]
    block = query_ref.shape[1]
    slice_rows = min(256, span)
    slices = span // slice_rows
    query = query_ref[...]
    head_row = lax.broadcasted_iota(jnp.int32, query.shape, 0) // HEAD_DIM
    ones = jnp.ones((16, slice_rows), jnp.bfloat16)

    @pl.when(pl.program_id(1) == 0)
    def _():
        keys = key_ref[...].astype(jnp.float32)
        lane_head = lax.broadcasted_iota(jnp.int32, (128, 128), 0) // HEAD_DIM
        column = lax.broadcasted_iota(jnp.int32, (128, 128), 1)
        pick = (lane_head == column).astype(jnp.float32).astype(jnp.bfloat16)
        norms = plain_dot((keys * keys).astype(jnp.bfloat16), pick)
        norm_ref[...] = jnp.broadcast_to(jnp.max(norms, axis=0, keepdims=True), norm_ref.shape)

    squares = query.astype(jnp.float32)
    squares = squares * squares
    bound = jnp.zeros((1, 1), jnp.float32)
    for head in range(PACK):
        rows = slice(head * HEAD_DIM, (head + 1) * HEAD_DIM)
        longest = jnp.max(
            jnp.sum(squares[rows], axis=0, keepdims=True), axis=1, keepdims=True
        )
        bound = jnp.maximum(bound, longest * norm_ref[0:1, head : head + 1])
    small = bound[0, 0] * 1.02 < SAFE_SCORE**2

    def run(shifted):
        lag = slices if shifted else min(2, slices)
        steps = PACK * slices
        highest, held = {}, {}
        own_query = partial_highest = mixed = None
        for now in range(steps + lag):
            if now < steps:
                head, at = divmod(now, slices)
                part = slice(at * slice_rows, (at + 1) * slice_rows)
                if at == 0:
                    own_query = jnp.where(head_row == head, query, jnp.zeros_like(query))
                    partial_highest = jnp.full((8, block), -jnp.inf, jnp.float32)
                scores = plain_dot(key_ref[part, :], own_query)
                held[now] = scores
                if shifted:
                    partial_highest = jnp.maximum(
                        partial_highest, jnp.max(scores.reshape(slice_rows // 8, 8, block), axis=0)
                    )
                    if at == slices - 1:
                        highest[head] = jnp.max(partial_highest, axis=0, keepdims=True)
            if now >= lag:
                head, at = divmod(now - lag, slices)
                rows = slice(head * HEAD_DIM, (head + 1) * HEAD_DIM)
                part = slice(at * slice_rows, (at + 1) * slice_rows)
                scores = held.pop(now - lag)
                if shifted:
                    scores = scores - highest[head]
                raised = jnp.exp2(scores).astype(jnp.bfloat16)
                raised_ref[head, part, :] = raised
                term = plain_dot(jnp.concatenate([value_ref[rows, part], ones], axis=0), raised)
                mixed = term if at == 0 else mixed + term
                if at == slices - 1:
                    total = mixed[HEAD_DIM : HEAD_DIM + 1]
                    total_ref[0, head : head + 1, :] = total
                    mean = mixed[:HEAD_DIM] / total
                    exact_ref[rows, :] = mean
                    mixed_ref[rows, :] = mean.astype(jnp.bfloat16)

    @pl.when(small)
    def _():
        run(False)

    @pl.when(jnp.logical_not(small))
    def _():
        run(True)


def attend(keys, query_t, value_t):
    width, rows = query_t.shape
    span = keys.shape[0]
    block = min(512, rows)
    groups = width // 128
    lane_block = pl.BlockSpec((128, block), lambda g, i: (g, i))
    return pl.pallas_call(
        attend_kernel,
        grid=(groups, rows // block),
        in_specs=[
            pl.BlockSpec((span, 128), lambda g, i: (0, g)),
            lane_block,
            pl.BlockSpec((128, span), lambda g, i: (g, 0)),
        ],
        out_specs=[
            lane_block,
            lane_block,
            pl.BlockSpec((1, 8, block), lambda g, i: (g, 0, i)),
            pl.BlockSpec((PACK, span, block), lambda g, i: (g, 0, i)),
        ],
        out_shape=[
            jax.ShapeDtypeStruct((width, rows), jnp.bfloat16),
            jax.ShapeDtypeStruct((width, rows), jnp.float32),
            jax.ShapeDtypeStruct((groups, 8, rows), jnp.float32),
            jax.ShapeDtypeStruct((HEADS, span, rows), jnp.bfloat16),
        ],
        scratch_shapes=[
            pltpu.VMEM((span // min(256, span) + 1, min(256, span), block), jnp.float32),
            pltpu.VMEM((8, 128), jnp.float32),
        ],
        compiler_params=pltpu.CompilerParams(vmem_limit_bytes=VMEM_LIMIT),
        cost_estimate=pl.CostEstimate(
            flops=HEADS * span * rows * 512,
            bytes_accessed=2 * HEADS * span * rows,
            transcendentals=HEADS * span * rows,
        ),
        name="attend",
    )(keys, query_t, value_t)


def middle_kernel(
    stream_ref,
    mixed_ref,
    cotangent_ref,
    output_ref,
    expand_ref,
    contract_ref,
    vector_ref,
    decoded_ref,
    grad_middle_ref,
    grad_attended_ref,
    flat_ref,
    small_ref,
    expand_sum,
    contract_sum,
    output_sum,
    small_sum,
):
    width = stream_ref.shape[1]
    chunks = expand_ref.shape[1] // width

    def vector(row):
        return vector_ref[row : row + 1, :]

    @pl.when(pl.program_id(0) == 0)
    def _():
        expand_sum[...] = jnp.zeros_like(expand_sum)
        contract_sum[...] = jnp.zeros_like(contract_sum)
        output_sum[...] = jnp.zeros_like(output_sum)
        small_sum[...] = jnp.zeros_like(small_sum)

    mixed_t = mixed_ref[...]
    cotangent = cotangent_ref[...]
    middle = (
        stream_ref[...]
        + lead_dot(mixed_t, output_ref[...])
        + vector(OUTPUT_BIAS)
    )
    normed, scale = normalize(middle)
    gain = vector(SECOND_GAIN)
    low = (normed * gain + vector(SECOND_SHIFT)).astype(jnp.bfloat16)
    low_t = turned(low)
    output = middle + vector(CONTRACT_BIAS)
    grad_normed = jnp.zeros_like(middle)
    for chunk in range(chunks):
        part = slice(chunk * width, (chunk + 1) * width)
        hidden = plain_dot(low, expand_ref[:, part]) + vector(EXPAND_BIAS + chunk)
        below = 0.5 + 0.5 * lax.erf(hidden * math.sqrt(0.5))
        slope = below + hidden * jnp.exp(-0.5 * hidden * hidden) * (1.0 / math.sqrt(2 * math.pi))
        active = (hidden * below).astype(jnp.bfloat16)
        grad_hidden = (trail_dot(cotangent, contract_ref[part, :]) * slope).astype(jnp.bfloat16)
        output = output + plain_dot(active, contract_ref[part, :])
        grad_normed = grad_normed + trail_dot(grad_hidden, expand_ref[:, part])
        contract_sum[part, :] += lead_dot(active, cotangent)
        expand_sum[part, :] += plain_dot(low_t, grad_hidden)
        small_sum[chunk : chunk + 1, :] += column_sum(grad_hidden)
    decoded_ref[...] = output.astype(jnp.bfloat16)
    grad_middle = cotangent.astype(jnp.float32) + normalize_back(grad_normed * gain, normed, scale)
    grad_middle_ref[...] = grad_middle
    branch = grad_middle.astype(jnp.bfloat16)
    grad_attended_ref[...] = trail_dot(output_ref[...], branch).astype(jnp.bfloat16)
    output_sum[...] += plain_dot(mixed_t, branch)
    small_sum[chunks : chunks + 1, :] += column_sum(cotangent)
    small_sum[chunks + 1 : chunks + 2, :] += column_sum(branch)
    small_sum[chunks + 2 : chunks + 3, :] += column_sum(grad_normed * normed)
    small_sum[chunks + 3 : chunks + 4, :] += column_sum(grad_normed)

    @pl.when(pl.program_id(0) == pl.num_programs(0) - 1)
    def _():
        at = 0
        for total in (expand_sum, contract_sum, output_sum):
            flat_ref[at : at + total.shape[0], :] = total[...].astype(flat_ref.dtype)
            at += total.shape[0]
        if at < flat_ref.shape[0]:
            flat_ref[at:, :] = jnp.zeros((flat_ref.shape[0] - at, width), flat_ref.dtype)
        small_ref[...] = small_sum[...]


def middle_block(
    stream,
    mixed_t,
    cotangent,
    output_weight,
    expand_weight,
    contract_weight,
    vectors,
    flat_rows,
):
    rows, width = stream.shape
    hidden = expand_weight.shape[1]
    block = min(512, rows)
    row_block = pl.BlockSpec((block, width), lambda i: (i, 0))
    lane_block = pl.BlockSpec((width, block), lambda i: (0, i))
    small_rows = hidden // width + 4
    return pl.pallas_call(
        middle_kernel,
        grid=(rows // block,),
        in_specs=[
            row_block,
            lane_block,
            row_block,
            whole((width, width)),
            whole((width, hidden)),
            whole((hidden, width)),
            whole(vectors.shape),
        ],
        out_specs=[
            row_block,
            row_block,
            lane_block,
            whole((flat_rows, width)),
            whole((small_rows, width)),
        ],
        out_shape=[
            jax.ShapeDtypeStruct((rows, width), jnp.bfloat16),
            jax.ShapeDtypeStruct((rows, width), jnp.float32),
            jax.ShapeDtypeStruct((width, rows), jnp.bfloat16),
            jax.ShapeDtypeStruct((flat_rows, width), jnp.bfloat16),
            jax.ShapeDtypeStruct((small_rows, width), jnp.float32),
        ],
        scratch_shapes=[
            pltpu.VMEM((hidden, width), jnp.float32),
            pltpu.VMEM((hidden, width), jnp.float32),
            pltpu.VMEM((width, width), jnp.float32),
            pltpu.VMEM((small_rows, width), jnp.float32),
        ],
        compiler_params=pltpu.CompilerParams(vmem_limit_bytes=VMEM_LIMIT),
        cost_estimate=pl.CostEstimate(
            flops=2 * rows * width * (6 * hidden + 3 * width),
            bytes_accessed=16 * rows * width,
            transcendentals=2 * rows * hidden,
        ),
        name="middle",
    )(
        stream,
        mixed_t,
        cotangent,
        output_weight,
        expand_weight,
        contract_weight,
        vectors,
    )


def attend_back_kernel(
    steps,
    raised_ref,
    total_ref,
    value_ref,
    key_ref,
    query_ref,
    exact_ref,
    grad_ref,
    flat_ref,
    rows_ref,
    latents_ref,
    grad_query_ref,
    grad_key_ref,
    grad_value_ref,
    summed_ref,
    decoded_ref,
    gathered_ref,
    key_sum,
    value_sum,
    exchange_sems,
    exchange_local,
    gather_sems,
    gather_local,
    *sum_refs,
):
    spot = Spot()
    tree = TreeSum(spot, flat_ref, summed_ref, sum_refs, True)
    clips, share = decoded_ref.shape[0], decoded_ref.shape[1]
    mine, part = spot.index % clips, spot.index // clips

    def member(step):
        return (mine + step) % clips

    def exchange(step):
        return send(
            rows_ref.at[span_of(member(step) * share, share)],
            decoded_ref.at[mine],
            exchange_sems,
            step,
            (spot.layer, part * clips + member(step)),
        )

    def own_rows():
        return pltpu.make_async_copy(
            rows_ref.at[span_of(mine * share, share)], decoded_ref.at[mine], exchange_local
        )

    capacity = latents_ref.shape[0]

    def held(core, chip):
        return gathered_ref.at[span_of((chip * 2 + core) * capacity, capacity)]

    def share_own(at, device):
        return send(latents_ref, held(spot.core, spot.chip), gather_sems, at, device)

    def pass_on(at, core, step):
        place = held(core, spot.chip_at(-step))
        return send(place, place, gather_sems, at, spot.sibling())

    def keep_own():
        return pltpu.make_async_copy(latents_ref, held(spot.core, spot.chip), gather_local)

    step_now = pl.program_id(0) * pl.num_programs(1) + pl.program_id(1)

    def at_step(fraction):
        return pl.when(step_now == fraction * steps // 32)

    @at_step(0)
    def _():
        others = spot.tree() + [
            (spot.layer, part * clips + member(step)) for step in range(1, clips)
        ]
        count = spot.meet(others)
        pl.semaphore_wait(pltpu.get_barrier_semaphore(), count)
        tree.start()

    @at_step(4)
    def _():
        tree.near_to_far()

    @at_step(11)
    def _():
        tree.far_to_deep()
        own_rows().start()
        for step in range(1, clips):
            exchange(step).start()
        keep_own().start()
        for step in range(1, spot.half):
            share_own(step, spot.peer(step)).start()
        share_own(0, spot.sibling()).start()

    @at_step(15)
    def _():
        tree.deep_to_layer()

    @at_step(19)
    def _():
        tree.layer_to_part()

    @at_step(24)
    def _():
        for step in range(1, spot.half):
            pass_on(step, spot.core, step).wait_recv()
            pass_on(spot.half + step, spot.core, step).start()

    @at_step(29)
    def _():
        tree.part_to_half()

    @at_step(31)
    def _():
        tree.finish()
        own_rows().wait()
        for step in range(1, clips):
            exchange(step).wait_send()
        for step in range(1, clips):
            send(
                rows_ref.at[span_of(mine * share, share)],
                decoded_ref.at[member(-step)],
                exchange_sems,
                step,
                (spot.layer, part * clips + member(step)),
            ).wait_recv()
        keep_own().wait()
        for step in range(1, spot.half):
            share_own(step, spot.peer(step)).wait_send()
        share_own(0, spot.sibling()).wait_send()
        pass_on(0, 1 - spot.core, 0).wait_recv()
        for step in range(1, spot.half):
            pass_on(spot.half + step, spot.core, step).wait_send()
            pass_on(spot.half + step, 1 - spot.core, step).wait_recv()

    @pl.when(pl.program_id(1) == 0)
    def _():
        key_sum[...] = jnp.zeros_like(key_sum)
        value_sum[...] = jnp.zeros_like(value_sum)

    block = query_ref.shape[1]
    head_row = lax.broadcasted_iota(jnp.int32, (128, block), 0) // HEAD_DIM
    head_col = lax.broadcasted_iota(jnp.int32, (block, 128), 1) // HEAD_DIM
    inverse = 1.0 / total_ref[0, 0:PACK]
    inverse = jnp.concatenate(
        [jnp.broadcast_to(inverse[h : h + 1], (HEAD_DIM, block)) for h in range(PACK)], axis=0
    )
    grad_low = (grad_ref[...].astype(jnp.float32) * inverse).astype(jnp.bfloat16)
    grad = grad_low.astype(jnp.float32)
    inner = grad * exact_ref[...]
    grad_turned = grad.T.astype(jnp.bfloat16)
    query_turned = turned(query_ref[...])
    span = value_ref.shape[0]
    slice_rows = min(256, span)
    units = [(head, at) for head in range(PACK) for at in range(0, span, slice_rows)]
    lag = 2
    weights = {}
    grad_query = None
    for now in range(len(units) + lag):
        if now < len(units):
            head, at = units[now]
            own_grad = jnp.where(head_row == head, grad_low, jnp.zeros_like(grad_low))
            weights[now] = plain_dot(value_ref[at : at + slice_rows, :], own_grad)
        if now >= lag:
            head, at = units[now - lag]
            rows = slice(head * HEAD_DIM, (head + 1) * HEAD_DIM)
            part = slice(at, at + slice_rows)
            row_inner = jnp.sum(inner[rows], axis=0, keepdims=True)
            raised = raised_ref[head, part, :]
            grad_scores = raised * (weights.pop(now - lag) - row_inner).astype(jnp.bfloat16)
            value_sum[part, :] += plain_dot(
                raised, jnp.where(head_col == head, grad_turned, jnp.zeros_like(grad_turned))
            )
            key_sum[part, :] += plain_dot(
                grad_scores, jnp.where(head_col == head, query_turned, jnp.zeros_like(query_turned))
            )
            term = plain_dot(key_ref[rows, part], grad_scores)
            grad_query = term if at == 0 else grad_query + term
            if at + slice_rows == span:
                grad_query_ref[rows, :] = (grad_query * HEAD_DIM ** (-0.5)).astype(jnp.bfloat16)

    @pl.when(pl.program_id(1) == pl.num_programs(1) - 1)
    def _():
        grad_key_ref[...] = (key_sum[...] * (1.0 / LOG2E)).astype(jnp.bfloat16)
        grad_value_ref[...] = value_sum[...].astype(jnp.bfloat16)


def attend_back(raised, total, values, key_t, query_t, exact_t, grad_t, flat, decoded_rows, latents):
    splits, layers = lax.axis_size("seq"), lax.axis_size("dp")
    clips, share, _ = decoded_rows.shape
    width, rows = query_t.shape
    span = values.shape[0]
    block = min(256, rows)
    groups = width // 128
    lane_block = pl.BlockSpec((128, block), lambda g, i: (g, i))
    return pl.pallas_call(
        partial(attend_back_kernel, groups * (rows // block)),
        grid=(groups, rows // block),
        in_specs=[
            pl.BlockSpec((PACK, span, block), lambda g, i: (g, 0, i)),
            pl.BlockSpec((1, 8, block), lambda g, i: (g, 0, i)),
            pl.BlockSpec((span, 128), lambda g, i: (0, g)),
            pl.BlockSpec((128, span), lambda g, i: (g, 0)),
            lane_block,
            lane_block,
            lane_block,
            pl.BlockSpec(memory_space=pl.ANY),
            pl.BlockSpec(memory_space=pl.ANY),
            pl.BlockSpec(memory_space=pl.ANY),
        ],
        out_specs=[
            lane_block,
            pl.BlockSpec((span, 128), lambda g, i: (0, g)),
            pl.BlockSpec((span, 128), lambda g, i: (0, g)),
            pl.BlockSpec(memory_space=pl.ANY),
            pl.BlockSpec(memory_space=pl.ANY),
            pl.BlockSpec(memory_space=pl.ANY),
        ],
        out_shape=[
            jax.ShapeDtypeStruct((width, rows), jnp.bfloat16),
            jax.ShapeDtypeStruct((span, width), jnp.bfloat16),
            jax.ShapeDtypeStruct((span, width), jnp.bfloat16),
            jax.ShapeDtypeStruct(flat.shape, flat.dtype),
            jax.ShapeDtypeStruct(decoded_rows.shape, decoded_rows.dtype),
            jax.ShapeDtypeStruct((splits * latents.shape[0], latents.shape[1]), latents.dtype),
        ],
        scratch_shapes=[
            pltpu.VMEM((span, 128), jnp.float32),
            pltpu.VMEM((span, 128), jnp.float32),
            pltpu.SemaphoreType.DMA((2, clips)),
            pltpu.SemaphoreType.DMA,
            pltpu.SemaphoreType.DMA((2, splits)),
            pltpu.SemaphoreType.DMA,
        ]
        + TreeSum.scratch(flat.shape[0], flat.shape[1], True, splits, layers),
        compiler_params=pltpu.CompilerParams(
            vmem_limit_bytes=VMEM_LIMIT, collective_id=1, has_side_effects=True
        ),
        cost_estimate=pl.CostEstimate(
            flops=HEADS * span * rows * 1024,
            bytes_accessed=2 * HEADS * span * rows,
            transcendentals=0,
        ),
        name="attend_back",
    )(raised, total, values, key_t, query_t, exact_t, grad_t, flat, decoded_rows.reshape(clips * share, width), latents)


def leave_kernel(
    grad_query_ref,
    grad_key_ref,
    grad_value_ref,
    stream_ref,
    empty_ref,
    low_ref,
    grad_middle_ref,
    vector_ref,
    joint_ref,
    slot_ref,
    latents_ref,
    embed_ref,
    early_ref,
    latent_grad_ref,
    joint_total_ref,
    embed_total_ref,
    joint_sum,
    small_sum,
    grad_all,
    joint_flat,
    embed_flat,
    back_all,
    near_in,
    far_out,
    far_in,
    latents_all,
    sems,
    local,
    *sum_refs,
):
    block, width = stream_ref.shape
    step_now = pl.program_id(0)
    spot = Spot()
    capacity = back_all.shape[0] // spot.splits
    others = spot.tree()
    blocks = pl.num_programs(0) // 2
    count = len(sum_refs) // 2
    joint_tree = TreeSum(spot, joint_flat, joint_total_ref, sum_refs[:count], True)
    embed_tree = TreeSum(spot, embed_flat, embed_total_ref, sum_refs[count:], False)

    def load_latents():
        return pltpu.make_async_copy(latents_ref, latents_all, local)

    @pl.when(step_now == 0)
    def _():
        spot.meet(others)
        load_latents().start()
        joint_sum[...] = jnp.zeros_like(joint_sum)
        small_sum[...] = jnp.zeros_like(small_sum)

    @pl.when(step_now < blocks)
    def _():
        low_t = turned(low_ref[...])
        sides = [turned(grad_query_ref[...]), grad_key_ref[...], grad_value_ref[...]]
        for at, side in enumerate(sides):
            joint_sum[at * width : (at + 1) * width, :] += plain_dot(low_t, side)
        small_sum[3:4, :] += column_sum(sides[0])
        small_sum[4:5, :] += column_sum(sides[2])

    @pl.when(step_now == blocks - 1)
    def _():
        rows = joint_sum.shape[0]
        joint_flat[:rows, :] = joint_sum[...].astype(jnp.bfloat16)
        if joint_flat.shape[0] > rows:
            joint_flat[rows:, :] = jnp.zeros(
                (joint_flat.shape[0] - rows, width), jnp.bfloat16
            )
        pl.semaphore_wait(pltpu.get_barrier_semaphore(), len(others))
        joint_tree.start()

    @pl.when(step_now == blocks + blocks // 4)
    def _():
        joint_tree.near_to_far()

    @pl.when(step_now >= blocks)
    def _():
        normed, scale = normalize(stream_ref[...])
        sides = [turned(grad_query_ref[...]), grad_key_ref[...], grad_value_ref[...]]
        grad_normed = jnp.zeros_like(normed)
        for at, side in enumerate(sides):
            grad_normed = grad_normed + trail_dot(
                side, joint_ref[:, at * width : (at + 1) * width]
            )
        grad_stream = grad_middle_ref[...] + normalize_back(
            grad_normed * vector_ref[FIRST_GAIN : FIRST_GAIN + 1, :], normed, scale
        )
        grad_all[pl.ds(pl.multiple_of((step_now - blocks) * block, block), block), :] = (
            grad_stream.astype(jnp.bfloat16)
        )
        small_sum[0:1, :] += column_sum(empty_ref[...] * grad_stream)
        small_sum[1:2, :] += column_sum(grad_normed * normed)
        small_sum[2:3, :] += column_sum(grad_normed)

    @pl.when(step_now == pl.num_programs(0) - 1)
    def _():
        place = lax.broadcasted_iota(jnp.int32, (1, grad_all.shape[0]), 1)

        def gathered(owner):
            slots = slot_ref[pl.ds(owner, 1), :].astype(jnp.float32)
            slots = jnp.broadcast_to(slots, (8, slots.shape[1])).T[:capacity, 0:1]
            takes = (slots.astype(jnp.int32) == place).astype(jnp.float32).astype(jnp.bfloat16)
            return plain_dot(takes, grad_all[...])

        def rows_of(owner):
            return span_of(owner * capacity, capacity)

        def part(at):
            return pl.ds(at * capacity, capacity)

        def near_copy(step):
            owner = spot.chip_at(step) * 2 + 1 - spot.core
            return send(
                back_all.at[rows_of(owner)], near_in.at[part(step)], sems, step, spot.sibling()
            )

        def far_copy(step):
            return send(
                far_out.at[part(step - 1)],
                far_in.at[part(step - 1)],
                sems,
                spot.half + step,
                spot.peer(step),
            )

        for step in list(range(1, spot.half)) + [0]:
            owner = spot.chip_at(step) * 2 + 1 - spot.core
            back_all[rows_of(owner), :] = gathered(owner).astype(jnp.bfloat16)
            near_copy(step).start()
            owner = spot.chip_at(step) * 2 + spot.core
            own = gathered(owner)
            back_all[rows_of(owner), :] = own.astype(jnp.bfloat16)
            near_copy(step).wait()
            own = own + near_in[part(step), :].astype(jnp.float32)
            if step > 0:
                far_out[part(step - 1), :] = own.astype(jnp.bfloat16)
                far_copy(step).start()
            if step == 1:
                joint_tree.far_to_deep()
        load_latents().wait()
        embed_rows = embed_ref.shape[0]
        embed_flat[:embed_rows, :] = lead_dot(latents_all[...], back_all[...]).astype(jnp.bfloat16)
        small_sum[5:6, :] = column_sum(back_all[...])
        small = jnp.concatenate([early_ref[...], small_sum[...]], axis=0)
        rest = embed_flat.shape[0] - embed_rows - small.shape[0]
        if rest:
            small = jnp.concatenate([small, jnp.zeros((rest, width), jnp.float32)], axis=0)
        embed_flat[embed_rows:, :] = small.astype(jnp.bfloat16)
        embed_tree.start()
        joint_tree.deep_to_layer()
        embed_tree.near_to_far()
        joint_tree.layer_to_part()
        embed_tree.far_to_deep()
        for step in range(1, spot.half):
            far_copy(step).wait()
            own = own + far_in[part(step - 1), :].astype(jnp.float32)
        grad_embedded = own[: latent_grad_ref.shape[0]].astype(jnp.bfloat16)
        latent_grad_ref[...] = trail_dot(grad_embedded, embed_ref[...]).astype(jnp.bfloat16)
        joint_tree.part_to_half()
        embed_tree.deep_to_layer()
        joint_tree.finish()
        embed_tree.part_to_half()
        embed_tree.finish()


def leave(
    grad_query_t,
    grad_key,
    grad_value,
    stream,
    empty,
    low,
    grad_middle,
    vectors,
    joint_weight,
    slot_place,
    latents_all,
    embed_weight,
    early_small,
    own_rows,
):
    splits, layers = lax.axis_size("seq"), lax.axis_size("dp")
    rows, width = stream.shape
    slots = latents_all.shape[0]
    latent_shape = (own_rows, latents_all.shape[1])
    capacity = slots // splits
    half = splits // 2
    block = min(256, rows)
    blocks = rows // block
    row_block = pl.BlockSpec((block, width), lambda i: (i % blocks, 0))
    first_block = pl.BlockSpec((block, width), lambda i: (jnp.minimum(i, blocks - 1), 0))
    later_block = pl.BlockSpec((block, width), lambda i: (jnp.maximum(i - blocks, 0), 0))
    lane_block = pl.BlockSpec((width, block), lambda i: (0, i % blocks))
    joint_rows = padded(3 * width, splits * layers * 16)
    embed_rows = padded(embed_weight.shape[0] + early_small.shape[0] + 8, splits * 16)
    return pl.pallas_call(
        leave_kernel,
        grid=(2 * blocks,),
        in_specs=[
            lane_block,
            row_block,
            row_block,
            later_block,
            pl.BlockSpec((block, 1), lambda i: (jnp.maximum(i - blocks, 0), 0)),
            first_block,
            later_block,
            whole(vectors.shape),
            whole((width, 3 * width)),
            whole(slot_place.shape),
            pl.BlockSpec(memory_space=pl.ANY),
            whole(embed_weight.shape),
            whole(early_small.shape),
        ],
        out_specs=[
            whole(latent_shape),
            pl.BlockSpec(memory_space=pl.ANY),
            pl.BlockSpec(memory_space=pl.ANY),
        ],
        out_shape=[
            jax.ShapeDtypeStruct(latent_shape, jnp.bfloat16),
            jax.ShapeDtypeStruct((joint_rows, width), jnp.bfloat16),
            jax.ShapeDtypeStruct((embed_rows, width), jnp.bfloat16),
        ],
        scratch_shapes=[
            pltpu.VMEM((3 * width, width), jnp.float32),
            pltpu.VMEM((8, width), jnp.float32),
            pltpu.VMEM((rows, width), jnp.bfloat16),
            pltpu.VMEM((joint_rows, width), jnp.bfloat16),
            pltpu.VMEM((embed_rows, width), jnp.bfloat16),
            pltpu.VMEM((slots, width), jnp.bfloat16),
            pltpu.VMEM((half * capacity, width), jnp.bfloat16),
            pltpu.VMEM((max(half - 1, 1) * capacity, width), jnp.bfloat16),
            pltpu.VMEM((max(half - 1, 1) * capacity, width), jnp.bfloat16),
            pltpu.VMEM(latents_all.shape, latents_all.dtype),
            pltpu.SemaphoreType.DMA((2, splits)),
            pltpu.SemaphoreType.DMA,
        ]
        + TreeSum.scratch(joint_rows, width, True, splits, layers)
        + TreeSum.scratch(embed_rows, width, False, splits, layers),
        compiler_params=pltpu.CompilerParams(
            vmem_limit_bytes=VMEM_LIMIT, collective_id=2, has_side_effects=True
        ),
        cost_estimate=pl.CostEstimate(
            flops=2 * rows * width * (slots + 6 * width),
            bytes_accessed=20 * rows * width,
            transcendentals=0,
        ),
        name="leave",
    )(
        grad_query_t,
        grad_key,
        grad_value,
        stream,
        empty,
        low,
        grad_middle,
        vectors,
        joint_weight,
        slot_place,
        latents_all,
        embed_weight,
        early_small,
    )


def finish_kernel(
    expand_ref,
    contract_ref,
    output_ref,
    joint_ref,
    embed_ref,
    small_ref,
    expand_out,
    contract_out,
    output_out,
    joint_out,
    embed_out,
    *small_outs,
):
    for source, target in (
        (expand_ref, expand_out),
        (contract_ref, contract_out),
        (output_ref, output_out),
        (joint_ref, joint_out),
        (embed_ref, embed_out),
    ):
        target[...] = source[...].astype(jnp.float32)
    small = small_ref[...].astype(jnp.float32)
    width = small.shape[1]
    at = 0
    for target in small_outs:
        for start in range(0, target.shape[0], width):
            target[start : start + width] = small[at]
            at += 1


def finish(early_sum, joint_sum, embed_sum, hidden, embed_rows, small_sizes):
    width = early_sum.shape[1]
    chunks = hidden // width
    square = (width, width)
    embed_block = (embed_rows // chunks, width)
    sides = 3
    return pl.pallas_call(
        finish_kernel,
        grid=(chunks,),
        in_specs=[
            pl.BlockSpec(square, lambda i: (i, 0)),
            pl.BlockSpec(square, lambda i: (chunks + i, 0)),
            pl.BlockSpec(square, lambda i: (2 * chunks, 0)),
            pl.BlockSpec(square, lambda i: (jnp.minimum(i, sides - 1), 0)),
            pl.BlockSpec(embed_block, lambda i: (i, 0)),
            pl.BlockSpec((16, width), lambda i: (embed_rows // 16, 0)),
        ],
        out_specs=[
            pl.BlockSpec(square, lambda i: (0, i)),
            pl.BlockSpec(square, lambda i: (i, 0)),
            pl.BlockSpec(square, lambda i: (0, 0)),
            pl.BlockSpec(square, lambda i: (0, jnp.minimum(i, sides - 1))),
            pl.BlockSpec(embed_block, lambda i: (i, 0)),
        ]
        + [whole((size,)) for size in small_sizes],
        out_shape=[
            jax.ShapeDtypeStruct((width, hidden), jnp.float32),
            jax.ShapeDtypeStruct((hidden, width), jnp.float32),
            jax.ShapeDtypeStruct(square, jnp.float32),
            jax.ShapeDtypeStruct((width, sides * width), jnp.float32),
            jax.ShapeDtypeStruct((embed_rows, width), jnp.float32),
        ]
        + [jax.ShapeDtypeStruct((size,), jnp.float32) for size in small_sizes],
        compiler_params=pltpu.CompilerParams(vmem_limit_bytes=VMEM_LIMIT),
        cost_estimate=pl.CostEstimate(
            flops=0, bytes_accessed=12 * width * (hidden + width), transcendentals=0
        ),
        name="finish",
    )(early_sum, early_sum, early_sum, joint_sum, embed_sum, embed_sum)


def body(
    latents,
    clip_ids,
    restore,
    counts,
    embed_weight,
    embed_bias,
    mask_token,
    first_gain,
    first_shift,
    joint_weight,
    query_bias,
    value_bias,
    output_weight,
    output_bias,
    second_gain,
    second_shift,
    expand_weight,
    expand_bias,
    contract_weight,
    contract_bias,
    cotangent,
):
    splits = lax.axis_size("seq")
    seq_index = lax.axis_index("seq")
    capacity = latents.shape[0]
    clip_count, clip_share, model_width = cotangent.shape
    sharers = splits // clip_count
    rows = clip_count * clip_share
    own_clip = seq_index % clip_count
    first_place = (seq_index // clip_count) * rows
    exchange_groups = [[s * clip_count + c for c in range(clip_count)] for s in range(sharers)]
    clip_groups = [[s * clip_count + c for s in range(sharers)] for c in range(clip_count)]

    def to_clips(blocks):
        return lax.all_to_all(
            blocks,
            "seq",
            split_axis=0,
            concat_axis=0,
            tiled=True,
            axis_index_groups=exchange_groups if sharers > 1 else None,
        )

    live = jnp.arange(capacity, dtype=jnp.int32)[None, :] < counts[:, None]
    mine = live & ((clip_ids % clip_count).reshape(splits, capacity) == own_clip)
    slot_place = jnp.where(mine, restore.reshape(splits, capacity) - first_place, -1)
    slot_place = jnp.pad(
        slot_place, ((0, 0), (0, padded(capacity, 128) - capacity)), constant_values=-1
    )
    (
        stream,
        empty,
        first_low,
        query_t,
        keys,
        key_t,
        values,
        value_t,
        vectors,
        latents,
    ) = enter(
        latents,
        embed_weight,
        slot_place,
        first_place,
        rows,
        [
            embed_bias,
            mask_token,
            first_gain,
            first_shift,
            query_bias,
            value_bias,
            output_bias,
            second_gain,
            second_shift,
            contract_bias,
            expand_bias,
        ],
        joint_weight,
    )
    cotangent, keys = lax.optimization_barrier((cotangent, keys))
    grad_output = to_clips(cotangent).reshape(rows, model_width)
    if sharers > 1:
        keys = lax.all_gather(keys, "seq", axis=0, tiled=True, axis_index_groups=clip_groups)
        values = lax.all_gather(values, "seq", axis=0, tiled=True, axis_index_groups=clip_groups)
        key_t, value_t = keys.T, values.T
    mixed_t, exact_t, total, raised = attend(keys, query_t, value_t)
    (
        decoded_rows,
        grad_middle,
        grad_attended_t,
        early_flat,
        early_small,
    ) = middle_block(
        stream,
        mixed_t,
        grad_output,
        output_weight,
        expand_weight,
        contract_weight,
        vectors,
        padded(2 * expand_weight.shape[1] + model_width, splits * lax.axis_size("dp") * 16),
    )
    grad_query_t, grad_key, grad_value, early_sum, decoded, latents_all = attend_back(
        raised,
        total,
        values,
        key_t,
        query_t,
        exact_t,
        grad_attended_t,
        early_flat,
        decoded_rows.reshape(clip_count, clip_share, model_width),
        latents,
    )
    if sharers > 1:
        grad_key, grad_value = (
            lax.psum_scatter(
                side, "seq", scatter_dimension=0, tiled=True, axis_index_groups=clip_groups
            )
            for side in (grad_key, grad_value)
        )
    latent_grad, joint_sum, embed_sum = leave(
        grad_query_t,
        grad_key,
        grad_value,
        stream,
        empty,
        first_low,
        grad_middle,
        vectors,
        joint_weight,
        slot_place,
        latents_all,
        embed_weight,
        early_small,
        capacity,
    )
    hidden_width = expand_weight.shape[1]
    (
        grad_expand,
        grad_contract,
        grad_output_weight,
        grad_joint_weight,
        grad_embed_weight,
        grad_expand_bias,
        grad_contract_bias,
        grad_output_bias,
        grad_second_gain,
        grad_second_shift,
        grad_mask,
        grad_first_gain,
        grad_first_shift,
        grad_query_bias,
        grad_value_bias,
        grad_embed_bias,
    ) = finish(
        early_sum,
        joint_sum,
        embed_sum,
        hidden_width,
        embed_weight.shape[0],
        [hidden_width] + [model_width] * 10,
    )
    return (
        decoded,
        latent_grad,
        grad_embed_weight,
        grad_embed_bias,
        grad_mask,
        grad_first_gain,
        grad_first_shift,
        grad_joint_weight,
        grad_query_bias,
        grad_value_bias,
        grad_output_weight,
        grad_output_bias,
        grad_second_gain,
        grad_second_shift,
        grad_expand,
        grad_expand_bias,
        grad_contract,
        grad_contract_bias,
    )


def solution(mesh):
    placed = (
        (P(("dp", "seq"), None),) + (P("dp"),) * 3 + (P(),) * 16 + (P("dp", "seq", None),)
    )
    return jax.shard_map(
        body,
        mesh=mesh,
        in_specs=placed,
        out_specs=(P("dp", "seq", None), P(("dp", "seq"), None)) + (P(),) * 16,
        check_vma=False,
    )
```
